32 devices in a mesh: row: 4 (over z), col: 8 (over y, x, core).
Axes of the slice: x: 2, y: 2, z: 4, core: 2. Of those that a mesh axis runs over, the one named last changes fastest.
Arguments:
- features: bfloat16 [8192, 512], P('row'), may hold values from -6 to 6
- logits: float32 [8192, 128], P(('row', 'col')), may hold values from -16 to 16
Outputs:
- memberships: float32 [8192, 128], P(('row', 'col'))
- standardized: float32 [8192, 128], P(('row', 'col'))
The draws below stay inside these ranges and needn't reach their ends.
All inputs are finite; a program needn't handle non-finite values.
Results may differ from the reference program's by a relative error of at most 0.0003.
Values may be sent and summed in bfloat16 or wider, within the bound.
No kernel may reach another device: no remote copies, remote signals or barrier semaphores. Data moves between devices by JAX's collectives and lax.ppermute only.
A program may use at most 64 MiB of HBM per device.

```python
import math
import jax
import jax.numpy as jnp
from jax import lax

F = 512
C = 128
ITERS = 2
N = 8192


def block_levels(rng, extent, split, smallest, top_value):
    loudness = 1.0
    for dim, shards_of in split:
        heights = jax.random.uniform(jax.random.fold_in(jax.random.fold_in(rng, 6), dim), (shards_of,), jnp.float32, smallest / len(split), top_value / len(split))
        loudness = loudness * jnp.repeat(jnp.exp(heights), extent[dim] // shards_of).reshape((-1,) + (1,) * (len(extent) - 1 - dim))
    return loudness


def gaussian(key, dims, scale, limit, shards=(), held_as=jnp.bfloat16):
    drawn = scale * jax.random.normal(key, dims, jnp.float32)
    if shards:
        drawn = drawn * block_levels(key, dims, shards, -0.22, 0.18)
    return jnp.clip(drawn, -limit, limit).astype(held_as)


def setup_inputs(seed: int = 0) -> dict:
    seeds = jax.random.split(jax.random.key(seed), 3)
    features = gaussian(seeds[0], (N, F), 1.0, 6.0, ((0, 4),))
    logits = gaussian(seeds[1], (N, C), 3.0, 16.0, ((0, 32),), jnp.float32)
    return {"features": features, "logits": logits}


def kernel_scores(features, members):
    total = features.shape[0]
    feature_width = features.shape[1]
    block_rows = math.gcd(total, 512)
    blocks = features.reshape(total // block_rows, block_rows, feature_width)

    def block_product(block):
        inner = jnp.dot(block, features.T, preferred_element_type=jnp.float32)
        base = 1.0 + inner / feature_width
        kernel = base * base * base
        return jnp.dot(kernel, members, precision=lax.Precision.HIGHEST, preferred_element_type=jnp.float32)
    return lax.map(block_product, blocks).reshape(total, members.shape[1])

def reference(features, logits):
    raised = jnp.exp(logits)
    members = raised / lax.optimization_barrier(jnp.sum(raised, axis=1, keepdims=True))
    standardized = members
    for iteration in range(ITERS):
        scores = kernel_scores(features, members)
        cluster_size = lax.optimization_barrier(jnp.sum(members, axis=0))
        weighted = lax.optimization_barrier(jnp.sum(members * scores, axis=0))
        compact = weighted / (cluster_size * cluster_size)
        distance = compact[None, :] - 2.0 * scores / cluster_size[None, :]
        centered = distance - lax.optimization_barrier(jnp.mean(distance, axis=1, keepdims=True))
        spread = lax.optimization_barrier(jnp.mean(centered * centered, axis=1, keepdims=True))
        standardized = centered / jnp.sqrt(spread + 1e-06)
        raised = jnp.exp(-2.0 * standardized)
        members = raised / lax.optimization_barrier(jnp.sum(raised, axis=1, keepdims=True))
    return (members, standardized)
```

```python
import functools

import jax
import jax.numpy as jnp
from jax import lax
from jax.experimental import pallas as pl
from jax.experimental.pallas import tpu as pltpu
from jax.sharding import PartitionSpec as P

ITERS = 2
STAT_ROWS = 8
VMEM_BYTES = 48 * 1024 * 1024


def split(x):
    high = x.astype(jnp.bfloat16)
    low = (x - high.astype(jnp.float32)).astype(jnp.bfloat16)
    return high, low


def kernel_body(rows_ref, plane_ref, high_ref, low_ref):
    inner = lax.dot_general(
        rows_ref[...],
        plane_ref[...],
        (((1,), (1,)), ((), ())),
        preferred_element_type=jnp.float32,
    )
    t = inner / rows_ref.shape[1]
    high_ref[...], low_ref[...] = split(t * (3.0 + t * (3.0 + t)))


def kernel_block(rows, plane):
    count, width = rows.shape
    total = plane.shape[0]
    step = min(total, 512)
    return pl.pallas_call(
        kernel_body,
        grid=(total // step,),
        in_specs=[
            pl.BlockSpec((count, width), lambda i: (0, 0)),
            pl.BlockSpec((step, width), lambda i: (i, 0)),
        ],
        out_specs=[pl.BlockSpec((count, step), lambda i: (0, i))] * 2,
        out_shape=[jax.ShapeDtypeStruct((count, total), jnp.bfloat16)] * 2,
        compiler_params=pltpu.CompilerParams(vmem_limit_bytes=VMEM_BYTES),
        cost_estimate=pl.CostEstimate(
            flops=2 * count * total * width,
            bytes_accessed=2 * (count + total) * width + 4 * count * total,
            transcendentals=0,
        ),
    )(rows, plane)


def standardize(scores, size, weighted):
    distance = weighted / (size * size) - 2.0 * scores / size
    centered = distance - jnp.mean(distance, axis=1, keepdims=True)
    spread = jnp.mean(centered * centered, axis=1, keepdims=True)
    return centered / jnp.sqrt(spread + 1e-06)


def normalize(raised):
    return raised / jnp.sum(raised, axis=1, keepdims=True)


def product_body(first, n, crosses, has_near, *refs):
    refs = list(refs)
    take = lambda count: [refs.pop(0) for _ in range(count)]
    stats = None if first else take(1)[0]
    (even, odd) = take(2)
    others = take(crosses + has_near)
    blocks = crosses + has_near + 1
    kernels = take(2 * blocks)
    diag_out, = take(1)
    other_outs = take(crosses + has_near)
    t_even, t_odd = take(2)
    plane_hl, = take(1)
    (other_m,) = take(1)
    half = even.shape[0]
    clusters = even.shape[1]

    if first:
        member_of = lambda x: normalize(jnp.exp(x))
    else:
        weighted = stats[0:1, :]
        size = stats[1:2, :]
        member_of = lambda x: normalize(jnp.exp(-2.0 * standardize(x, size, weighted)))

    own = None
    for part, src in enumerate((even, odd)):
        for j in range(half // n):
            m = member_of(src[j * n : (j + 1) * n, :])
            if own is None:
                own = m
            high, low = split(m)
            at = part * half + j * n
            plane_hl[at : at + n, :clusters] = high
            plane_hl[at : at + n, clusters:] = low
    for i, src in enumerate(others):
        other_m[i * n : (i + 1) * n, :] = member_of(src[...])

    def product(high, low):
        both = jnp.dot(high[...], plane_hl[...], preferred_element_type=jnp.float32)
        rest = jnp.dot(low[...], plane_hl[:, :clusters], preferred_element_type=jnp.float32)
        return both[:, :clusters] + (both[:, clusters:] + rest)

    s = product(kernels[0], kernels[1])
    diag_out[...] = s
    total = jnp.sum(own * s, axis=0, keepdims=True)
    for i in range(crosses + has_near):
        s = product(kernels[2 + 2 * i], kernels[3 + 2 * i])
        other_outs[i][...] = s
        scale = 1.0 if has_near and i == 0 else 2.0
        total += scale * jnp.sum(other_m[i * n : (i + 1) * n, :] * s, axis=0, keepdims=True)
    over = (((0,), (0,)), ((), ()))
    for part, dst in enumerate((t_even, t_odd)):
        acc = None
        for i in range(has_near, crosses + has_near):
            high, low = split(other_m[i * n : (i + 1) * n, :])
            both = jnp.concatenate([high, low], axis=1)
            cols = slice(part * half, (part + 1) * half)
            a = lax.dot_general(
                kernels[2 + 2 * i][:, cols], both, over, preferred_element_type=jnp.float32
            )
            b = lax.dot_general(
                kernels[3 + 2 * i][:, cols], high, over, preferred_element_type=jnp.float32
            )
            a = a[:, :clusters] + (a[:, clusters:] + b)
            acc = a if acc is None else acc + a
        dst[:half, :] = jnp.zeros((half, clusters), jnp.float32) if acc is None else acc
    row = lax.broadcasted_iota(jnp.int32, (STAT_ROWS, clusters), 0)
    size = jnp.sum(own, axis=0, keepdims=True)
    stat = jnp.where(row == 0, total, jnp.where(row == 1, size, 0.0))
    t_even[half:, :] = stat
    t_odd[half:, :] = stat


def product_call(first, n, has_near, stats, even, odd, others, kernels):
    half, clusters = even.shape
    crosses = len(others) - has_near
    vmem = pl.BlockSpec(memory_space=pltpu.VMEM)
    args = ([] if first else [stats]) + [even, odd] + others + kernels
    f32 = jnp.float32
    outs = [jax.ShapeDtypeStruct((n, clusters), f32)] * (1 + len(others))
    outs += [jax.ShapeDtypeStruct((half + STAT_ROWS, clusters), f32)] * 2
    return pl.pallas_call(
        functools.partial(product_body, first, n, crosses, has_near),
        in_specs=[vmem] * len(args),
        out_specs=[vmem] * len(outs),
        out_shape=outs,
        scratch_shapes=[
            pltpu.VMEM((2 * half, 2 * clusters), jnp.bfloat16),
            pltpu.VMEM((max(n * len(others), 8), clusters), f32),
        ],
        compiler_params=pltpu.CompilerParams(vmem_limit_bytes=VMEM_BYTES),
        cost_estimate=pl.CostEstimate(
            flops=6 * (1 + len(others) + crosses) * n * 2 * half * clusters,
            bytes_accessed=8 * (1 + len(others)) * n * half,
            transcendentals=2 * half * clusters,
        ),
    )(*args)


def on_device(rows, cols, features, logits):
    n = logits.shape[0]
    column = lax.axis_index("col")
    masks = list(range(2, cols, 2))
    order = [0] + masks
    order = order + [k + 1 for k in order]
    has_near = int(rows % 2 == 0)
    half_rows = rows // 2
    if has_near:
        place = [2 * q if q < half_rows else 2 * (q - half_rows) + 1 for q in range(rows)]
        offsets = range(1, half_rows)
    else:
        place = list(range(rows))
        offsets = range(1, half_rows + 1)

    def by_col(x, mask):
        return lax.ppermute(x, "col", [(i, i ^ mask) for i in range(cols)])

    def near(x):
        return lax.ppermute(x, "row", [(i, i ^ 1) for i in range(rows)])

    def cross(x, d):
        return lax.ppermute(x, "row", [(place[(q + d) % rows], place[q]) for q in range(rows)])

    def cross_back(x, d):
        return lax.ppermute(x, "row", [(place[q], place[(q + d) % rows]) for q in range(rows)])

    def gather(x):
        crossed = [cross(x, d) for d in offsets]
        even = jnp.concatenate([x] + [by_col(x, k) for k in masks])
        nears = [near(x)] if has_near else []
        return even, by_col(even, 1), nears + crossed

    own_rows = lax.dynamic_slice_in_dim(features, column * n, n, 0)
    row_blocks = [cross(own_rows, d) for d in offsets]
    row_blocks = [own_rows] + ([near(own_rows)] if has_near else []) + row_blocks
    even, odd, others = gather(logits)
    plane = jnp.concatenate(
        [lax.dynamic_slice_in_dim(features, (column ^ k) * n, n, 0) for k in order]
    )
    kernels = []
    for block in row_blocks:
        kernels += kernel_block(block, plane)

    half = even.shape[0]
    stats = None
    for iteration in range(ITERS):
        outs = product_call(iteration == 0, n, has_near, stats, even, odd, others, kernels)
        own, back, t_even, t_odd = outs[0], outs[1:-2], outs[-2], outs[-1]
        back = list(back)
        scores = own
        if has_near:
            scores = scores + near(back.pop(0))
        for d, part in zip(offsets, back):
            scores = scores + cross_back(part, d)
        summed = t_even + by_col(t_odd, 1)
        stats = summed[half:]
        scores = scores + summed[:n]
        for j, k in enumerate(masks):
            sent = jnp.concatenate([summed[(j + 1) * n : (j + 2) * n], summed[half:]])
            part = by_col(sent, k)
            scores = scores + part[:n]
            stats = stats + part[n:]
        own_stats = stats
        for k in range(1, rows):
            stats = stats + lax.ppermute(
                own_stats, "row", [(i, (i + k) % rows) for i in range(rows)]
            )
        if iteration < ITERS - 1:
            even, odd, others = gather(scores)
    standardized = standardize(scores, stats[1:2], stats[0:1])
    members = normalize(jnp.exp(-2.0 * standardized))
    return (members, standardized)


def solution(mesh):
    return jax.shard_map(
        functools.partial(on_device, mesh.shape["row"], mesh.shape["col"]),
        mesh=mesh,
        in_specs=(P("row", None), P(("row", "col"), None)),
        out_specs=(P(("row", "col"), None), P(("row", "col"), None)),
        check_vma=False,
    )
```

```python
import functools

import jax
import jax.numpy as jnp
from jax import lax
from jax.experimental import pallas as pl
from jax.experimental.pallas import tpu as pltpu
from jax.sharding import PartitionSpec as P

ITERS = 2
STAT_ROWS = 8
BACK_ROWS = 16
VMEM_BYTES = 24 * 1024 * 1024


def split(x):
    high = x.astype(jnp.bfloat16)
    low = (x - high.astype(jnp.float32)).astype(jnp.bfloat16)
    return high, low


def kernel_body(order, own, column_ref, *refs):
    plane_ref, high_ref, low_ref = refs[-3:]
    n, total = high_ref.shape[0], plane_ref.shape[0]
    column = column_ref[0]

    def frames(k):
        start = pl.multiple_of(lax.bitwise_xor(column, k) * n, n)
        return plane_ref[pl.ds(start, n), :]

    rows = frames(0) if own else refs[0][...]
    for j, k in enumerate(order):
        inner = lax.dot_general(
            rows, frames(k), (((1,), (1,)), ((), ())), preferred_element_type=jnp.float32
        )
        t = inner / plane_ref.shape[1]
        high, low = split(t * (3.0 + t * (3.0 + t)))
        high_ref[:, j * n : (j + 1) * n] = high
        low_ref[:, j * n : (j + 1) * n] = low


def kernel_block(order, column, rows, plane, n):
    total, width = plane.shape
    vmem = pl.BlockSpec(memory_space=pltpu.VMEM)
    own = rows is None
    args = ([] if own else [rows]) + [plane]
    return pl.pallas_call(
        functools.partial(kernel_body, order, own),
        in_specs=[pl.BlockSpec(memory_space=pltpu.SMEM)] + [vmem] * len(args),
        out_specs=[vmem] * 2,
        out_shape=[jax.ShapeDtypeStruct((n, total), jnp.bfloat16)] * 2,
        compiler_params=pltpu.CompilerParams(vmem_limit_bytes=VMEM_BYTES),
        cost_estimate=pl.CostEstimate(
            flops=2 * n * total * width,
            bytes_accessed=2 * (n + total) * width + 4 * n * total,
            transcendentals=0,
        ),
    )(column, *args)


def standardize(scores, size, weighted):
    distance = weighted / (size * size) - 2.0 * scores / size
    centered = distance - jnp.mean(distance, axis=1, keepdims=True)
    spread = jnp.mean(centered * centered, axis=1, keepdims=True)
    return centered / jnp.sqrt(spread + 1e-06)


def normalize(raised):
    return raised / jnp.sum(raised, axis=1, keepdims=True)


VMEM = pl.BlockSpec(memory_space=pltpu.VMEM)
ANY = pl.BlockSpec(memory_space=pl.ANY)
F32 = jnp.float32


def call(body, args, outs, unused=(), scratch=(), flops=0):
    bytes_accessed = sum(x.size * x.dtype.itemsize for x in list(args) + list(outs))
    return pl.pallas_call(
        body,
        in_specs=[VMEM] * len(args) + [ANY] * len(unused),
        out_specs=[VMEM] * len(outs),
        out_shape=list(outs),
        scratch_shapes=list(scratch),
        compiler_params=pltpu.CompilerParams(vmem_limit_bytes=VMEM_BYTES),
        cost_estimate=pl.CostEstimate(
            flops=flops, bytes_accessed=bytes_accessed, transcendentals=0
        ),
    )(*args, *unused)


def shaped(rows, columns, dtype=F32):
    return jax.ShapeDtypeStruct((rows, columns), dtype)


def members_body(first, n, smalls, parts, others, unused, *refs):
    refs = list(refs)
    stats, refs = refs[:smalls], refs[smalls:]
    evens, refs = refs[:parts], refs[parts:]
    rest, refs = refs[:others], refs[others + unused :]
    even_hl, member = refs
    clusters = member.shape[1]
    if first:
        member_of = lambda x: normalize(jnp.exp(x))
    else:
        stat = stats[0][...]
        for ref in stats[1:]:
            stat += ref[...]
        for ref in rest:
            stat += ref[n:, :]
        weighted = stat[0:1, :]
        size = stat[1:2, :]
        member_of = lambda x: normalize(jnp.exp(-2.0 * standardize(x, size, weighted)))
    for j, src in enumerate(evens):
        m = member_of(src[...])
        high, low = split(m)
        even_hl[j * n : (j + 1) * n, :clusters] = high
        even_hl[j * n : (j + 1) * n, clusters:] = low
        if j == 0:
            member[:n, :] = m
    for i, src in enumerate(rest):
        member[(i + 1) * n : (i + 2) * n, :] = member_of(src[:n, :])


def members_call(first, n, stats, evens, others, unused):
    clusters = evens[0].shape[1]
    return call(
        functools.partial(
            members_body, first, n, len(stats), len(evens), len(others), len(unused)
        ),
        stats + evens + others,
        [
            shaped(n * len(evens), 2 * clusters, jnp.bfloat16),
            shaped(n * (1 + len(others)), clusters),
        ],
        unused,
    )


def product(high, low, members):
    clusters = members.shape[1] // 2
    both = jnp.dot(high, members, preferred_element_type=F32)
    rest = jnp.dot(low, members[:, :clusters], preferred_element_type=F32)
    return both[:, :clusters] + (both[:, clusters:] + rest)


def even_body(n, half, members, *refs):
    out = refs[-1]
    for i in range(len(refs) // 2):
        out[i * n : (i + 1) * n, :] = product(
            refs[2 * i][:, :half], refs[2 * i + 1][:, :half], members[...]
        )


def even_call(n, members, kernels):
    half, clusters = members.shape[0], members.shape[1] // 2
    rows = n * len(kernels) // 2
    return call(
        functools.partial(even_body, n, half),
        [members] + kernels,
        [shaped(rows, clusters)],
        flops=6 * rows * half * clusters,
    )[0]


def odd_body(n, has_near, members, partial, member, *refs):
    half, clusters = members.shape[0], members.shape[1] // 2
    blocks = partial.shape[0] // n
    kernels, refs = refs[: 2 * blocks], refs[2 * blocks :]
    outs, (t_even, t_odd) = refs[:blocks], refs[blocks:]
    total = None
    for i in range(blocks):
        rows = slice(i * n, (i + 1) * n)
        s = partial[rows, :] + product(
            kernels[2 * i][:, half:], kernels[2 * i + 1][:, half:], members[...]
        )
        outs[i][:n, :] = s
        if i > 0:
            outs[i][n:, :] = jnp.zeros((BACK_ROWS, clusters), F32)
        part = jnp.sum(member[rows, :] * s, axis=0, keepdims=True)
        if i > has_near:
            part = 2.0 * part
        total = part if total is None else total + part
    over = (((0,), (0,)), ((), ()))
    for part, dst in enumerate((t_even, t_odd)):
        columns = slice(part * half, (part + 1) * half)
        acc = jnp.zeros((half, clusters), F32)
        for i in range(has_near + 1, blocks):
            high, low = split(member[i * n : (i + 1) * n, :])
            both = jnp.concatenate([high, low], axis=1)
            a = lax.dot_general(
                kernels[2 * i][:, columns], both, over, preferred_element_type=F32
            )
            b = lax.dot_general(
                kernels[2 * i + 1][:, columns], high, over, preferred_element_type=F32
            )
            acc += a[:, :clusters] + (a[:, clusters:] + b)
        dst[:half, :] = acc
    row = lax.broadcasted_iota(jnp.int32, (STAT_ROWS, clusters), 0)
    size = jnp.sum(member[:n, :], axis=0, keepdims=True)
    stat = jnp.where(row == 0, total, jnp.where(row == 1, size, 0.0))
    t_even[half:, :] = stat
    t_odd[half:, :] = stat


def odd_call(n, has_near, members, partial, member, kernels):
    half, clusters = members.shape[0], members.shape[1] // 2
    blocks = partial.shape[0] // n
    return call(
        functools.partial(odd_body, n, has_near),
        [members, partial, member] + kernels,
        [shaped(n, clusters)]
        + [shaped(n + BACK_ROWS, clusters)] * (blocks - 1)
        + [shaped(half + STAT_ROWS, clusters)] * 2,
        flops=6 * (2 * blocks - has_near) * n * half * clusters,
    )


def fold_body(n, t_even, received, *outs):
    half = t_even.shape[0] - STAT_ROWS
    stat = t_even[half:, :] + received[half:, :]
    for j, out in enumerate(outs):
        rows = slice(j * n, (j + 1) * n)
        out[:n, :] = t_even[rows, :] + received[rows, :]
        out[n:, :] = stat


def sum_body(n, *refs):
    wide, backs, (full, scores, stats) = refs[0], refs[1:-3], refs[-3:]
    total = wide[:n, :]
    stat = wide[n:, :]
    for ref in backs:
        total += ref[:n, :]
        if ref.shape[0] == n + STAT_ROWS:
            stat += ref[n:, :]
    full[:n, :] = total
    full[n:, :] = stat
    scores[...] = total
    stats[...] = stat


def finish_body(scores, *refs):
    stats, (members, standardized) = refs[:-2], refs[-2:]
    stat = stats[0][...]
    for ref in stats[1:]:
        stat += ref[...]
    x = standardize(scores[...], stat[1:2, :], stat[0:1, :])
    standardized[...] = x
    members[...] = normalize(jnp.exp(-2.0 * x))


def on_device(rows, cols, features, logits):
    n = logits.shape[0]
    column = lax.axis_index("col")
    masks = list(range(2, cols, 2))
    order = [0] + masks
    order = order + [k + 1 for k in order]
    has_near = int(rows % 2 == 0)
    half_rows = rows // 2
    if has_near:
        place = [2 * q if q < half_rows else 2 * (q - half_rows) + 1 for q in range(rows)]
        offsets = list(range(1, half_rows))
    else:
        place = list(range(rows))
        offsets = list(range(1, half_rows + 1))

    def by_col(x, mask):
        return lax.ppermute(x, "col", [(i, i ^ mask) for i in range(cols)])

    def near(x):
        return lax.ppermute(x, "row", [(i, i ^ 1) for i in range(rows)])

    def shift(x, d):
        return lax.ppermute(x, "row", [(place[(q + d) % rows], place[q]) for q in range(rows)])

    own_rows = lax.dynamic_slice_in_dim(features, column * n, n, 0)
    row_blocks = [None] + ([near(own_rows)] if has_near else [])
    row_blocks += [shift(own_rows, d) for d in offsets]
    index = jnp.reshape(column, (1,)).astype(jnp.int32)
    kernels = []
    for block in row_blocks:
        kernels += kernel_block(tuple(order), index, block, features, n)

    evens = [logits] + [by_col(logits, k) for k in masks]
    padded = jnp.pad(logits, ((0, BACK_ROWS), (0, 0)))
    others = ([near(logits)] if has_near else []) + [shift(padded, d) for d in offsets]
    stats, after = [], kernels[1::2]
    for iteration in range(ITERS):
        even, member = members_call(iteration == 0, n, stats, evens, others, after)
        odd = by_col(even, 1)
        partial = even_call(n, even, kernels)
        outs = odd_call(n, has_near, odd, partial, member, kernels)
        own, back, t_even, t_odd = outs[0], list(outs[1:-2]), outs[-2], outs[-1]
        clusters = own.shape[1]
        sent = call(
            functools.partial(fold_body, n),
            [t_even, by_col(t_odd, 1)],
            [shaped(n + STAT_ROWS, clusters)] * (1 + len(masks)),
        )
        parts = [by_col(x, k) for k, x in zip(masks, sent[1:])]
        back = [
            near(x) if d == 0 else shift(x, -d)
            for d, x in zip(([0] if has_near else []) + offsets, back)
        ]
        full, scores, stats = call(
            functools.partial(sum_body, n),
            [sent[0], own] + back + parts,
            [shaped(n + STAT_ROWS, clusters), shaped(n, clusters), shaped(STAT_ROWS, clusters)],
        )
        if iteration < ITERS - 1:
            evens = [scores] + [by_col(scores, k) for k in masks]
            others = ([near(full)] if has_near else []) + [shift(full, d) for d in offsets]
            stats = [stats] + [shift(stats, -d) for d in offsets]
            after = []
    stats = [stats] + [shift(stats, d) for d in range(1, rows)]
    return tuple(call(finish_body, [scores] + stats, [shaped(*scores.shape)] * 2))


def solution(mesh):
    return jax.shard_map(
        functools.partial(on_device, mesh.shape["row"], mesh.shape["col"]),
        mesh=mesh,
        in_specs=(P("row", None), P(("row", "col"), None)),
        out_specs=(P(("row", "col"), None), P(("row", "col"), None)),
        check_vma=False,
    )
```

```python
import functools

import jax
import jax.numpy as jnp
from jax import lax
from jax.experimental import pallas as pl
from jax.experimental.pallas import tpu as pltpu
from jax.sharding import PartitionSpec as P

ITERS = 2
STAT_ROWS = 8
BACK_ROWS = 16
VMEM_BYTES = 24 * 1024 * 1024
VMEM = pl.BlockSpec(memory_space=pltpu.VMEM)
SMEM = pl.BlockSpec(memory_space=pltpu.SMEM)
ANY = pl.BlockSpec(memory_space=pl.ANY)
HBM = pl.BlockSpec(memory_space=pltpu.HBM)
BF16 = jnp.bfloat16
F32 = jnp.float32


def shaped(rows, columns, dtype=F32):
    return jax.ShapeDtypeStruct((rows, columns), dtype)


def call(body, args, outs, specs=None, scratch=(), flops=0, hidden=False):
    bytes_accessed = sum(x.size * x.dtype.itemsize for x in list(args) + list(outs))
    if hidden:
        flops = bytes_accessed = 0
    made = pl.pallas_call(
        body,
        in_specs=specs or [VMEM] * len(args),
        out_specs=[VMEM] * len(outs),
        out_shape=list(outs),
        scratch_shapes=list(scratch),
        compiler_params=pltpu.CompilerParams(vmem_limit_bytes=VMEM_BYTES),
        cost_estimate=pl.CostEstimate(
            flops=flops, bytes_accessed=bytes_accessed, transcendentals=0
        ),
    )(*args)
    return list(made)


def split(x):
    high = x.astype(BF16)
    low = (x - high.astype(F32)).astype(BF16)
    return high, low


def whole(pair):
    clusters = pair.shape[1] // 2
    return pair[:, :clusters].astype(F32) + pair[:, clusters:].astype(F32)


def standardize(scores, size, weighted):
    distance = weighted / (size * size) - 2.0 * scores / size
    centered = distance - jnp.mean(distance, axis=1, keepdims=True)
    spread = jnp.mean(centered * centered, axis=1, keepdims=True)
    return centered / jnp.sqrt(spread + 1e-06)


def normalize(raised):
    return raised / jnp.sum(raised, axis=1, keepdims=True)


def store_pair(out, rows, x):
    clusters = x.shape[1]
    high, low = split(x)
    out[rows, :clusters] = high
    out[rows, clusters:] = low


def prepare_body(column_ref, features, logits, message, pair, sem):
    n, clusters = logits.shape
    width = features.shape[1]
    start = pl.multiple_of(column_ref[0] * n, n)
    copy = pltpu.make_async_copy(
        features.at[pl.ds(start, n), :], message.at[:, pl.ds(0, width)], sem
    )
    copy.start()
    high, low = split(normalize(jnp.exp(logits[...])))
    pair[:, :clusters] = high
    pair[:, clusters:] = low
    message[:, width : width + clusters] = high
    message[:, width + clusters :] = low
    copy.wait()


def kernel_body(order, column_ref, rows_ref, plane_ref, *refs):
    high_ref, low_ref = refs[-2:]
    n, width = rows_ref.shape[0], plane_ref.shape[1]
    column = column_ref[0]
    rows = rows_ref[:, :width]
    for j, k in enumerate(order):
        start = pl.multiple_of(lax.bitwise_xor(column, k) * n, n)
        inner = lax.dot_general(
            rows,
            plane_ref[pl.ds(start, n), :],
            (((1,), (1,)), ((), ())),
            preferred_element_type=F32,
        )
        t = inner / width
        high, low = split(t * (3.0 + t * (3.0 + t)))
        high_ref[:, j * n : (j + 1) * n] = high
        low_ref[:, j * n : (j + 1) * n] = low


def kernel_call(order, column, rows, plane, after=()):
    n, total = rows.shape[0], plane.shape[0]
    return call(
        functools.partial(kernel_body, tuple(order)),
        [column, rows, plane, *after],
        [shaped(n, total, BF16)] * 2,
        [SMEM, VMEM, VMEM] + [ANY] * len(after),
        hidden=True,
    )


def scores_body(at, pieces, kernels, partials, *refs):
    members, refs = refs[:pieces], refs[pieces:]
    blocks, refs = refs[:kernels], refs[kernels:]
    before, outs = refs[:partials], refs[partials:]
    n = blocks[0].shape[0]
    clusters = members[0].shape[1] // 2
    for i, out in enumerate(outs):
        both, rest, start = None, None, at
        for piece in members:
            columns = slice(start, start + piece.shape[0])
            start += piece.shape[0]
            a = jnp.dot(blocks[2 * i][:, columns], piece[...], preferred_element_type=F32)
            b = jnp.dot(
                blocks[2 * i + 1][:, columns],
                piece[:, :clusters],
                preferred_element_type=F32,
            )
            both = a if both is None else both + a
            rest = b if rest is None else rest + b
        s = both[:, :clusters] + (both[:, clusters:] + rest)
        if partials:
            s += before[i][:n, :]
        out[:n, :] = s
        if out.shape[0] > n:
            out[n:, :] = jnp.zeros((out.shape[0] - n, clusters), F32)


def scores_call(at, members, kernels, partials, extra, hidden=False):
    n, clusters = kernels[0].shape[0], members[0].shape[1] // 2
    depth = sum(x.shape[0] for x in members)
    return call(
        functools.partial(scores_body, at, len(members), len(kernels), len(partials)),
        members + kernels + partials,
        [shaped(n + e, clusters) for e in extra],
        flops=3 * n * len(kernels) * depth * clusters,
        hidden=hidden,
    )


def members_body(n, smalls, evens, others, *refs):
    stats, refs = refs[:smalls], refs[smalls:]
    own, refs = refs[:evens], refs[evens:]
    rest, refs = refs[:others], refs[others:]
    even, pairs = refs[0], refs[1:]
    stat = stats[0][...]
    for ref in stats[1:]:
        stat += ref[...]
    for ref in rest:
        stat += ref[n:, :]
    weighted, size = stat[0:1, :], stat[1:2, :]

    def member_of(x):
        return normalize(jnp.exp(-2.0 * standardize(x, size, weighted)))

    for j, ref in enumerate(own):
        store_pair(even, slice(j * n, (j + 1) * n), member_of(ref[...]))
    for pair, ref in zip(pairs, rest):
        store_pair(pair, slice(0, n), member_of(ref[:n, :]))


def members_call(n, stats, evens, others):
    clusters = evens[0].shape[1]
    return call(
        functools.partial(members_body, n, len(stats), len(evens), len(others)),
        stats + evens + others,
        [shaped(n * len(evens), 2 * clusters, BF16)]
        + [shaped(n, 2 * clusters, BF16)] * len(others),
    )


def stat_body(has_near, own, *refs):
    out, refs = refs[-1], refs[:-1]
    count = len(refs) // 2
    scores, pairs = refs[: count + 1], refs[count + 1 :]
    n, clusters = scores[0].shape
    member = whole(own[:n, :])
    total = jnp.sum(member * scores[0][...], axis=0, keepdims=True)
    for i in range(count):
        pair = pairs[i]
        other = whole(pair[:, pair.shape[1] - 2 * clusters :])
        part = jnp.sum(other * scores[i + 1][:n, :], axis=0, keepdims=True)
        total += part if i < has_near else 2.0 * part
    size = jnp.sum(member, axis=0, keepdims=True)
    row = lax.broadcasted_iota(jnp.int32, out.shape, 0)
    out[...] = jnp.where(row == 0, total, jnp.where(row == 1, size, 0.0))


def stat_call(has_near, own, scores, pairs):
    clusters = scores[0].shape[1]
    return call(
        functools.partial(stat_body, has_near),
        [own] + scores + pairs,
        [shaped(STAT_ROWS, clusters)],
    )[0]


def other_body(count, *refs):
    pairs, refs = refs[:count], refs[count:]
    kernels, refs = refs[: 2 * count], refs[2 * count :]
    stat, (even, odd) = refs[:-2], refs[-2:]
    half, clusters = even.shape
    over = (((0,), (0,)), ((), ()))
    for part, out in enumerate((odd, even)):
        columns = slice((1 - part) * half, (2 - part) * half)
        acc = jnp.zeros((half, clusters), F32)
        for i, pair in enumerate(pairs):
            both = pair[:, pair.shape[1] - 2 * clusters :]
            a = lax.dot_general(
                kernels[2 * i][:, columns], both, over, preferred_element_type=F32
            )
            b = lax.dot_general(
                kernels[2 * i + 1][:, columns],
                both[:, :clusters],
                over,
                preferred_element_type=F32,
            )
            acc += a[:, :clusters] + (a[:, clusters:] + b)
        out[:half, :] = acc
    if stat:
        odd[half:, :] = stat[0][...]


def other_call(half, clusters, pairs, kernels, stat):
    n = pairs[0].shape[0] if pairs else 0
    return call(
        functools.partial(other_body, len(pairs)),
        pairs + kernels + stat,
        [shaped(half, clusters), shaped(half + STAT_ROWS * len(stat), clusters)],
        flops=12 * n * len(pairs) * half * clusters,
    )


def fold_body(n, count, even, received, *refs):
    stats, outs = refs[:count], refs[count:]
    half = even.shape[0]
    stat = stats[0][...]
    for ref in stats[1:]:
        stat += ref[...]
    if received.shape[0] > half:
        stat += received[half:, :]
    for j, out in enumerate(outs):
        rows = slice(j * n, (j + 1) * n)
        out[:n, :] = even[rows, :] + received[rows, :]
        out[n:, :] = stat


def sum_body(n, last, *refs):
    many = 2 if last else 3
    refs, outs = refs[:-many], refs[-many:]
    total, stat = refs[0][:n, :], refs[0][n:, :]
    for ref in refs[1:]:
        total += ref[:n, :]
        if ref.shape[0] == n + STAT_ROWS:
            stat += ref[n:, :]
    if last:
        members, standardized = outs
        x = standardize(total, stat[1:2, :], stat[0:1, :])
        standardized[...] = x
        members[...] = normalize(jnp.exp(-2.0 * x))
    else:
        full, scores, stats = outs
        full[:n, :] = total
        full[n:, :] = stat
        scores[...] = total
        stats[...] = stat


def on_device(rows, cols, features, logits):
    n, clusters = logits.shape
    width = features.shape[1]
    half = n * cols // 2
    masks = list(range(2, cols, 2))
    order = [0] + masks
    order = order + [k + 1 for k in order]
    has_near = int(rows % 2 == 0)
    half_rows = rows // 2
    if has_near:
        place = [2 * q if q < half_rows else 2 * (q - half_rows) + 1 for q in range(rows)]
        offsets = list(range(1, half_rows))
    else:
        place = list(range(rows))
        offsets = list(range(1, half_rows + 1))
    steps = ([0] if has_near else []) + offsets

    def by_col(x, mask):
        return lax.ppermute(x, "col", [(i, i ^ mask) for i in range(cols)])

    def shift(x, d):
        if d == 0:
            pairs = [(i, i ^ 1) for i in range(rows)]
        else:
            pairs = [(place[(q + d) % rows], place[q]) for q in range(rows)]
        return lax.ppermute(x, "row", pairs)

    column = jnp.reshape(lax.axis_index("col"), (1,)).astype(jnp.int32)
    message, pair = call(
        prepare_body,
        [column, features, logits],
        [shaped(n, width + 2 * clusters, BF16), shaped(n, 2 * clusters, BF16)],
        [SMEM, HBM, VMEM],
        [pltpu.SemaphoreType.DMA],
    )
    others = [shift(message, d) for d in steps]
    members = [pair] + [by_col(pair, k) for k in order[1:]]
    early = 1 + has_near
    extra = [0] + [BACK_ROWS] * len(steps)
    rows_of = [message] + others
    kernels = []
    for x in rows_of[:early]:
        kernels += kernel_call(order, column, x, features)
    scores = scores_call(0, members, kernels, [], extra[:early], True)
    cross = []
    for x in rows_of[early:]:
        cross += kernel_call(order, column, x, features, scores)
    scores += scores_call(0, members, cross, [], extra[early:], True)
    kernels += cross
    own = pair

    for iteration in range(ITERS):
        last = iteration == ITERS - 1
        if iteration > 0:
            even, *others = members_call(n, stats, evens, others)
            odd = by_col(even, 1)
            scores = scores_call(0, [even], kernels, [], extra)
            scores = scores_call(half, [odd], kernels, scores, extra)
            own = even
        stat = stat_call(has_near, own, scores, others)
        t_even, t_odd = other_call(
            half, clusters, others[has_near:], cross, [] if last else [stat]
        )
        if last:
            planes = [shift(stat, d) for d in list(range(1, rows))]
            for x in planes:
                stat = stat + x
            stats = [stat, by_col(stat, 1)]
        else:
            stats = [stat]
        sent = call(
            functools.partial(fold_body, n, len(stats)),
            [t_even, by_col(t_odd, 1)] + stats,
            [shaped(n + STAT_ROWS, clusters)] * (1 + len(masks)),
        )
        parts = [by_col(x, k) for k, x in zip(masks, sent[1:])]
        back = [shift(x, -d) for d, x in zip(steps, scores[1:])]
        outs = [shaped(n, clusters)] * 2
        if not last:
            outs = [shaped(n + STAT_ROWS, clusters), outs[0], shaped(STAT_ROWS, clusters)]
        done = call(
            functools.partial(sum_body, n, last),
            [sent[0], scores[0]] + back + parts,
            outs,
        )
        if not last:
            full, total, stats = done
            evens = [total] + [by_col(total, k) for k in masks]
            others = [shift(full, d) for d in steps]
            stats = [stats] + [shift(stats, -d) for d in offsets]
    return tuple(done)


def solution(mesh):
    return jax.shard_map(
        functools.partial(on_device, mesh.shape["row"], mesh.shape["col"]),
        mesh=mesh,
        in_specs=(P("row", None), P(("row", "col"), None)),
        out_specs=(P(("row", "col"), None), P(("row", "col"), None)),
        check_vma=False,
    )
```

```python
import functools

import jax
import jax.numpy as jnp
from jax import lax
from jax.experimental import pallas as pl
from jax.experimental.pallas import tpu as pltpu
from jax.sharding import PartitionSpec as P

ITERS = 2
STAT_ROWS = 8
BACK_ROWS = 16
VMEM_BYTES = 24 * 1024 * 1024
PREPARE_BYTES = 62 * 1024 * 1024
VMEM = pl.BlockSpec(memory_space=pltpu.VMEM)
SMEM = pl.BlockSpec(memory_space=pltpu.SMEM)
ANY = pl.BlockSpec(memory_space=pl.ANY)
HBM = pl.BlockSpec(memory_space=pltpu.HBM)
BF16 = jnp.bfloat16
F32 = jnp.float32


def shaped(rows, columns, dtype=F32):
    return jax.ShapeDtypeStruct((rows, columns), dtype)


def call(body, args, outs, specs=None, scratch=(), flops=0, hidden=False, vmem=None):
    bytes_accessed = sum(x.size * x.dtype.itemsize for x in list(args) + list(outs))
    if hidden:
        flops = bytes_accessed = 0
    made = pl.pallas_call(
        body,
        in_specs=specs or [VMEM] * len(args),
        out_specs=[VMEM] * len(outs),
        out_shape=list(outs),
        scratch_shapes=list(scratch),
        compiler_params=pltpu.CompilerParams(vmem_limit_bytes=vmem or VMEM_BYTES),
        cost_estimate=pl.CostEstimate(
            flops=flops, bytes_accessed=bytes_accessed, transcendentals=0
        ),
    )(*args)
    return list(made)


def split(x):
    high = x.astype(BF16)
    low = (x - high.astype(F32)).astype(BF16)
    return high, low


def whole(pair):
    clusters = pair.shape[1] // 2
    return pair[:, :clusters].astype(F32) + pair[:, clusters:].astype(F32)


def standardize(scores, size, weighted):
    distance = weighted / (size * size) - 2.0 * scores / size
    centered = distance - jnp.mean(distance, axis=1, keepdims=True)
    spread = jnp.mean(centered * centered, axis=1, keepdims=True)
    return centered / jnp.sqrt(spread + 1e-06)


def normalize(raised):
    return raised / jnp.sum(raised, axis=1, keepdims=True)


def store_pair(out, rows, x):
    clusters = x.shape[1]
    high, low = split(x)
    out[rows, :clusters] = high
    out[rows, clusters:] = low


def prepare_body(column_ref, features, logits, near, cross, pair, sems):
    n, clusters = logits.shape
    width = features.shape[1]
    start = pl.multiple_of(column_ref[0] * n, n)
    copies = [
        pltpu.make_async_copy(
            features.at[pl.ds(start, n), :],
            out.at[pl.ds(0, n), pl.ds(0, width)],
            sems.at[i],
        )
        for i, out in enumerate((near, cross))
    ]
    for copy in copies:
        copy.start()
    rows = slice(0, n)
    high, low = split(normalize(jnp.exp(logits[...])))
    for out, at in ((pair, 0), (near, width), (cross, width)):
        out[rows, at : at + clusters] = high
        out[rows, at + clusters : at + 2 * clusters] = low
    cross[n:, :] = jnp.zeros((cross.shape[0] - n, cross.shape[1]), BF16)
    for copy in copies:
        copy.wait()


def kernel_body(order, column_ref, rows_ref, plane_ref, *refs):
    high_ref, low_ref = refs[-2:]
    n, width = high_ref.shape[0], plane_ref.shape[1]
    column = column_ref[0]
    rows = rows_ref[:n, :width]
    for j, k in enumerate(order):
        start = pl.multiple_of(lax.bitwise_xor(column, k) * n, n)
        inner = lax.dot_general(
            rows,
            plane_ref[pl.ds(start, n), :],
            (((1,), (1,)), ((), ())),
            preferred_element_type=F32,
        )
        t = inner / width
        high, low = split(t * (3.0 + t * (3.0 + t)))
        high_ref[:, j * n : (j + 1) * n] = high
        low_ref[:, j * n : (j + 1) * n] = low


def kernel_call(n, order, column, rows, plane, after=()):
    total = plane.shape[0]
    return call(
        functools.partial(kernel_body, tuple(order)),
        [column, rows, plane, *after],
        [shaped(n, total, BF16)] * 2,
        [SMEM, VMEM, VMEM] + [ANY] * len(after),
        hidden=True,
    )


def scores_body(at, pieces, kernels, partials, unused, *refs):
    members, refs = refs[:pieces], refs[pieces:]
    blocks, refs = refs[:kernels], refs[kernels:]
    before, outs = refs[:partials], refs[partials + unused :]
    n = blocks[0].shape[0]
    clusters = members[0].shape[1] // 2
    for i, out in enumerate(outs):
        both, rest, start = None, None, at
        for piece in members:
            columns = slice(start, start + piece.shape[0])
            start += piece.shape[0]
            a = jnp.dot(blocks[2 * i][:, columns], piece[...], preferred_element_type=F32)
            b = jnp.dot(
                blocks[2 * i + 1][:, columns],
                piece[:, :clusters],
                preferred_element_type=F32,
            )
            both = a if both is None else both + a
            rest = b if rest is None else rest + b
        s = both[:, :clusters] + (both[:, clusters:] + rest)
        if partials:
            s += before[i][:n, :]
        out[:n, :] = s
        if out.shape[0] > n:
            out[n:, :] = jnp.zeros((out.shape[0] - n, clusters), F32)


def scores_call(at, members, kernels, partials, extra, hidden=False, after=()):
    n, clusters = kernels[0].shape[0], members[0].shape[1] // 2
    depth = sum(x.shape[0] for x in members)
    return call(
        functools.partial(
            scores_body, at, len(members), len(kernels), len(partials), len(after)
        ),
        [*members, *kernels, *partials, *after],
        [shaped(n + e, clusters) for e in extra],
        [VMEM] * (len(members) + len(kernels) + len(partials)) + [ANY] * len(after),
        flops=3 * n * len(kernels) * depth * clusters,
        hidden=hidden,
    )


def members_body(n, smalls, evens, others, *refs):
    stats, refs = refs[:smalls], refs[smalls:]
    own, refs = refs[:evens], refs[evens:]
    rest, refs = refs[:others], refs[others:]
    even, pairs = refs[0], refs[1:]
    stat = stats[0][...]
    for ref in stats[1:]:
        stat += ref[...]
    for ref in rest:
        stat += ref[n:, :]
    weighted, size = stat[0:1, :], stat[1:2, :]

    def member_of(x):
        return normalize(jnp.exp(-2.0 * standardize(x, size, weighted)))

    for j, ref in enumerate(own):
        store_pair(even, slice(j * n, (j + 1) * n), member_of(ref[...]))
    for pair, ref in zip(pairs, rest):
        store_pair(pair, slice(0, n), member_of(ref[:n, :]))


def members_call(n, stats, evens, others):
    clusters = evens[0].shape[1]
    return call(
        functools.partial(members_body, n, len(stats), len(evens), len(others)),
        stats + evens + others,
        [shaped(n * len(evens), 2 * clusters, BF16)]
        + [shaped(n, 2 * clusters, BF16)] * len(others),
    )


def stat_body(has_near, own, *refs):
    out, refs = refs[-1], refs[:-1]
    count = len(refs) // 2
    scores, pairs = refs[: count + 1], refs[count + 1 :]
    n, clusters = scores[0].shape
    member = whole(own[:n, :])
    total = jnp.sum(member * scores[0][...], axis=0, keepdims=True)
    for i in range(count):
        pair = pairs[i]
        other = whole(pair[:n, pair.shape[1] - 2 * clusters :])
        part = jnp.sum(other * scores[i + 1][:n, :], axis=0, keepdims=True)
        total += part if i < has_near else 2.0 * part
    size = jnp.sum(member, axis=0, keepdims=True)
    row = lax.broadcasted_iota(jnp.int32, out.shape, 0)
    out[...] = jnp.where(row == 0, total, jnp.where(row == 1, size, 0.0))


def stat_call(has_near, own, scores, pairs):
    clusters = scores[0].shape[1]
    return call(
        functools.partial(stat_body, has_near),
        [own] + scores + pairs,
        [shaped(STAT_ROWS, clusters)],
    )[0]


def other_body(n, count, *refs):
    pairs, refs = refs[:count], refs[count:]
    kernels, refs = refs[: 2 * count], refs[2 * count :]
    stat, (even, odd) = refs[:-2], refs[-2:]
    half, clusters = even.shape
    over = (((0,), (0,)), ((), ()))
    for part, out in enumerate((odd, even)):
        columns = slice((1 - part) * half, (2 - part) * half)
        acc = jnp.zeros((half, clusters), F32)
        for i, pair in enumerate(pairs):
            both = pair[:n, pair.shape[1] - 2 * clusters :]
            a = lax.dot_general(
                kernels[2 * i][:, columns], both, over, preferred_element_type=F32
            )
            b = lax.dot_general(
                kernels[2 * i + 1][:, columns],
                both[:, :clusters],
                over,
                preferred_element_type=F32,
            )
            acc += a[:, :clusters] + (a[:, clusters:] + b)
        out[:half, :] = acc
    if stat:
        odd[half:, :] = stat[0][...]


def other_call(n, half, clusters, pairs, kernels, stat):
    return call(
        functools.partial(other_body, n, len(pairs)),
        pairs + kernels + stat,
        [shaped(half, clusters), shaped(half + STAT_ROWS * len(stat), clusters)],
        flops=12 * n * len(pairs) * half * clusters,
    )


def fold_body(n, count, even, received, *refs):
    stats, outs = refs[:count], refs[count:]
    half = even.shape[0]
    for j, out in enumerate(outs):
        rows = slice(j * n, (j + 1) * n)
        out[:n, :] = even[rows, :] + received[rows, :]
        if count:
            out[n:, :] = stats[0][...] + received[half:, :]


def fold_call(n, even, received, stats, extra):
    half, clusters = even.shape
    return call(
        functools.partial(fold_body, n, len(stats)),
        [even, received] + stats,
        [shaped(n + extra, clusters)] * (half // n),
    )


def widen_body(n, *refs):
    count = (len(refs) - 2) // 2
    stat = refs[count][...] + refs[count + 1][...]
    for ref, out in zip(refs[:count], refs[count + 2 :]):
        out[:n, :] = ref[...]
        out[n:, :] = stat


def widen_call(n, parts, stats):
    clusters = parts[0].shape[1]
    return call(
        functools.partial(widen_body, n),
        parts + stats,
        [shaped(n + STAT_ROWS, clusters)] * len(parts),
    )


def sum_body(n, last, *refs):
    many = 2 if last else 3
    refs, outs = refs[:-many], refs[-many:]
    total, stat = refs[0][:n, :], refs[0][n:, :]
    for ref in refs[1:]:
        total += ref[:n, :]
        if ref.shape[0] == n + STAT_ROWS:
            stat += ref[n:, :]
    if last:
        members, standardized = outs
        x = standardize(total, stat[1:2, :], stat[0:1, :])
        standardized[...] = x
        members[...] = normalize(jnp.exp(-2.0 * x))
    else:
        full, scores, stats = outs
        full[:n, :] = total
        full[n:, :] = stat
        scores[...] = total
        stats[...] = stat


def on_device(rows, cols, features, logits):
    n, clusters = logits.shape
    width = features.shape[1]
    half = n * cols // 2
    masks = list(range(2, cols, 2))
    order = [0] + masks
    order = order + [k + 1 for k in order]
    has_near = int(rows % 2 == 0)
    half_rows = rows // 2
    if has_near:
        place = [2 * q if q < half_rows else 2 * (q - half_rows) + 1 for q in range(rows)]
        offsets = list(range(1, half_rows))
    else:
        place = list(range(rows))
        offsets = list(range(1, half_rows + 1))
    steps = ([0] if has_near else []) + offsets

    def by_col(x, mask):
        return lax.ppermute(x, "col", [(i, i ^ mask) for i in range(cols)])

    def shift(x, d):
        if d == 0:
            pairs = [(i, i ^ 1) for i in range(rows)]
        else:
            pairs = [(place[(q + d) % rows], place[q]) for q in range(rows)]
        return lax.ppermute(x, "row", pairs)

    column = jnp.reshape(lax.axis_index("col"), (1,)).astype(jnp.int32)
    message, wide, pair = call(
        prepare_body,
        [column, features, logits],
        [
            shaped(n, width + 2 * clusters, BF16),
            shaped(n + BACK_ROWS, width + 2 * clusters, BF16),
            shaped(n, 2 * clusters, BF16),
        ],
        [SMEM, ANY, VMEM],
        [pltpu.SemaphoreType.DMA((2,))],
        vmem=PREPARE_BYTES,
    )
    others = [shift(message if d == 0 else wide, d) for d in steps]
    evens = [pair] + [by_col(pair, k) for k in masks]
    members = evens + [by_col(x, 1) for x in evens]
    early = 1 + has_near
    extra = [0] + [BACK_ROWS] * len(steps)
    rows_of = [message] + others
    kernels = []
    for x in rows_of[:early]:
        kernels += kernel_call(n, order, column, x, features)
    scores = scores_call(0, members, kernels, [], extra[:early], True)
    cross = []
    for x in rows_of[early:]:
        cross += kernel_call(n, order, column, x, features, scores)
    scores += scores_call(0, members, cross, [], extra[early:], True)
    kernels += cross
    own = pair

    for iteration in range(ITERS):
        last = iteration == ITERS - 1
        if iteration > 0:
            even, *others = members_call(n, stats, evens, others)
            odd = by_col(even, 1)
            own = even
            scores = scores_call(0, [even], kernels, [], extra)
        if last:
            t_even, t_odd = other_call(n, half, clusters, others[has_near:], cross, [])
            sent = fold_call(n, t_even, by_col(t_odd, 1), [], 0)
            scores = scores_call(half, [odd], kernels, scores, extra, after=sent[:1])
            stat = stat_call(has_near, own, scores, others)
            for x in [shift(stat, d) for d in range(1, rows)]:
                stat = stat + x
            sent = widen_call(n, sent, [stat, by_col(stat, 1)])
        else:
            if iteration > 0:
                scores = scores_call(half, [odd], kernels, scores, extra)
            stat = stat_call(has_near, own, scores, others)
            t_even, t_odd = other_call(n, half, clusters, others[has_near:], cross, [stat])
            sent = fold_call(n, t_even, by_col(t_odd, 1), [stat], STAT_ROWS)
        parts = [by_col(x, k) for k, x in zip(masks, sent[1:])]
        back = [shift(x, -d) for d, x in zip(steps, scores[1:])]
        outs = [shaped(n, clusters)] * 2
        if not last:
            outs = [shaped(n + STAT_ROWS, clusters), outs[0], shaped(STAT_ROWS, clusters)]
        done = call(
            functools.partial(sum_body, n, last),
            [sent[0], scores[0]] + back + parts,
            outs,
        )
        if not last:
            full, total, stats = done
            evens = [total] + [by_col(total, k) for k in masks]
            others = [shift(full, d) for d in steps]
            stats = [stats] + [shift(stats, -d) for d in offsets]
    return tuple(done)


def solution(mesh):
    return jax.shard_map(
        functools.partial(on_device, mesh.shape["row"], mesh.shape["col"]),
        mesh=mesh,
        in_specs=(P("row", None), P(("row", "col"), None)),
        out_specs=(P(("row", "col"), None), P(("row", "col"), None)),
        check_vma=False,
    )
```

```python
import functools

import jax
import jax.numpy as jnp
from jax import lax
from jax.experimental import pallas as pl
from jax.experimental.pallas import tpu as pltpu
from jax.sharding import PartitionSpec as P

ITERS = 2
STAT_ROWS = 8
WIDE_ROWS = 16
BACK_ROWS = 16
VMEM_BYTES = 24 * 1024 * 1024
KERNEL_FLOPS = 5.4
VMEM = pl.BlockSpec(memory_space=pltpu.VMEM)
SMEM = pl.BlockSpec(memory_space=pltpu.SMEM)
ANY = pl.BlockSpec(memory_space=pl.ANY)
BF16 = jnp.bfloat16
F32 = jnp.float32


def shaped(rows, columns, dtype=F32):
    return jax.ShapeDtypeStruct((rows, columns), dtype)


def call(body, args, outs, specs=None, scratch=(), flops=0, hidden=False):
    bytes_accessed = sum(x.size * x.dtype.itemsize for x in list(args) + list(outs))
    if hidden:
        flops = bytes_accessed = 0
    made = pl.pallas_call(
        body,
        in_specs=specs or [VMEM] * len(args),
        out_specs=[VMEM] * len(outs),
        out_shape=list(outs),
        scratch_shapes=list(scratch),
        compiler_params=pltpu.CompilerParams(vmem_limit_bytes=VMEM_BYTES),
        cost_estimate=pl.CostEstimate(
            flops=flops, bytes_accessed=bytes_accessed, transcendentals=0
        ),
    )(*args)
    return list(made)


def split(x):
    high = x.astype(BF16)
    low = (x - high.astype(F32)).astype(BF16)
    return high, low


def whole(pair):
    clusters = pair.shape[1] // 2
    return pair[:, :clusters].astype(F32) + pair[:, clusters:].astype(F32)


def standardize(scores, size, weighted):
    distance = weighted / (size * size) - 2.0 * scores / size
    centered = distance - jnp.mean(distance, axis=1, keepdims=True)
    spread = jnp.mean(centered * centered, axis=1, keepdims=True)
    return centered / jnp.sqrt(spread + 1e-06)


def normalize(raised):
    return raised / jnp.sum(raised, axis=1, keepdims=True)


def store_pair(out, rows, x):
    clusters = x.shape[1]
    high, low = split(x)
    out[rows, :clusters] = high
    out[rows, clusters:] = low


def prepare_body(logits, unused, pair, wide):
    n = logits.shape[0]
    member = normalize(jnp.exp(logits[...]))
    store_pair(pair, slice(0, n), member)
    store_pair(wide, slice(0, n), member)
    wide[n:, :] = jnp.zeros((wide.shape[0] - n, wide.shape[1]), BF16)


def kernel_body(order, column_ref, rows_ref, plane_ref, *refs):
    high_ref, low_ref = refs[-2:]
    n, width = high_ref.shape[0], plane_ref.shape[1]
    column = column_ref[0]
    rows = rows_ref[:n, :width]
    for j, k in enumerate(order):
        start = pl.multiple_of(lax.bitwise_xor(column, k) * n, n)
        inner = lax.dot_general(
            rows,
            plane_ref[pl.ds(start, n), :],
            (((1,), (1,)), ((), ())),
            preferred_element_type=F32,
        )
        t = inner / width
        high, low = split(t * (3.0 + t * (3.0 + t)))
        high_ref[:, j * n : (j + 1) * n] = high
        low_ref[:, j * n : (j + 1) * n] = low


def kernel_call(n, order, column, rows, plane, after=()):
    total = plane.shape[0]
    return call(
        functools.partial(kernel_body, tuple(order)),
        [column, rows, plane, *after],
        [shaped(n, total, BF16)] * 2,
        [SMEM, VMEM, VMEM] + [ANY] * len(after),
        flops=int(KERNEL_FLOPS * n) * total * plane.shape[1],
    )


def scores_body(at, pieces, kernels, partials, unused, weights, has_near, *refs):
    members, refs = refs[:pieces], refs[pieces:]
    blocks, refs = refs[:kernels], refs[kernels:]
    before, refs = refs[:partials], refs[partials:]
    own, outs = refs[:weights], refs[weights + unused :]
    n = blocks[0].shape[0]
    clusters = members[0].shape[1] // 2
    for i, out in enumerate(outs[: kernels // 2]):
        both, rest, start = None, None, at
        for piece in members:
            columns = slice(start, start + piece.shape[0])
            start += piece.shape[0]
            a = jnp.dot(blocks[2 * i][:, columns], piece[...], preferred_element_type=F32)
            b = jnp.dot(
                blocks[2 * i + 1][:, columns],
                piece[:, :clusters],
                preferred_element_type=F32,
            )
            both = a if both is None else both + a
            rest = b if rest is None else rest + b
        s = both[:, :clusters] + (both[:, clusters:] + rest)
        if partials:
            s += before[i][:n, :]
        out[:n, :] = s
        if out.shape[0] > n:
            out[n:, :] = jnp.zeros((out.shape[0] - n, clusters), F32)
    if weights:
        count = len(outs) - 1
        stat = outs[count]
        stat_body(has_near, *own[:1], *outs[:count], *own[1:], stat)
        for out in outs[1:count]:
            out[n : n + STAT_ROWS, :] = stat[...]


def scores_call(
    at, members, kernels, partials, extra, hidden=False, after=(), weights=(), has_near=0
):
    n, clusters = kernels[0].shape[0], members[0].shape[1] // 2
    depth = sum(x.shape[0] for x in members)
    return call(
        functools.partial(
            scores_body,
            at,
            len(members),
            len(kernels),
            len(partials),
            len(after),
            len(weights),
            has_near,
        ),
        [*members, *kernels, *partials, *weights, *after],
        [shaped(n + e, clusters) for e in extra]
        + [shaped(STAT_ROWS, clusters)] * (len(weights) > 0),
        [VMEM] * (len(members) + len(kernels) + len(partials) + len(weights))
        + [ANY] * len(after),
        flops=3 * n * len(kernels) * depth * clusters,
        hidden=hidden,
    )


def members_body(n, smalls, evens, others, *refs):
    stats, refs = refs[:smalls], refs[smalls:]
    own, refs = refs[:evens], refs[evens:]
    rest, refs = refs[:others], refs[others:]
    even, pairs = refs[0], refs[1:]
    stat = stats[0][...]
    for ref in stats[1:]:
        stat += ref[...]
    for ref in rest:
        stat += ref[n:, :]
    weighted, size = stat[0:1, :], stat[1:2, :]

    def member_of(x):
        return normalize(jnp.exp(-2.0 * standardize(x, size, weighted)))

    for j, ref in enumerate(own):
        store_pair(even, slice(j * n, (j + 1) * n), member_of(ref[...]))
    for pair, ref in zip(pairs, rest):
        store_pair(pair, slice(0, n), member_of(ref[:n, :]))


def members_call(n, stats, evens, others):
    clusters = evens[0].shape[1]
    return call(
        functools.partial(members_body, n, len(stats), len(evens), len(others)),
        stats + evens + others,
        [shaped(n * len(evens), 2 * clusters, BF16)]
        + [shaped(n, 2 * clusters, BF16)] * len(others),
    )


def stat_body(has_near, own, *refs):
    out, refs = refs[-1], refs[:-1]
    count = len(refs) // 2
    scores, pairs = refs[: count + 1], refs[count + 1 :]
    n, clusters = scores[0].shape
    member = whole(own[:n, :])
    total = jnp.sum(member * scores[0][...], axis=0, keepdims=True)
    for i in range(count):
        pair = pairs[i]
        other = whole(pair[:n, pair.shape[1] - 2 * clusters :])
        part = jnp.sum(other * scores[i + 1][:n, :], axis=0, keepdims=True)
        total += part if i < has_near else 2.0 * part
    size = jnp.sum(member, axis=0, keepdims=True)
    row = lax.broadcasted_iota(jnp.int32, out.shape, 0)
    out[...] = jnp.where(row == 0, total, jnp.where(row == 1, size, 0.0))


def stat_call(has_near, own, scores, pairs):
    clusters = scores[0].shape[1]
    return call(
        functools.partial(stat_body, has_near),
        [own] + scores + pairs,
        [shaped(STAT_ROWS, clusters)],
    )[0]


def other_body(n, count, *refs):
    pairs, refs = refs[:count], refs[count:]
    kernels, refs = refs[: 2 * count], refs[2 * count :]
    stat, (even, odd) = refs[:-2], refs[-2:]
    half, clusters = even.shape
    over = (((0,), (0,)), ((), ()))
    for part, out in enumerate((odd, even)):
        columns = slice((1 - part) * half, (2 - part) * half)
        acc = jnp.zeros((half, clusters), F32)
        for i, pair in enumerate(pairs):
            both = pair[:n, pair.shape[1] - 2 * clusters :]
            a = lax.dot_general(
                kernels[2 * i][:, columns], both, over, preferred_element_type=F32
            )
            b = lax.dot_general(
                kernels[2 * i + 1][:, columns],
                both[:, :clusters],
                over,
                preferred_element_type=F32,
            )
            acc += a[:, :clusters] + (a[:, clusters:] + b)
        out[:half, :] = acc
    if stat:
        odd[half:, :] = stat[0][...]


def other_call(n, half, clusters, pairs, kernels, stat):
    return call(
        functools.partial(other_body, n, len(pairs)),
        pairs + kernels + stat,
        [shaped(half, clusters), shaped(half + STAT_ROWS * len(stat), clusters)],
        flops=12 * n * len(pairs) * half * clusters,
    )


def fold_body(n, count, even, received, *refs):
    stats, outs = refs[:count], refs[count:]
    half = even.shape[0]
    for j, out in enumerate(outs):
        rows = slice(j * n, (j + 1) * n)
        out[:n, :] = even[rows, :] + received[rows, :]
        if count:
            out[n:, :] = stats[0][...] + received[half:, :]


def fold_call(n, even, received, stats, extra):
    half, clusters = even.shape
    return call(
        functools.partial(fold_body, n, len(stats)),
        [even, received] + stats,
        [shaped(n + extra, clusters)] * (half // n),
    )


def add_body(*refs):
    refs, out = refs[:-1], refs[-1]
    n = out.shape[0]
    total = refs[0][:n, :]
    for ref in refs[1:]:
        total += ref[:n, :]
    out[...] = total


def plane_body(count, *refs):
    total = refs[0][...]
    for ref in refs[1:count]:
        total += ref[...]
    refs[-1][...] = total


def sum_body(n, last, *refs):
    many = 2 if last else 3
    refs, outs = refs[:-many], refs[-many:]
    if last:
        stat = refs[0][...] + refs[1][...]
        refs = refs[2:]
    else:
        stat = refs[0][n:, :]
    total = refs[0][:n, :]
    for ref in refs[1:]:
        total += ref[:n, :]
        if not last and ref.shape[0] == n + STAT_ROWS:
            stat += ref[n:, :]
    if last:
        members, standardized = outs
        x = standardize(total, stat[1:2, :], stat[0:1, :])
        standardized[...] = x
        members[...] = normalize(jnp.exp(-2.0 * x))
    else:
        full, scores, stats = outs
        full[:n, :] = total
        full[n:, :] = stat
        scores[...] = total
        stats[...] = stat


def on_device(rows, cols, features, logits):
    n, clusters = logits.shape
    width = features.shape[1]
    half = n * cols // 2
    masks = list(range(2, cols, 2))
    order = [0] + masks
    order = order + [k + 1 for k in order]
    has_near = int(rows % 2 == 0)
    half_rows = rows // 2
    if has_near:
        place = [2 * q if q < half_rows else 2 * (q - half_rows) + 1 for q in range(rows)]
        offsets = list(range(1, half_rows))
    else:
        place = list(range(rows))
        offsets = list(range(1, half_rows + 1))
    steps = ([0] if has_near else []) + offsets

    def by_col(x, mask):
        return lax.ppermute(x, "col", [(i, i ^ mask) for i in range(cols)])

    def shift(x, d):
        if d == 0:
            pairs = [(i, i ^ 1) for i in range(rows)]
        else:
            pairs = [(place[(q + d) % rows], place[q]) for q in range(rows)]
        return lax.ppermute(x, "row", pairs)

    column = jnp.reshape(lax.axis_index("col"), (1,)).astype(jnp.int32)
    own_rows = lax.dynamic_slice_in_dim(features, lax.axis_index("col") * n, n, 0)
    pair, wide = call(
        prepare_body,
        [logits, own_rows],
        [shaped(n, 2 * clusters, BF16), shaped(n + WIDE_ROWS, 2 * clusters, BF16)],
        [VMEM, ANY],
        hidden=True,
    )
    far_rows = [shift(own_rows, d) for d in steps]
    others = [shift(wide if d else pair, d) for d in steps]
    evens = [pair] + [by_col(pair, k) for k in masks]
    members = evens + [by_col(x, 1) for x in evens]
    early = 1 + has_near
    extra = [0] + [BACK_ROWS] * len(steps)
    blocks = [kernel_call(n, order, column, own_rows, features)]
    for x in reversed(far_rows):
        blocks.append(kernel_call(n, order, column, x, features, blocks[-1][:1]))
    blocks = blocks[:1] + blocks[:0:-1]
    kernels = [x for block in blocks for x in block]
    cross = kernels[2 * early :]
    scores = scores_call(0, members, kernels, [], extra, True)
    own = pair

    for iteration in range(ITERS):
        last = iteration == ITERS - 1
        if iteration > 0:
            even, *others = members_call(n, stats, evens, others)
            odd = by_col(even, 1)
            own = even
            scores = scores_call(0, [even], kernels, [], extra)
        if last:
            t_even, t_odd = other_call(n, half, clusters, others[has_near:], cross, [])
            sent = fold_call(n, t_even, by_col(t_odd, 1), [], 0)
            *scores, stat = scores_call(
                half, [odd], kernels, scores, extra, False, sent[:1], [own] + others, has_near
            )
        else:
            if iteration > 0:
                scores = scores_call(half, [odd], kernels, scores, extra)
            stat = stat_call(has_near, own, scores, others)
            t_even, t_odd = other_call(n, half, clusters, others[has_near:], cross, [stat])
            sent = fold_call(n, t_even, by_col(t_odd, 1), [stat], STAT_ROWS)
        parts = [by_col(x, k) for k, x in zip(masks, sent[1:])]
        back = [shift(x, -d) for d, x in zip(steps, scores[1:])]
        total = []
        if last:
            for x in [shift(stat, d) for d in offsets]:
                stat = stat + x
            for x in back:
                stat = stat + x[n : n + STAT_ROWS]
            plane = stat
            sent = call(add_body, [sent[0], scores[0]] + parts, [shaped(n, clusters)])
            stats = [plane] + [by_col(plane, k) for k in masks]
            stat = call(
                functools.partial(plane_body, len(stats)),
                stats + sent,
                [shaped(STAT_ROWS, clusters)],
                [VMEM] * len(stats) + [ANY],
            )[0]
            total = [stat, by_col(stat, 1)]
            parts = []
        outs = [shaped(n, clusters)] * 2
        if not last:
            outs = [shaped(n + STAT_ROWS, clusters), outs[0], shaped(STAT_ROWS, clusters)]
        done = call(
            functools.partial(sum_body, n, last),
            total + ([sent[0]] if last else [sent[0], scores[0]]) + back + parts,
            outs,
        )
        if not last:
            full, total, stats = done
            evens = [total] + [by_col(total, k) for k in masks]
            others = [shift(full, d) for d in steps]
            stats = [stats] + [shift(stats, -d) for d in offsets]
    return tuple(done)


def solution(mesh):
    return jax.shard_map(
        functools.partial(on_device, mesh.shape["row"], mesh.shape["col"]),
        mesh=mesh,
        in_specs=(P("row", None), P(("row", "col"), None)),
        out_specs=(P(("row", "col"), None), P(("row", "col"), None)),
        check_vma=False,
    )
```

```python
import functools

import jax
import jax.numpy as jnp
from jax import lax
from jax.experimental import pallas as pl
from jax.experimental.pallas import tpu as pltpu
from jax.sharding import PartitionSpec as P

ITERS = 2
STAT_ROWS = 8
GATHER_ROWS = (8, 16, 24)
WIDE_ROWS = 16
BACK_ROWS = 16
VMEM_BYTES = 24 * 1024 * 1024
CROSS_COST = 6
VMEM = pl.BlockSpec(memory_space=pltpu.VMEM)
SMEM = pl.BlockSpec(memory_space=pltpu.SMEM)
ANY = pl.BlockSpec(memory_space=pl.ANY)
BF16 = jnp.bfloat16
F32 = jnp.float32


def shaped(rows, columns, dtype=F32):
    return jax.ShapeDtypeStruct((rows, columns), dtype)


def call(body, args, outs, specs=None, scratch=(), flops=0, hidden=False):
    bytes_accessed = sum(x.size * x.dtype.itemsize for x in list(args) + list(outs))
    if hidden:
        flops = bytes_accessed = 0
    made = pl.pallas_call(
        body,
        in_specs=specs or [VMEM] * len(args),
        out_specs=[VMEM] * len(outs),
        out_shape=list(outs),
        scratch_shapes=list(scratch),
        compiler_params=pltpu.CompilerParams(vmem_limit_bytes=VMEM_BYTES),
        cost_estimate=pl.CostEstimate(
            flops=flops, bytes_accessed=bytes_accessed, transcendentals=0
        ),
    )(*args)
    return list(made)


def split(x):
    high = x.astype(BF16)
    low = (x - high.astype(F32)).astype(BF16)
    return high, low


def whole(pair):
    clusters = pair.shape[1] // 2
    return pair[:, :clusters].astype(F32) + pair[:, clusters:].astype(F32)


def standardize(scores, size, weighted):
    distance = weighted / (size * size) - 2.0 * scores / size
    centered = distance - jnp.mean(distance, axis=1, keepdims=True)
    spread = jnp.mean(centered * centered, axis=1, keepdims=True)
    return centered / jnp.sqrt(spread + 1e-06)


def normalize(raised):
    return raised / jnp.sum(raised, axis=1, keepdims=True)


def store_pair(out, rows, x):
    clusters = x.shape[1]
    high, low = split(x)
    out[rows, :clusters] = high
    out[rows, clusters:] = low


def prepare_body(logits, rows, pair, wide, message):
    n, width = rows.shape
    member = normalize(jnp.exp(logits[...]))
    store_pair(pair, slice(0, n), member)
    store_pair(wide, slice(0, n), member)
    wide[n:, :] = jnp.zeros((wide.shape[0] - n, wide.shape[1]), BF16)
    message[:, :width] = rows[...]
    message[:, width:] = pair[...]


def kernel_body(order, column_ref, rows_ref, plane_ref, *refs):
    high_ref, low_ref = refs[-2:]
    n, width = high_ref.shape[0], plane_ref.shape[1]
    column = column_ref[0]
    rows = rows_ref[:n, :width]
    for j, k in enumerate(order):
        start = pl.multiple_of(lax.bitwise_xor(column, k) * n, n)
        inner = lax.dot_general(
            rows,
            plane_ref[pl.ds(start, n), :],
            (((1,), (1,)), ((), ())),
            preferred_element_type=F32,
        )
        t = inner / width
        high, low = split(t * (3.0 + t * (3.0 + t)))
        high_ref[:, j * n : (j + 1) * n] = high
        low_ref[:, j * n : (j + 1) * n] = low


def kernel_call(n, order, column, rows, plane, after=(), cost=1):
    total = plane.shape[0]
    return call(
        functools.partial(kernel_body, tuple(order)),
        [column, rows, plane, *after],
        [shaped(n, total, BF16)] * 2,
        [SMEM, VMEM, VMEM] + [ANY] * len(after),
        flops=int(2 * cost * n) * total * plane.shape[1],
    )


def scores_body(at, pieces, kernels, partials, unused, weights, has_near, *refs):
    members, refs = refs[:pieces], refs[pieces:]
    blocks, refs = refs[:kernels], refs[kernels:]
    before, refs = refs[:partials], refs[partials:]
    own, outs = refs[:weights], refs[weights + unused :]
    n = blocks[0].shape[0]
    clusters = members[0].shape[1] // 2
    for i, out in enumerate(outs[: kernels // 2]):
        both, rest, start = None, None, at
        for piece in members:
            columns = slice(start, start + piece.shape[0])
            start += piece.shape[0]
            a = jnp.dot(blocks[2 * i][:, columns], piece[...], preferred_element_type=F32)
            b = jnp.dot(
                blocks[2 * i + 1][:, columns],
                piece[:, :clusters],
                preferred_element_type=F32,
            )
            both = a if both is None else both + a
            rest = b if rest is None else rest + b
        s = both[:, :clusters] + (both[:, clusters:] + rest)
        if partials:
            s += before[i][:n, :]
        out[:n, :] = s
        if out.shape[0] > n:
            out[n:, :] = jnp.zeros((out.shape[0] - n, clusters), F32)
    if weights:
        count = len(outs) - 1
        stat = outs[count]
        stat_body(has_near, *own[:1], *outs[:count], *own[1:], stat)
        for out in outs[1:count]:
            out[n : n + STAT_ROWS, :] = stat[...]


def scores_call(
    at, members, kernels, partials, extra, hidden=False, after=(), weights=(), has_near=0
):
    n, clusters = kernels[0].shape[0], members[0].shape[1] // 2
    depth = sum(x.shape[0] for x in members)
    return call(
        functools.partial(
            scores_body,
            at,
            len(members),
            len(kernels),
            len(partials),
            len(after),
            len(weights),
            has_near,
        ),
        [*members, *kernels, *partials, *weights, *after],
        [shaped(n + e, clusters) for e in extra]
        + [shaped(STAT_ROWS, clusters)] * (len(weights) > 0),
        [VMEM] * (len(members) + len(kernels) + len(partials) + len(weights))
        + [ANY] * len(after),
        flops=3 * n * len(kernels) * depth * clusters,
        hidden=hidden,
    )


def members_body(n, smalls, evens, others, *refs):
    stats, refs = refs[:smalls], refs[smalls:]
    own, refs = refs[:evens], refs[evens:]
    rest, refs = refs[:others], refs[others:]
    even, pairs = refs[0], refs[1:]
    stat = stats[0][...]
    for ref in stats[1:]:
        stat += ref[...]
    for ref in rest:
        stat += ref[n : n + STAT_ROWS, :]
    weighted, size = stat[0:1, :], stat[1:2, :]

    def member_of(x):
        return normalize(jnp.exp(-2.0 * standardize(x, size, weighted)))

    for j, ref in enumerate(own):
        store_pair(even, slice(j * n, (j + 1) * n), member_of(ref[:n, :]))
    for pair, ref in zip(pairs, rest):
        store_pair(pair, slice(0, n), member_of(ref[:n, :]))


def members_call(n, stats, evens, others):
    clusters = evens[0].shape[1]
    return call(
        functools.partial(members_body, n, len(stats), len(evens), len(others)),
        stats + evens + others,
        [shaped(n * len(evens), 2 * clusters, BF16)]
        + [shaped(n, 2 * clusters, BF16)] * len(others),
    )


def stat_body(has_near, own, *refs):
    out, refs = refs[-1], refs[:-1]
    count = len(refs) // 2
    scores, pairs = refs[: count + 1], refs[count + 1 :]
    n, clusters = scores[0].shape
    member = whole(own[:n, :])
    total = jnp.sum(member * scores[0][...], axis=0, keepdims=True)
    for i in range(count):
        pair = pairs[i]
        other = whole(pair[:n, pair.shape[1] - 2 * clusters :])
        part = jnp.sum(other * scores[i + 1][:n, :], axis=0, keepdims=True)
        total += part if i < has_near else 2.0 * part
    size = jnp.sum(member, axis=0, keepdims=True)
    row = lax.broadcasted_iota(jnp.int32, out.shape, 0)
    out[...] = jnp.where(row == 0, total, jnp.where(row == 1, size, 0.0))


def stat_call(has_near, own, scores, pairs):
    clusters = scores[0].shape[1]
    return call(
        functools.partial(stat_body, has_near),
        [own] + scores + pairs,
        [shaped(STAT_ROWS, clusters)],
    )[0]


def other_body(n, count, *refs):
    pairs, refs = refs[:count], refs[count:]
    kernels, refs = refs[: 2 * count], refs[2 * count :]
    stat, (even, odd) = refs[:-2], refs[-2:]
    half, clusters = even.shape
    over = (((0,), (0,)), ((), ()))
    for part, out in enumerate((odd, even)):
        columns = slice((1 - part) * half, (2 - part) * half)
        acc = jnp.zeros((half, clusters), F32)
        for i, pair in enumerate(pairs):
            both = pair[:n, pair.shape[1] - 2 * clusters :]
            a = lax.dot_general(
                kernels[2 * i][:, columns], both, over, preferred_element_type=F32
            )
            b = lax.dot_general(
                kernels[2 * i + 1][:, columns],
                both[:, :clusters],
                over,
                preferred_element_type=F32,
            )
            acc += a[:, :clusters] + (a[:, clusters:] + b)
        out[:half, :] = acc
    if stat:
        odd[half:, :] = stat[0][...]


def other_call(n, half, clusters, pairs, kernels, stat):
    return call(
        functools.partial(other_body, n, len(pairs)),
        pairs + kernels + stat,
        [shaped(half, clusters), shaped(half + STAT_ROWS * len(stat), clusters)],
        flops=12 * n * len(pairs) * half * clusters,
    )


def fold_body(n, count, unused, even, received, *refs):
    stats, outs = refs[:count], refs[count + unused :]
    half = even.shape[0]
    for j, out in enumerate(outs):
        rows = slice(j * n, (j + 1) * n)
        out[:n, :] = even[rows, :] + received[rows, :]
        if count:
            out[n:, :] = stats[0][...] + received[half:, :]
        else:
            out[n:, :] = jnp.zeros((out.shape[0] - n, out.shape[1]), F32)


def fold_call(n, even, received, stats, extra, after=()):
    half, clusters = even.shape
    return call(
        functools.partial(fold_body, n, len(stats), len(after)),
        [even, received, *stats, *after],
        [shaped(n + extra, clusters)] * (half // n),
        [VMEM] * (2 + len(stats)) + [ANY] * len(after),
    )


def add_body(*refs):
    refs, out = refs[:-1], refs[-1]
    n = out.shape[0]
    total = refs[0][:n, :]
    for ref in refs[1:]:
        total += ref[:n, :]
    out[...] = total


def column_body(n, *refs):
    total = refs[0][...]
    for ref in refs[1:-1]:
        total += ref[...] if ref.shape[0] < n else ref[n : n + STAT_ROWS, :]
    refs[-1][...] = total


def plane_body(count, *refs):
    total = refs[0][...]
    for ref in refs[1:count]:
        total += ref[...]
    refs[-1][...] = total


def sum_body(n, last, *refs):
    many = 2 if last else 1 + len(GATHER_ROWS)
    refs, outs = refs[:-many], refs[-many:]
    if last:
        stat = refs[0][...] + refs[1][...]
        refs = refs[2:]
    else:
        stat = refs[0][n:, :]
    total = refs[0][:n, :]
    for ref in refs[1:]:
        total += ref[:n, :]
        if not last and ref.shape[0] == n + STAT_ROWS:
            stat += ref[n:, :]
    if last:
        members, standardized = outs
        x = standardize(total, stat[1:2, :], stat[0:1, :])
        standardized[...] = x
        members[...] = normalize(jnp.exp(-2.0 * x))
    else:
        stats, fulls = outs[0], outs[1:]
        stats[...] = stat
        for full in fulls:
            full[:n, :] = total
            full[n : n + STAT_ROWS, :] = stat
            rest = full.shape[0] - n - STAT_ROWS
            if rest:
                full[n + STAT_ROWS :, :] = jnp.zeros((rest, full.shape[1]), F32)


def on_device(rows, cols, features, logits):
    n, clusters = logits.shape
    width = features.shape[1]
    half = n * cols // 2
    masks = list(range(2, cols, 2))
    order = [0] + masks
    order = order + [k + 1 for k in order]
    has_near = int(rows % 2 == 0)
    half_rows = rows // 2
    if has_near:
        place = [2 * q if q < half_rows else 2 * (q - half_rows) + 1 for q in range(rows)]
        offsets = list(range(1, half_rows))
    else:
        place = list(range(rows))
        offsets = list(range(1, half_rows + 1))
    steps = ([0] if has_near else []) + offsets

    def by_col(x, mask):
        return lax.ppermute(x, "col", [(i, i ^ mask) for i in range(cols)])

    def shift(x, d):
        if d == 0:
            pairs = [(i, i ^ 1) for i in range(rows)]
        else:
            pairs = [(place[(q + d) % rows], place[q]) for q in range(rows)]
        return lax.ppermute(x, "row", pairs)

    column = jnp.reshape(lax.axis_index("col"), (1,)).astype(jnp.int32)
    own_rows = lax.dynamic_slice_in_dim(features, lax.axis_index("col") * n, n, 0)
    pair, wide, message = call(
        prepare_body,
        [logits, own_rows],
        [
            shaped(n, 2 * clusters, BF16),
            shaped(n + WIDE_ROWS, 2 * clusters, BF16),
            shaped(n, width + 2 * clusters, BF16),
        ],
        hidden=True,
    )
    far_rows = [shift(own_rows if d else message, d) for d in steps]
    others = [shift(wide, d) if d else far_rows[0] for d in steps]
    evens = [pair] + [by_col(pair, k) for k in masks]
    members = evens + [by_col(x, 1) for x in evens]
    early = 1 + has_near
    extra = [0] + [BACK_ROWS] * len(steps)
    kernels = kernel_call(n, order, column, own_rows, features)
    cross = []
    for x in far_rows[has_near:]:
        after = (cross or kernels)[-2:]
        cross += kernel_call(n, order, column, x, features, after, CROSS_COST)
    scores = scores_call(
        0, members, kernels + cross, [], extra[:1] + extra[early:], hidden=True
    )
    if has_near:
        near = kernel_call(n, order, column, far_rows[0], features, scores[-1:])
        kernels += near
        scores[1:1] = scores_call(0, members, near, [], extra[1:2], hidden=True)
    kernels += cross
    own = pair

    for iteration in range(ITERS):
        last = iteration == ITERS - 1
        if iteration > 0:
            even, *others = members_call(n, stats, evens, others)
            odd = by_col(even, 1)
            own = even
            scores = scores_call(0, [even], kernels, [], extra)
        if last:
            t_even, t_odd = other_call(n, half, clusters, others[has_near:], cross, [])
            extra = [0] + [STAT_ROWS] * len(steps)
            *scores, stat = scores_call(
                half, [odd], kernels, scores, extra, False, (), [own] + others, has_near
            )
            small = [shift(stat, d) for d in offsets]
            sent = fold_call(n, t_even, by_col(t_odd, 1), [], STAT_ROWS, small)
        else:
            if iteration > 0:
                scores = scores_call(half, [odd], kernels, scores, extra)
            stat = stat_call(has_near, own, scores, others)
            t_even, t_odd = other_call(n, half, clusters, others[has_near:], cross, [stat])
            sent = fold_call(n, t_even, by_col(t_odd, 1), [stat], STAT_ROWS)
        parts = [by_col(x, k) for k, x in zip(masks, sent[1:])]
        back = [shift(x, -d) for d, x in zip(steps, scores[1:])]
        total = []
        if last:
            plane = call(
                functools.partial(column_body, n),
                [stat] + back + small,
                [shaped(STAT_ROWS, clusters)],
            )[0]
            sent = call(add_body, [sent[0], scores[0]] + parts, [shaped(n, clusters)])
            stats = [plane] + [by_col(plane, k) for k in masks]
            stat = call(
                functools.partial(plane_body, len(stats)),
                stats + sent,
                [shaped(STAT_ROWS, clusters)],
                [VMEM] * len(stats) + [ANY],
            )[0]
            total = [stat, by_col(stat, 1)]
            parts = []
        outs = [shaped(n, clusters)] * 2
        if not last:
            outs = [shaped(STAT_ROWS, clusters)]
            outs += [shaped(n + r, clusters) for r in GATHER_ROWS]
        done = call(
            functools.partial(sum_body, n, last),
            total + ([sent[0]] if last else [sent[0], scores[0]]) + back + parts,
            outs,
        )
        if not last:
            stats, near_full, part_full, cross_full = done
            evens = [part_full] + [by_col(part_full, k) for k in masks]
            others = [shift(cross_full if d else near_full, d) for d in steps]
            stats = [stats] + [shift(stats, -d) for d in offsets]
    return tuple(done)


def solution(mesh):
    return jax.shard_map(
        functools.partial(on_device, mesh.shape["row"], mesh.shape["col"]),
        mesh=mesh,
        in_specs=(P("row", None), P(("row", "col"), None)),
        out_specs=(P(("row", "col"), None), P(("row", "col"), None)),
        check_vma=False,
    )
```

```python
import functools

import jax
import jax.numpy as jnp
from jax import lax
from jax.experimental import pallas as pl
from jax.experimental.pallas import tpu as pltpu
from jax.sharding import PartitionSpec as P

ITERS = 2
STAT_ROWS = 8
GATHER_ROWS = (STAT_ROWS, 0)
WIDE_ROWS = 16
LAST_ROWS = 32
BACK_ROWS = 16
VMEM_BYTES = 24 * 1024 * 1024
CROSS_COST = 2.7
VMEM = pl.BlockSpec(memory_space=pltpu.VMEM)
SMEM = pl.BlockSpec(memory_space=pltpu.SMEM)
ANY = pl.BlockSpec(memory_space=pl.ANY)
BF16 = jnp.bfloat16
F32 = jnp.float32


def shaped(rows, columns, dtype=F32):
    return jax.ShapeDtypeStruct((rows, columns), dtype)


def call(body, args, outs, specs=None, scratch=(), flops=0, hidden=False):
    bytes_accessed = sum(x.size * x.dtype.itemsize for x in list(args) + list(outs))
    if hidden:
        flops = bytes_accessed = 0
    made = pl.pallas_call(
        body,
        in_specs=specs or [VMEM] * len(args),
        out_specs=[VMEM] * len(outs),
        out_shape=list(outs),
        scratch_shapes=list(scratch),
        compiler_params=pltpu.CompilerParams(vmem_limit_bytes=VMEM_BYTES),
        cost_estimate=pl.CostEstimate(
            flops=flops, bytes_accessed=bytes_accessed, transcendentals=0
        ),
    )(*args)
    return list(made)


def split(x):
    high = x.astype(BF16)
    low = (x - high.astype(F32)).astype(BF16)
    return high, low


def whole(pair):
    clusters = pair.shape[1] // 2
    return pair[:, :clusters].astype(F32) + pair[:, clusters:].astype(F32)


def standardize(scores, size, weighted):
    distance = weighted / (size * size) - 2.0 * scores / size
    centered = distance - jnp.mean(distance, axis=1, keepdims=True)
    spread = jnp.mean(centered * centered, axis=1, keepdims=True)
    return centered / jnp.sqrt(spread + 1e-06)


def normalize(raised):
    return raised / jnp.sum(raised, axis=1, keepdims=True)


def store_pair(out, rows, x):
    clusters = x.shape[1]
    high, low = split(x)
    out[rows, :clusters] = high
    out[rows, clusters:] = low


def prepare_body(logits, rows, pair, wide, message):
    n, width = rows.shape
    member = normalize(jnp.exp(logits[...]))
    store_pair(pair, slice(0, n), member)
    store_pair(wide, slice(0, n), member)
    wide[n:, :] = jnp.zeros((wide.shape[0] - n, wide.shape[1]), BF16)
    message[:, :width] = rows[...]
    message[:, width:] = pair[...]


def kernel_body(order, column_ref, rows_ref, plane_ref, *refs):
    high_ref, low_ref = refs[-2:]
    n, width = high_ref.shape[0], plane_ref.shape[1]
    column = column_ref[0]
    rows = rows_ref[:n, :width]
    for j, k in enumerate(order):
        start = pl.multiple_of(lax.bitwise_xor(column, k) * n, n)
        inner = lax.dot_general(
            rows,
            plane_ref[pl.ds(start, n), :],
            (((1,), (1,)), ((), ())),
            preferred_element_type=F32,
        )
        t = inner / width
        high, low = split(t * (3.0 + t * (3.0 + t)))
        high_ref[:, j * n : (j + 1) * n] = high
        low_ref[:, j * n : (j + 1) * n] = low


def kernel_call(n, order, column, rows, plane, after=(), cost=1):
    total = plane.shape[0]
    return call(
        functools.partial(kernel_body, tuple(order)),
        [column, rows, plane, *after],
        [shaped(n, total, BF16)] * 2,
        [SMEM, VMEM, VMEM] + [ANY] * len(after),
        flops=int(2 * cost * n) * total * plane.shape[1],
    )


def scores_body(at, pieces, kernels, partials, unused, weights, has_near, *refs):
    members, refs = refs[:pieces], refs[pieces:]
    blocks, refs = refs[:kernels], refs[kernels:]
    before, refs = refs[:partials], refs[partials:]
    own, outs = refs[:weights], refs[weights + unused :]
    n = blocks[0].shape[0]
    clusters = members[0].shape[1] // 2
    for i, out in enumerate(outs[: kernels // 2]):
        both, rest, start = None, None, at
        for piece in members:
            columns = slice(start, start + piece.shape[0])
            start += piece.shape[0]
            a = jnp.dot(blocks[2 * i][:, columns], piece[...], preferred_element_type=F32)
            b = jnp.dot(
                blocks[2 * i + 1][:, columns],
                piece[:, :clusters],
                preferred_element_type=F32,
            )
            both = a if both is None else both + a
            rest = b if rest is None else rest + b
        s = both[:, :clusters] + (both[:, clusters:] + rest)
        if partials:
            s += before[i][:n, :]
        out[:n, :] = s
        if out.shape[0] > n:
            out[n:, :] = jnp.zeros((out.shape[0] - n, clusters), F32)
    if weights:
        count = len(outs) - 1
        stat = outs[count]
        stat_body(has_near, *own[:1], *outs[:count], *own[1:], stat)


def scores_call(
    at, members, kernels, partials, extra, hidden=False, after=(), weights=(), has_near=0
):
    n, clusters = kernels[0].shape[0], members[0].shape[1] // 2
    depth = sum(x.shape[0] for x in members)
    return call(
        functools.partial(
            scores_body,
            at,
            len(members),
            len(kernels),
            len(partials),
            len(after),
            len(weights),
            has_near,
        ),
        [*members, *kernels, *partials, *weights, *after],
        [shaped(n + e, clusters) for e in extra]
        + [shaped(STAT_ROWS, clusters)] * (len(weights) > 0),
        [VMEM] * (len(members) + len(kernels) + len(partials) + len(weights))
        + [ANY] * len(after),
        flops=3 * n * len(kernels) * depth * clusters,
        hidden=hidden,
    )


def members_body(n, smalls, evens, others, *refs):
    stats, refs = refs[:smalls], refs[smalls:]
    own, refs = refs[:evens], refs[evens:]
    rest, refs = refs[:others], refs[others:]
    even, pairs = refs[0], refs[1:]
    stat = stats[0][...]
    for ref in stats[1:]:
        stat += ref[...]
    for ref in rest:
        stat += ref[n : n + STAT_ROWS, :]
    weighted, size = stat[0:1, :], stat[1:2, :]

    def member_of(x):
        return normalize(jnp.exp(-2.0 * standardize(x, size, weighted)))

    for j, ref in enumerate(own):
        store_pair(even, slice(j * n, (j + 1) * n), member_of(ref[:n, :]))
    for pair, ref in zip(pairs, rest):
        store_pair(pair, slice(0, n), member_of(ref[:n, :]))


def members_call(n, stats, evens, others):
    clusters = evens[0].shape[1]
    return call(
        functools.partial(members_body, n, len(stats), len(evens), len(others)),
        stats + evens + others,
        [shaped(n * len(evens), 2 * clusters, BF16)]
        + [shaped(n, 2 * clusters, BF16)] * len(others),
    )


def stat_body(has_near, own, *refs):
    out, refs = refs[-1], refs[:-1]
    count = len(refs) // 2
    scores, pairs = refs[: count + 1], refs[count + 1 :]
    n, clusters = scores[0].shape
    member = whole(own[:n, :])
    total = jnp.sum(member * scores[0][...], axis=0, keepdims=True)
    for i in range(count):
        pair = pairs[i]
        other = whole(pair[:n, pair.shape[1] - 2 * clusters :])
        part = jnp.sum(other * scores[i + 1][:n, :], axis=0, keepdims=True)
        total += part if i < has_near else 2.0 * part
    size = jnp.sum(member, axis=0, keepdims=True)
    row = lax.broadcasted_iota(jnp.int32, out.shape, 0)
    out[...] = jnp.where(row == 0, total, jnp.where(row == 1, size, 0.0))


def stat_call(has_near, own, scores, pairs):
    clusters = scores[0].shape[1]
    return call(
        functools.partial(stat_body, has_near),
        [own] + scores + pairs,
        [shaped(STAT_ROWS, clusters)],
    )[0]


def other_body(n, count, *refs):
    pairs, refs = refs[:count], refs[count:]
    kernels, refs = refs[: 2 * count], refs[2 * count :]
    stat, (even, odd) = refs[:-2], refs[-2:]
    half, clusters = even.shape
    over = (((0,), (0,)), ((), ()))
    for part, out in enumerate((odd, even)):
        columns = slice((1 - part) * half, (2 - part) * half)
        acc = jnp.zeros((half, clusters), F32)
        for i, pair in enumerate(pairs):
            both = pair[:n, pair.shape[1] - 2 * clusters :]
            a = lax.dot_general(
                kernels[2 * i][:, columns], both, over, preferred_element_type=F32
            )
            b = lax.dot_general(
                kernels[2 * i + 1][:, columns],
                both[:, :clusters],
                over,
                preferred_element_type=F32,
            )
            acc += a[:, :clusters] + (a[:, clusters:] + b)
        out[:half, :] = acc
    if stat:
        odd[half:, :] = stat[0][...]


def other_call(n, half, clusters, pairs, kernels, stat):
    return call(
        functools.partial(other_body, n, len(pairs)),
        pairs + kernels + stat,
        [shaped(half, clusters), shaped(half + STAT_ROWS * len(stat), clusters)],
        flops=12 * n * len(pairs) * half * clusters,
    )


def fold_body(n, count, even, received, *refs):
    stats, outs = refs[:count], refs[count:]
    half = even.shape[0]
    stat = stats[0][...]
    for ref in stats[1:]:
        stat += ref[...]
    if received.shape[0] > half:
        stat += received[half:, :]
    for j, out in enumerate(outs):
        rows = slice(j * n, (j + 1) * n)
        out[:n, :] = even[rows, :] + received[rows, :]
        out[n:, :] = stat


def fold_call(n, even, received, stats, extra):
    half, clusters = even.shape
    return call(
        functools.partial(fold_body, n, len(stats)),
        [even, received] + stats,
        [shaped(n + extra, clusters)] * (half // n),
    )


def sum_body(n, last, *refs):
    many = 2 if last else 1 + len(GATHER_ROWS)
    refs, outs = refs[:-many], refs[-many:]
    total, stat = refs[0][:n, :], refs[0][n:, :]
    for ref in refs[1:]:
        total += ref[:n, :]
        if ref.shape[0] == n + STAT_ROWS:
            stat += ref[n:, :]
    if last:
        members, standardized = outs
        x = standardize(total, stat[1:2, :], stat[0:1, :])
        standardized[...] = x
        members[...] = normalize(jnp.exp(-2.0 * x))
    else:
        stats, fulls = outs[0], outs[1:]
        stats[...] = stat
        for full in fulls:
            full[:n, :] = total
            if full.shape[0] > n:
                full[n:, :] = stat


def on_device(rows, cols, features, logits):
    n, clusters = logits.shape
    width = features.shape[1]
    half = n * cols // 2
    masks = list(range(2, cols, 2))
    order = [0] + masks
    order = order + [k + 1 for k in order]
    has_near = int(rows % 2 == 0)
    half_rows = rows // 2
    if has_near:
        place = [2 * q if q < half_rows else 2 * (q - half_rows) + 1 for q in range(rows)]
        offsets = list(range(1, half_rows))
    else:
        place = list(range(rows))
        offsets = list(range(1, half_rows + 1))
    steps = ([0] if has_near else []) + offsets

    def by_col(x, mask):
        return lax.ppermute(x, "col", [(i, i ^ mask) for i in range(cols)])

    def shift(x, d):
        if d == 0:
            pairs = [(i, i ^ 1) for i in range(rows)]
        else:
            pairs = [(place[(q + d) % rows], place[q]) for q in range(rows)]
        return lax.ppermute(x, "row", pairs)

    column = jnp.reshape(lax.axis_index("col"), (1,)).astype(jnp.int32)
    own_rows = lax.dynamic_slice_in_dim(features, lax.axis_index("col") * n, n, 0)
    pair, wide, message = call(
        prepare_body,
        [logits, own_rows],
        [
            shaped(n, 2 * clusters, BF16),
            shaped(n + WIDE_ROWS, 2 * clusters, BF16),
            shaped(n, width + 2 * clusters, BF16),
        ],
        hidden=True,
    )
    far_rows = [shift(own_rows if d else message, d) for d in steps]
    others = [shift(wide, d) if d else far_rows[0] for d in steps]
    evens = [pair] + [by_col(pair, k) for k in masks]
    members = evens + [by_col(x, 1) for x in evens]
    early = 1 + has_near
    extra = [0] + [BACK_ROWS] * len(steps)
    blocks = [kernel_call(n, order, column, own_rows, features)]
    for x in reversed(far_rows):
        blocks.append(
            kernel_call(n, order, column, x, features, blocks[-1][:1], CROSS_COST)
        )
    blocks = blocks[:1] + blocks[:0:-1]
    kernels = [x for block in blocks for x in block]
    cross = kernels[2 * early :]
    scores = scores_call(0, members, kernels, [], extra, hidden=True)
    own = pair

    for iteration in range(ITERS):
        last = iteration == ITERS - 1
        if iteration > 0:
            even, *others = members_call(n, stats, evens, others)
            odd = by_col(even, 1)
            own = even
            scores = scores_call(0, [even], kernels, [], extra)
        if last:
            t_even, t_odd = other_call(n, half, clusters, others[has_near:], cross, [])
            extra = [0] + [LAST_ROWS] * len(steps)
            *scores, stat = scores_call(
                half, [odd], kernels, scores, extra, False, (), [own] + others, has_near
            )
            for x in [shift(stat, d) for d in range(1, rows)]:
                stat = stat + x
            sent = fold_call(
                n, t_even, by_col(t_odd, 1), [stat, by_col(stat, 1)], STAT_ROWS
            )
        else:
            if iteration > 0:
                scores = scores_call(half, [odd], kernels, scores, extra)
            stat = stat_call(has_near, own, scores, others)
            t_even, t_odd = other_call(n, half, clusters, others[has_near:], cross, [stat])
            sent = fold_call(n, t_even, by_col(t_odd, 1), [stat], STAT_ROWS)
        parts = [by_col(x, k) for k, x in zip(masks, sent[1:])]
        back = [shift(x, -d) for d, x in zip(steps, scores[1:])]
        outs = [shaped(n, clusters)] * 2
        if not last:
            outs = [shaped(STAT_ROWS, clusters)]
            outs += [shaped(n + r, clusters) for r in GATHER_ROWS]
        done = call(
            functools.partial(sum_body, n, last),
            [sent[0], scores[0]] + back + parts,
            outs,
        )
        if not last:
            stats, full, total = done
            evens = [total] + [by_col(total, k) for k in masks]
            others = [shift(full, d) for d in steps]
            stats = [stats] + [shift(stats, -d) for d in offsets]
    return tuple(done)


def solution(mesh):
    return jax.shard_map(
        functools.partial(on_device, mesh.shape["row"], mesh.shape["col"]),
        mesh=mesh,
        in_specs=(P("row", None), P(("row", "col"), None)),
        out_specs=(P(("row", "col"), None), P(("row", "col"), None)),
        check_vma=False,
    )
```

```python
import functools

import jax
import jax.numpy as jnp
from jax import lax
from jax.experimental import pallas as pl
from jax.experimental.pallas import tpu as pltpu
from jax.sharding import PartitionSpec as P

STAT_ROWS = 8
FAR_ROWS = 16
WIDE_ROWS = 16
LAST_ROWS = 32
BACK_ROWS = 16
VMEM_BYTES = 24 * 1024 * 1024
NEAR_COST = 10
CROSS_COST = 4
VMEM = pl.BlockSpec(memory_space=pltpu.VMEM)
SMEM = pl.BlockSpec(memory_space=pltpu.SMEM)
ANY = pl.BlockSpec(memory_space=pl.ANY)
BF16 = jnp.bfloat16
F32 = jnp.float32


def shaped(rows, columns, dtype=F32):
    return jax.ShapeDtypeStruct((rows, columns), dtype)


def call(body, args, outs, specs=None, scratch=(), flops=0, hidden=False):
    bytes_accessed = sum(x.size * x.dtype.itemsize for x in list(args) + list(outs))
    if hidden:
        flops = bytes_accessed = 0
    made = pl.pallas_call(
        body,
        in_specs=specs or [VMEM] * len(args),
        out_specs=[VMEM] * len(outs),
        out_shape=list(outs),
        scratch_shapes=list(scratch),
        compiler_params=pltpu.CompilerParams(vmem_limit_bytes=VMEM_BYTES),
        cost_estimate=pl.CostEstimate(
            flops=flops, bytes_accessed=bytes_accessed, transcendentals=0
        ),
    )(*args)
    return list(made)


def split(x):
    high = x.astype(BF16)
    low = (x - high.astype(F32)).astype(BF16)
    return high, low


def whole(pair):
    clusters = pair.shape[1] // 2
    return pair[:, :clusters].astype(F32) + pair[:, clusters:].astype(F32)


def standardize(scores, size, weighted):
    distance = weighted / (size * size) - 2.0 * scores / size
    centered = distance - jnp.mean(distance, axis=1, keepdims=True)
    spread = jnp.mean(centered * centered, axis=1, keepdims=True)
    return centered / jnp.sqrt(spread + 1e-06)


def normalize(raised):
    return raised / jnp.sum(raised, axis=1, keepdims=True)


def store_pair(out, rows, x):
    clusters = x.shape[1]
    high, low = split(x)
    out[rows, :clusters] = high
    out[rows, clusters:] = low


def prepare_body(logits, rows, pair, wide, message):
    n, width = rows.shape
    member = normalize(jnp.exp(logits[...]))
    store_pair(pair, slice(0, n), member)
    store_pair(wide, slice(0, n), member)
    wide[n:, :] = jnp.zeros((wide.shape[0] - n, wide.shape[1]), BF16)
    message[:, :width] = rows[...]
    message[:, width:] = pair[...]


def kernel_body(order, column_ref, rows_ref, plane_ref, *refs):
    high_ref, low_ref = refs[-2:]
    n, width = high_ref.shape[0], plane_ref.shape[1]
    column = column_ref[0]
    rows = rows_ref[:n, :width]
    for j, k in enumerate(order):
        start = pl.multiple_of(lax.bitwise_xor(column, k) * n, n)
        inner = lax.dot_general(
            rows,
            plane_ref[pl.ds(start, n), :],
            (((1,), (1,)), ((), ())),
            preferred_element_type=F32,
        )
        t = inner / width
        high, low = split(t * (3.0 + t * (3.0 + t)))
        high_ref[:, j * n : (j + 1) * n] = high
        low_ref[:, j * n : (j + 1) * n] = low


def kernel_call(n, order, column, rows, plane, after=(), cost=1):
    total = plane.shape[0]
    return call(
        functools.partial(kernel_body, tuple(order)),
        [column, rows, plane, *after],
        [shaped(n, total, BF16)] * 2,
        [SMEM, VMEM, VMEM] + [ANY] * len(after),
        flops=int(2 * cost * n) * total * plane.shape[1],
    )


def scores_body(at, pieces, kernels, partials, unused, weights, has_near, *refs):
    members, refs = refs[:pieces], refs[pieces:]
    blocks, refs = refs[:kernels], refs[kernels:]
    before, refs = refs[:partials], refs[partials:]
    own, outs = refs[:weights], refs[weights + unused :]
    n = blocks[0].shape[0]
    clusters = members[0].shape[1] // 2
    for i, out in enumerate(outs[: kernels // 2]):
        both, rest, start = None, None, at
        for piece in members:
            columns = slice(start, start + piece.shape[0])
            start += piece.shape[0]
            a = jnp.dot(blocks[2 * i][:, columns], piece[...], preferred_element_type=F32)
            b = jnp.dot(
                blocks[2 * i + 1][:, columns],
                piece[:, :clusters],
                preferred_element_type=F32,
            )
            both = a if both is None else both + a
            rest = b if rest is None else rest + b
        s = both[:, :clusters] + (both[:, clusters:] + rest)
        if partials:
            s += before[i][:n, :]
        out[:n, :] = s
        if out.shape[0] > n:
            out[n:, :] = jnp.zeros((out.shape[0] - n, clusters), F32)
    if weights:
        count = len(outs) - 1
        stat = outs[count]
        stat_body(has_near, count - 1, *own[:1], *outs[:count], *own[1:], stat)


def scores_call(
    at, members, kernels, partials, extra, hidden=False, after=(), weights=(), has_near=0
):
    n, clusters = kernels[0].shape[0], members[0].shape[1] // 2
    depth = sum(x.shape[0] for x in members)
    return call(
        functools.partial(
            scores_body,
            at,
            len(members),
            len(kernels),
            len(partials),
            len(after),
            len(weights),
            has_near,
        ),
        [*members, *kernels, *partials, *weights, *after],
        [shaped(n + e, clusters) for e in extra]
        + [shaped(STAT_ROWS, clusters)] * (len(weights) > 0),
        [VMEM] * (len(members) + len(kernels) + len(partials) + len(weights))
        + [ANY] * len(after),
        flops=3 * n * len(kernels) * depth * clusters,
        hidden=hidden,
    )


def members_body(n, evens, *refs):
    own, refs = refs[:evens], refs[evens:]
    others = (len(refs) - 1) // 2
    rest, even, pairs = refs[:others], refs[others], refs[others + 1 :]
    stat = own[0][n:, :]
    for ref in own[1:]:
        stat += ref[n:, :]
    weighted, size = stat[0:1, :], stat[1:2, :]

    def member_of(x):
        return normalize(jnp.exp(-2.0 * standardize(x, size, weighted)))

    for j, ref in enumerate(own):
        store_pair(even, slice(j * n, (j + 1) * n), member_of(ref[:n, :]))
    for pair, ref in zip(pairs, rest):
        store_pair(pair, slice(0, n), member_of(ref[:n, :]))


def members_call(n, evens, others):
    clusters = evens[0].shape[1]
    return call(
        functools.partial(members_body, n, len(evens)),
        evens + others,
        [shaped(n * len(evens), 2 * clusters, BF16)]
        + [shaped(n, 2 * clusters, BF16)] * len(others),
    )


def stat_body(has_near, count, own, *refs):
    scores, refs = refs[: count + 1], refs[count + 1 :]
    pairs, out, wide = refs[:count], refs[count], refs[count + 1 :]
    n, clusters = scores[0].shape
    member = whole(own[:n, :])
    total = jnp.sum(member * scores[0][...], axis=0, keepdims=True)
    for i in range(count):
        pair = pairs[i]
        other = whole(pair[:n, pair.shape[1] - 2 * clusters :])
        part = jnp.sum(other * scores[i + 1][:n, :], axis=0, keepdims=True)
        total += part if i < has_near else 2.0 * part
    size = jnp.sum(member, axis=0, keepdims=True)
    row = lax.broadcasted_iota(jnp.int32, out.shape, 0)
    stat = jnp.where(row == 0, total, jnp.where(row == 1, size, 0.0))
    out[...] = stat
    for back, score in zip(wide, scores[1:]):
        back[:n, :] = score[:n, :]
        back[n : n + STAT_ROWS, :] = stat
        rest = back.shape[0] - n - STAT_ROWS
        if rest:
            back[n + STAT_ROWS :, :] = jnp.zeros((rest, clusters), F32)


def stat_call(has_near, own, scores, pairs, extra):
    n, clusters = scores[0].shape
    return call(
        functools.partial(stat_body, has_near, len(pairs)),
        [own] + scores + pairs,
        [shaped(STAT_ROWS, clusters)] + [shaped(n + extra, clusters)] * len(pairs),
    )


def other_body(n, count, *refs):
    pairs, refs = refs[:count], refs[count:]
    kernels, refs = refs[: 2 * count], refs[2 * count :]
    even, odd = refs[-2:]
    half, clusters = even.shape
    over = (((0,), (0,)), ((), ()))
    for part, out in enumerate((odd, even)):
        columns = slice((1 - part) * half, (2 - part) * half)
        acc = jnp.zeros((half, clusters), F32)
        for i, pair in enumerate(pairs):
            both = pair[:n, pair.shape[1] - 2 * clusters :]
            a = lax.dot_general(
                kernels[2 * i][:, columns], both, over, preferred_element_type=F32
            )
            b = lax.dot_general(
                kernels[2 * i + 1][:, columns],
                both[:, :clusters],
                over,
                preferred_element_type=F32,
            )
            acc += a[:, :clusters] + (a[:, clusters:] + b)
        out[...] = acc


def other_call(n, half, clusters, pairs, kernels, after=()):
    return call(
        functools.partial(other_body, n, len(pairs)),
        [*pairs, *kernels, *after],
        [shaped(half, clusters)] * 2,
        [VMEM] * (len(pairs) + len(kernels)) + [ANY] * len(after),
        flops=12 * n * len(pairs) * half * clusters,
    )


def fold_body(n, count, even, received, *refs):
    stats, outs = refs[:count], refs[count:]
    for j, out in enumerate(outs):
        rows = slice(j * n, (j + 1) * n)
        out[:n, :] = even[rows, :] + received[rows, :]
        if count:
            out[n:, :] = stats[0][...] + stats[1][...]


def fold_call(n, even, received, stats):
    half, clusters = even.shape
    extra = STAT_ROWS if stats else 0
    return call(
        functools.partial(fold_body, n, len(stats)),
        [even, received] + stats,
        [shaped(n + extra, clusters)] * (half // n),
    )


def first_body(n, stats, backs, *refs):
    smalls, refs = refs[:stats], refs[stats:]
    (*parts, far, out, stat_out) = refs
    stat = smalls[0][...]
    for ref in smalls[1:]:
        stat += ref[...]
    total = parts[0][:n, :]
    for ref in parts[1:]:
        total += ref[:n, :]
    for ref in parts[len(parts) - backs :]:
        stat += ref[n : n + STAT_ROWS, :]
    out[...] = total
    far[:n, :] = total
    far[n:, :] = jnp.zeros((far.shape[0] - n, far.shape[1]), F32)
    stat_out[...] = stat


def widen_body(scores, stat, other, out):
    n = scores.shape[0]
    out[:n, :] = scores[...]
    out[n:, :] = stat[...] + other[...]


def last_body(n, *refs):
    parts, (members, standardized) = refs[:-2], refs[-2:]
    total, stat = parts[0][:n, :], parts[0][n:, :]
    for ref in parts[1:]:
        total += ref[:n, :]
        if ref.shape[0] == n + STAT_ROWS:
            stat += ref[n:, :]
    x = standardize(total, stat[1:2, :], stat[0:1, :])
    standardized[...] = x
    members[...] = normalize(jnp.exp(-2.0 * x))


def on_device(rows, cols, features, logits):
    n, clusters = logits.shape
    width = features.shape[1]
    half = n * cols // 2
    masks = list(range(2, cols, 2))
    order = [0] + masks
    order = order + [k + 1 for k in order]
    has_near = int(rows % 2 == 0)
    half_rows = rows // 2
    if has_near:
        place = [2 * q if q < half_rows else 2 * (q - half_rows) + 1 for q in range(rows)]
        offsets = list(range(1, half_rows))
    else:
        place = list(range(rows))
        offsets = list(range(1, half_rows + 1))
    steps = ([0] if has_near else []) + offsets

    def by_col(x, mask):
        return lax.ppermute(x, "col", [(i, i ^ mask) for i in range(cols)])

    def shift(x, d):
        if d == 0:
            pairs = [(i, i ^ 1) for i in range(rows)]
        else:
            pairs = [(place[(q + d) % rows], place[q]) for q in range(rows)]
        return lax.ppermute(x, "row", pairs)

    column = jnp.reshape(lax.axis_index("col"), (1,)).astype(jnp.int32)
    own_rows = lax.dynamic_slice_in_dim(features, lax.axis_index("col") * n, n, 0)
    pair, wide, message = call(
        prepare_body,
        [logits, own_rows],
        [
            shaped(n, 2 * clusters, BF16),
            shaped(n + WIDE_ROWS, 2 * clusters, BF16),
            shaped(n, width + 2 * clusters, BF16),
        ],
        hidden=True,
    )
    far_rows = [shift(own_rows if d else message, d) for d in steps]
    others = [shift(wide, d) if d else far_rows[0] for d in steps]
    evens = [pair] + [by_col(pair, k) for k in masks]
    members = evens + [by_col(x, 1) for x in evens]
    half = n * len(evens)
    odds = members[len(evens) :]
    diag = kernel_call(n, order, column, own_rows, features)
    cross = []
    for x in far_rows[has_near:]:
        after = (cross or diag)[-1:]
        cross += kernel_call(n, order, column, x, features, after, CROSS_COST)
    extra = [0] + [BACK_ROWS] * len(offsets)
    scores = scores_call(0, evens, diag + cross, [], extra, hidden=True)
    near = []
    scores = scores_call(half, odds, diag + cross, scores, extra, hidden=True)
    t_even, t_odd = other_call(n, half, clusters, others[has_near:], cross, scores[:1])
    if has_near:
        near = kernel_call(n, order, column, far_rows[0], features, cross[-1:], NEAR_COST)
        scores[1:1] = scores_call(
            0, members, near, [], [BACK_ROWS], hidden=True, after=[t_even]
        )
    stat, *backs = stat_call(has_near, pair, scores, others, BACK_ROWS)
    sent = fold_call(n, t_even, by_col(t_odd, 1), [])
    parts = [by_col(x, k) for k, x in zip(masks, sent[1:])]
    backs = [shift(x, -d) for d, x in zip(steps, backs)]
    stats = [stat] + [shift(stat, d) for d in offsets]
    far, total, stat = call(
        functools.partial(first_body, n, len(stats), len(backs)),
        stats + [sent[0], scores[0]] + parts + backs,
        [shaped(n + FAR_ROWS, clusters), shaped(n, clusters), shaped(STAT_ROWS, clusters)],
    )

    kernels = diag + near + cross
    others = [shift(far, d) for d in steps]
    (full,) = call(
        widen_body, [total, stat, by_col(stat, 1)], [shaped(n + STAT_ROWS, clusters)]
    )
    evens = [full] + [by_col(full, k) for k in masks]
    even, *others = members_call(n, evens, others)
    odd = by_col(even, 1)
    extra = [0] + [LAST_ROWS] * len(steps)
    scores = scores_call(0, [even], kernels, [], extra)
    t_even, t_odd = other_call(n, half, clusters, others[has_near:], cross)
    *scores, stat = scores_call(
        half, [odd], kernels, scores, extra, weights=[even] + others, has_near=has_near
    )
    for x in [shift(stat, d) for d in range(1, rows)]:
        stat = stat + x
    sent = fold_call(n, t_even, by_col(t_odd, 1), [stat, by_col(stat, 1)])
    parts = [by_col(x, k) for k, x in zip(masks, sent[1:])]
    backs = [shift(x, -d) for d, x in zip(steps, scores[1:])]
    return tuple(
        call(
            functools.partial(last_body, n),
            [sent[0], scores[0]] + backs + parts,
            [shaped(n, clusters)] * 2,
        )
    )


def solution(mesh):
    return jax.shard_map(
        functools.partial(on_device, mesh.shape["row"], mesh.shape["col"]),
        mesh=mesh,
        in_specs=(P("row", None), P(("row", "col"), None)),
        out_specs=(P(("row", "col"), None), P(("row", "col"), None)),
        check_vma=False,
    )
```

```python
import functools

import jax
import jax.numpy as jnp
from jax import lax
from jax.experimental import pallas as pl
from jax.experimental.pallas import tpu as pltpu
from jax.sharding import PartitionSpec as P

ITERS = 2
STAT_ROWS = 8
GATHER_ROWS = (STAT_ROWS, 0)
WIDE_ROWS = 16
LAST_ROWS = 32
BACK_ROWS = 16
VMEM_BYTES = 24 * 1024 * 1024
NEAR_COST = 2.7
CROSS_COST = 3
VMEM = pl.BlockSpec(memory_space=pltpu.VMEM)
SMEM = pl.BlockSpec(memory_space=pltpu.SMEM)
ANY = pl.BlockSpec(memory_space=pl.ANY)
BF16 = jnp.bfloat16
F32 = jnp.float32


def shaped(rows, columns, dtype=F32):
    return jax.ShapeDtypeStruct((rows, columns), dtype)


def call(body, args, outs, specs=None, scratch=(), flops=0, hidden=False):
    bytes_accessed = sum(x.size * x.dtype.itemsize for x in list(args) + list(outs))
    if hidden:
        flops = bytes_accessed = 0
    made = pl.pallas_call(
        body,
        in_specs=specs or [VMEM] * len(args),
        out_specs=[VMEM] * len(outs),
        out_shape=list(outs),
        scratch_shapes=list(scratch),
        compiler_params=pltpu.CompilerParams(vmem_limit_bytes=VMEM_BYTES),
        cost_estimate=pl.CostEstimate(
            flops=flops, bytes_accessed=bytes_accessed, transcendentals=0
        ),
    )(*args)
    return list(made)


def split(x):
    high = x.astype(BF16)
    low = (x - high.astype(F32)).astype(BF16)
    return high, low


def whole(pair):
    clusters = pair.shape[1] // 2
    return pair[:, :clusters].astype(F32) + pair[:, clusters:].astype(F32)


def standardize(scores, size, weighted):
    distance = weighted / (size * size) - 2.0 * scores / size
    centered = distance - jnp.mean(distance, axis=1, keepdims=True)
    spread = jnp.mean(centered * centered, axis=1, keepdims=True)
    return centered / jnp.sqrt(spread + 1e-06)


def normalize(raised):
    return raised / jnp.sum(raised, axis=1, keepdims=True)


def store_pair(out, rows, x):
    clusters = x.shape[1]
    high, low = split(x)
    out[rows, :clusters] = high
    out[rows, clusters:] = low


def prepare_body(logits, rows, pair, wide, message):
    n, width = rows.shape
    member = normalize(jnp.exp(logits[...]))
    store_pair(pair, slice(0, n), member)
    store_pair(wide, slice(0, n), member)
    wide[n:, :] = jnp.zeros((wide.shape[0] - n, wide.shape[1]), BF16)
    message[:, :width] = rows[...]
    message[:, width:] = pair[...]


def kernel_body(order, column_ref, rows_ref, plane_ref, *refs):
    high_ref, low_ref = refs[-2:]
    n, width = high_ref.shape[0], plane_ref.shape[1]
    column = column_ref[0]
    rows = rows_ref[:n, :width]
    for j, k in enumerate(order):
        start = pl.multiple_of(lax.bitwise_xor(column, k) * n, n)
        inner = lax.dot_general(
            rows,
            plane_ref[pl.ds(start, n), :],
            (((1,), (1,)), ((), ())),
            preferred_element_type=F32,
        )
        t = inner / width
        high, low = split(t * (3.0 + t * (3.0 + t)))
        high_ref[:, j * n : (j + 1) * n] = high
        low_ref[:, j * n : (j + 1) * n] = low


def kernel_call(n, order, column, rows, plane, after=(), cost=1):
    total = plane.shape[0]
    return call(
        functools.partial(kernel_body, tuple(order)),
        [column, rows, plane, *after],
        [shaped(n, total, BF16)] * 2,
        [SMEM, VMEM, VMEM] + [ANY] * len(after),
        flops=int(2 * cost * n) * total * plane.shape[1],
    )


def scores_body(at, pieces, kernels, partials, unused, weights, has_near, *refs):
    members, refs = refs[:pieces], refs[pieces:]
    blocks, refs = refs[:kernels], refs[kernels:]
    before, refs = refs[:partials], refs[partials:]
    own, outs = refs[:weights], refs[weights + unused :]
    n = blocks[0].shape[0]
    clusters = members[0].shape[1] // 2
    for i, out in enumerate(outs[: kernels // 2]):
        both, rest, start = None, None, at
        for piece in members:
            columns = slice(start, start + piece.shape[0])
            start += piece.shape[0]
            a = jnp.dot(blocks[2 * i][:, columns], piece[...], preferred_element_type=F32)
            b = jnp.dot(
                blocks[2 * i + 1][:, columns],
                piece[:, :clusters],
                preferred_element_type=F32,
            )
            both = a if both is None else both + a
            rest = b if rest is None else rest + b
        s = both[:, :clusters] + (both[:, clusters:] + rest)
        if partials:
            s += before[i][:n, :]
        out[:n, :] = s
        if out.shape[0] > n:
            out[n:, :] = jnp.zeros((out.shape[0] - n, clusters), F32)
    if weights:
        count = len(outs) - 1
        stat = outs[count]
        stat_body(has_near, *own[:1], *outs[:count], *own[1:], stat)


def scores_call(
    at, members, kernels, partials, extra, hidden=False, after=(), weights=(), has_near=0
):
    n, clusters = kernels[0].shape[0], members[0].shape[1] // 2
    depth = sum(x.shape[0] for x in members)
    return call(
        functools.partial(
            scores_body,
            at,
            len(members),
            len(kernels),
            len(partials),
            len(after),
            len(weights),
            has_near,
        ),
        [*members, *kernels, *partials, *weights, *after],
        [shaped(n + e, clusters) for e in extra]
        + [shaped(STAT_ROWS, clusters)] * (len(weights) > 0),
        [VMEM] * (len(members) + len(kernels) + len(partials) + len(weights))
        + [ANY] * len(after),
        flops=3 * n * len(kernels) * depth * clusters,
        hidden=hidden,
    )


def members_body(n, smalls, evens, others, *refs):
    stats, refs = refs[:smalls], refs[smalls:]
    own, refs = refs[:evens], refs[evens:]
    rest, refs = refs[:others], refs[others:]
    even, pairs = refs[0], refs[1:]
    stat = stats[0][...]
    for ref in stats[1:]:
        stat += ref[...]
    for ref in rest:
        stat += ref[n : n + STAT_ROWS, :]
    weighted, size = stat[0:1, :], stat[1:2, :]

    def member_of(x):
        return normalize(jnp.exp(-2.0 * standardize(x, size, weighted)))

    for j, ref in enumerate(own):
        store_pair(even, slice(j * n, (j + 1) * n), member_of(ref[:n, :]))
    for pair, ref in zip(pairs, rest):
        store_pair(pair, slice(0, n), member_of(ref[:n, :]))


def members_call(n, stats, evens, others):
    clusters = evens[0].shape[1]
    return call(
        functools.partial(members_body, n, len(stats), len(evens), len(others)),
        stats + evens + others,
        [shaped(n * len(evens), 2 * clusters, BF16)]
        + [shaped(n, 2 * clusters, BF16)] * len(others),
    )


def stat_body(has_near, own, *refs):
    out, refs = refs[-1], refs[:-1]
    count = len(refs) // 2
    scores, pairs = refs[: count + 1], refs[count + 1 :]
    n, clusters = scores[0].shape
    member = whole(own[:n, :])
    total = jnp.sum(member * scores[0][...], axis=0, keepdims=True)
    for i in range(count):
        pair = pairs[i]
        other = whole(pair[:n, pair.shape[1] - 2 * clusters :])
        part = jnp.sum(other * scores[i + 1][:n, :], axis=0, keepdims=True)
        total += part if i < has_near else 2.0 * part
    size = jnp.sum(member, axis=0, keepdims=True)
    row = lax.broadcasted_iota(jnp.int32, out.shape, 0)
    out[...] = jnp.where(row == 0, total, jnp.where(row == 1, size, 0.0))


def stat_call(has_near, own, scores, pairs):
    clusters = scores[0].shape[1]
    return call(
        functools.partial(stat_body, has_near),
        [own] + scores + pairs,
        [shaped(STAT_ROWS, clusters)],
    )[0]


def other_body(n, count, *refs):
    pairs, refs = refs[:count], refs[count:]
    kernels, refs = refs[: 2 * count], refs[2 * count :]
    even, odd = refs[-2:]
    half, clusters = even.shape
    over = (((0,), (0,)), ((), ()))
    for part, out in enumerate((odd, even)):
        columns = slice((1 - part) * half, (2 - part) * half)
        acc = jnp.zeros((half, clusters), F32)
        for i, pair in enumerate(pairs):
            both = pair[:n, pair.shape[1] - 2 * clusters :]
            a = lax.dot_general(
                kernels[2 * i][:, columns], both, over, preferred_element_type=F32
            )
            b = lax.dot_general(
                kernels[2 * i + 1][:, columns],
                both[:, :clusters],
                over,
                preferred_element_type=F32,
            )
            acc += a[:, :clusters] + (a[:, clusters:] + b)
        out[...] = acc


def other_call(n, half, clusters, pairs, kernels, stat, after=()):
    return call(
        functools.partial(other_body, n, len(pairs)),
        [*pairs, *kernels, *stat, *after],
        [shaped(half, clusters), shaped(half + STAT_ROWS * len(stat), clusters)],
        [VMEM] * (len(pairs) + len(kernels) + len(stat)) + [ANY] * len(after),
        flops=12 * n * len(pairs) * half * clusters,
    )


def fold_body(n, count, even, received, *refs):
    stats, outs = refs[:count], refs[count:]
    half = even.shape[0]
    stat = stats[0][...]
    for ref in stats[1:]:
        stat += ref[...]
    if received.shape[0] > half:
        stat += received[half:, :]
    for j, out in enumerate(outs):
        rows = slice(j * n, (j + 1) * n)
        out[:n, :] = even[rows, :] + received[rows, :]
        out[n:, :] = stat


def fold_call(n, even, received, stats, extra):
    half, clusters = even.shape
    return call(
        functools.partial(fold_body, n, len(stats)),
        [even, received] + stats,
        [shaped(n + extra, clusters)] * (half // n),
    )


def sum_body(n, last, *refs):
    many = 2 if last else 1 + len(GATHER_ROWS)
    refs, outs = refs[:-many], refs[-many:]
    total, stat = refs[0][:n, :], refs[0][n:, :]
    for ref in refs[1:]:
        total += ref[:n, :]
        if ref.shape[0] == n + STAT_ROWS:
            stat += ref[n:, :]
    if last:
        members, standardized = outs
        x = standardize(total, stat[1:2, :], stat[0:1, :])
        standardized[...] = x
        members[...] = normalize(jnp.exp(-2.0 * x))
    else:
        stats, fulls = outs[0], outs[1:]
        stats[...] = stat
        for full in fulls:
            full[:n, :] = total
            if full.shape[0] > n:
                full[n:, :] = stat


def on_device(rows, cols, features, logits):
    n, clusters = logits.shape
    width = features.shape[1]
    half = n * cols // 2
    masks = list(range(2, cols, 2))
    order = [0] + masks
    order = order + [k + 1 for k in order]
    has_near = int(rows % 2 == 0)
    half_rows = rows // 2
    if has_near:
        place = [2 * q if q < half_rows else 2 * (q - half_rows) + 1 for q in range(rows)]
        offsets = list(range(1, half_rows))
    else:
        place = list(range(rows))
        offsets = list(range(1, half_rows + 1))
    steps = ([0] if has_near else []) + offsets

    def by_col(x, mask):
        return lax.ppermute(x, "col", [(i, i ^ mask) for i in range(cols)])

    def shift(x, d):
        if d == 0:
            pairs = [(i, i ^ 1) for i in range(rows)]
        else:
            pairs = [(place[(q + d) % rows], place[q]) for q in range(rows)]
        return lax.ppermute(x, "row", pairs)

    column = jnp.reshape(lax.axis_index("col"), (1,)).astype(jnp.int32)
    own_rows = lax.dynamic_slice_in_dim(features, lax.axis_index("col") * n, n, 0)
    pair, wide, message = call(
        prepare_body,
        [logits, own_rows],
        [
            shaped(n, 2 * clusters, BF16),
            shaped(n + WIDE_ROWS, 2 * clusters, BF16),
            shaped(n, width + 2 * clusters, BF16),
        ],
        hidden=True,
    )
    far_rows = [shift(own_rows if d else message, d) for d in steps]
    others = [shift(wide, d) if d else far_rows[0] for d in steps]
    evens = [pair] + [by_col(pair, k) for k in masks]
    members = evens + [by_col(x, 1) for x in evens]
    early = 1 + has_near
    extra = [0] + [BACK_ROWS] * len(steps)
    half = n * len(evens)
    diag = kernel_call(n, order, column, own_rows, features)
    cross = []
    for x in far_rows[has_near:]:
        after = (cross or diag)[-1:]
        cross += kernel_call(n, order, column, x, features, after, CROSS_COST)
    some = extra[:1] + extra[early:]
    near, far_scores = [], []
    if has_near:
        near = kernel_call(n, order, column, far_rows[0], features, cross[-1:], NEAR_COST)
    scores = scores_call(0, members, diag + cross, [], some, hidden=True)
    after = scores[:1] + near[:1]
    if has_near:
        scores[1:1] = scores_call(0, members, near, [], extra[1:2], hidden=True)
    kernels = diag + near + cross
    own = pair

    for iteration in range(ITERS):
        last = iteration == ITERS - 1
        if iteration > 0:
            even, *others = members_call(n, stats, evens, others)
            odd = by_col(even, 1)
            own = even
            scores = scores_call(0, [even], kernels, [], extra)
        if last:
            t_even, t_odd = other_call(n, half, clusters, others[has_near:], cross, [])
            extra = [0] + [LAST_ROWS] * len(steps)
            *scores, stat = scores_call(
                half, [odd], kernels, scores, extra, False, (), [own] + others, has_near
            )
            for x in [shift(stat, d) for d in range(1, rows)]:
                stat = stat + x
            sent = fold_call(
                n, t_even, by_col(t_odd, 1), [stat, by_col(stat, 1)], STAT_ROWS
            )
        else:
            if iteration > 0:
                scores = scores_call(half, [odd], kernels, scores, extra)
            stat = stat_call(has_near, own, scores, others)
            t_even, t_odd = other_call(
                n, half, clusters, others[has_near:], cross, [], after
            )
            sent = fold_call(
                n, t_even, by_col(t_odd, 1), [stat, by_col(stat, 1)], STAT_ROWS
            )
        parts = [by_col(x, k) for k, x in zip(masks, sent[1:])]
        back = [shift(x, -d) for d, x in zip(steps, scores[1:])]
        outs = [shaped(n, clusters)] * 2
        if not last:
            outs = [shaped(STAT_ROWS, clusters)]
            outs += [shaped(n + r, clusters) for r in GATHER_ROWS]
        done = call(
            functools.partial(sum_body, n, last),
            [sent[0], scores[0]] + back + parts,
            outs,
        )
        if not last:
            stats, full, total = done
            evens = [total] + [by_col(total, k) for k in masks]
            others = [shift(full, d) for d in steps]
            stats = [stats] + [shift(stats, -d) for d in offsets]
    return tuple(done)


def solution(mesh):
    return jax.shard_map(
        functools.partial(on_device, mesh.shape["row"], mesh.shape["col"]),
        mesh=mesh,
        in_specs=(P("row", None), P(("row", "col"), None)),
        out_specs=(P(("row", "col"), None), P(("row", "col"), None)),
        check_vma=False,
    )
```

```python
import functools

import jax
import jax.numpy as jnp
from jax import lax
from jax.experimental import pallas as pl
from jax.experimental.pallas import tpu as pltpu
from jax.sharding import PartitionSpec as P

ITERS = 2
STAT_ROWS = 8
GATHER_ROWS = (STAT_ROWS, 0)
WIDE_ROWS = 16
LAST_ROWS = 32
BACK_ROWS = 16
VMEM_BYTES = 24 * 1024 * 1024
NEAR_COST = 3
CROSS_COST = 2.7
VMEM = pl.BlockSpec(memory_space=pltpu.VMEM)
SMEM = pl.BlockSpec(memory_space=pltpu.SMEM)
ANY = pl.BlockSpec(memory_space=pl.ANY)
BF16 = jnp.bfloat16
F32 = jnp.float32


def shaped(rows, columns, dtype=F32):
    return jax.ShapeDtypeStruct((rows, columns), dtype)


def call(body, args, outs, specs=None, scratch=(), flops=0, hidden=False):
    bytes_accessed = sum(x.size * x.dtype.itemsize for x in list(args) + list(outs))
    if hidden:
        flops = bytes_accessed = 0
    made = pl.pallas_call(
        body,
        in_specs=specs or [VMEM] * len(args),
        out_specs=[VMEM] * len(outs),
        out_shape=list(outs),
        scratch_shapes=list(scratch),
        compiler_params=pltpu.CompilerParams(vmem_limit_bytes=VMEM_BYTES),
        cost_estimate=pl.CostEstimate(
            flops=flops, bytes_accessed=bytes_accessed, transcendentals=0
        ),
    )(*args)
    return list(made)


def split(x):
    high = x.astype(BF16)
    low = (x - high.astype(F32)).astype(BF16)
    return high, low


def whole(pair):
    clusters = pair.shape[1] // 2
    return pair[:, :clusters].astype(F32) + pair[:, clusters:].astype(F32)


def standardize(scores, size, weighted):
    distance = weighted / (size * size) - 2.0 * scores / size
    centered = distance - jnp.mean(distance, axis=1, keepdims=True)
    spread = jnp.mean(centered * centered, axis=1, keepdims=True)
    return centered / jnp.sqrt(spread + 1e-06)


def normalize(raised):
    return raised / jnp.sum(raised, axis=1, keepdims=True)


def store_pair(out, rows, x):
    clusters = x.shape[1]
    high, low = split(x)
    out[rows, :clusters] = high
    out[rows, clusters:] = low


def prepare_body(logits, rows, pair, wide, message):
    n, width = rows.shape
    member = normalize(jnp.exp(logits[...]))
    store_pair(pair, slice(0, n), member)
    store_pair(wide, slice(0, n), member)
    wide[n:, :] = jnp.zeros((wide.shape[0] - n, wide.shape[1]), BF16)
    message[:, :width] = rows[...]
    message[:, width:] = pair[...]


def kernel_body(order, column_ref, rows_ref, plane_ref, *refs):
    high_ref, low_ref = refs[-2:]
    n, width = high_ref.shape[0], plane_ref.shape[1]
    column = column_ref[0]
    rows = rows_ref[:n, :width]
    for j, k in enumerate(order):
        start = pl.multiple_of(lax.bitwise_xor(column, k) * n, n)
        inner = lax.dot_general(
            rows,
            plane_ref[pl.ds(start, n), :],
            (((1,), (1,)), ((), ())),
            preferred_element_type=F32,
        )
        t = inner / width
        high, low = split(t * (3.0 + t * (3.0 + t)))
        high_ref[:, j * n : (j + 1) * n] = high
        low_ref[:, j * n : (j + 1) * n] = low


def kernel_call(n, order, column, rows, plane, after=(), cost=1):
    total = plane.shape[0]
    return call(
        functools.partial(kernel_body, tuple(order)),
        [column, rows, plane, *after],
        [shaped(n, total, BF16)] * 2,
        [SMEM, VMEM, VMEM] + [ANY] * len(after),
        flops=int(2 * cost * n) * total * plane.shape[1],
    )


def scores_body(at, pieces, kernels, partials, unused, weights, has_near, *refs):
    members, refs = refs[:pieces], refs[pieces:]
    blocks, refs = refs[:kernels], refs[kernels:]
    before, refs = refs[:partials], refs[partials:]
    own, outs = refs[:weights], refs[weights + unused :]
    n = blocks[0].shape[0]
    clusters = members[0].shape[1] // 2
    for i, out in enumerate(outs[: kernels // 2]):
        both, rest, start = None, None, at
        for piece in members:
            columns = slice(start, start + piece.shape[0])
            start += piece.shape[0]
            a = jnp.dot(blocks[2 * i][:, columns], piece[...], preferred_element_type=F32)
            b = jnp.dot(
                blocks[2 * i + 1][:, columns],
                piece[:, :clusters],
                preferred_element_type=F32,
            )
            both = a if both is None else both + a
            rest = b if rest is None else rest + b
        s = both[:, :clusters] + (both[:, clusters:] + rest)
        if partials:
            s += before[i][:n, :]
        out[:n, :] = s
        if out.shape[0] > n:
            out[n:, :] = jnp.zeros((out.shape[0] - n, clusters), F32)
    if weights:
        count = len(outs) - 1
        stat = outs[count]
        stat_body(has_near, *own[:1], *outs[:count], *own[1:], stat)


def scores_call(
    at, members, kernels, partials, extra, hidden=False, after=(), weights=(), has_near=0
):
    n, clusters = kernels[0].shape[0], members[0].shape[1] // 2
    depth = sum(x.shape[0] for x in members)
    return call(
        functools.partial(
            scores_body,
            at,
            len(members),
            len(kernels),
            len(partials),
            len(after),
            len(weights),
            has_near,
        ),
        [*members, *kernels, *partials, *weights, *after],
        [shaped(n + e, clusters) for e in extra]
        + [shaped(STAT_ROWS, clusters)] * (len(weights) > 0),
        [VMEM] * (len(members) + len(kernels) + len(partials) + len(weights))
        + [ANY] * len(after),
        flops=3 * n * len(kernels) * depth * clusters,
        hidden=hidden,
    )


def members_body(n, smalls, evens, others, *refs):
    stats, refs = refs[:smalls], refs[smalls:]
    own, refs = refs[:evens], refs[evens:]
    rest, refs = refs[:others], refs[others:]
    even, pairs = refs[0], refs[1:]
    stat = stats[0][...]
    for ref in stats[1:]:
        stat += ref[...]
    for ref in rest:
        stat += ref[n : n + STAT_ROWS, :]
    weighted, size = stat[0:1, :], stat[1:2, :]

    def member_of(x):
        return normalize(jnp.exp(-2.0 * standardize(x, size, weighted)))

    for j, ref in enumerate(own):
        store_pair(even, slice(j * n, (j + 1) * n), member_of(ref[:n, :]))
    for pair, ref in zip(pairs, rest):
        store_pair(pair, slice(0, n), member_of(ref[:n, :]))


def members_call(n, stats, evens, others):
    clusters = evens[0].shape[1]
    return call(
        functools.partial(members_body, n, len(stats), len(evens), len(others)),
        stats + evens + others,
        [shaped(n * len(evens), 2 * clusters, BF16)]
        + [shaped(n, 2 * clusters, BF16)] * len(others),
    )


def stat_body(has_near, own, *refs):
    out, refs = refs[-1], refs[:-1]
    count = len(refs) // 2
    scores, pairs = refs[: count + 1], refs[count + 1 :]
    n, clusters = scores[0].shape
    member = whole(own[:n, :])
    total = jnp.sum(member * scores[0][...], axis=0, keepdims=True)
    for i in range(count):
        pair = pairs[i]
        other = whole(pair[:n, pair.shape[1] - 2 * clusters :])
        part = jnp.sum(other * scores[i + 1][:n, :], axis=0, keepdims=True)
        total += part if i < has_near else 2.0 * part
    size = jnp.sum(member, axis=0, keepdims=True)
    row = lax.broadcasted_iota(jnp.int32, out.shape, 0)
    out[...] = jnp.where(row == 0, total, jnp.where(row == 1, size, 0.0))


def stat_call(has_near, own, scores, pairs):
    clusters = scores[0].shape[1]
    return call(
        functools.partial(stat_body, has_near),
        [own] + scores + pairs,
        [shaped(STAT_ROWS, clusters)],
    )[0]


def other_body(n, count, *refs):
    pairs, refs = refs[:count], refs[count:]
    kernels, refs = refs[: 2 * count], refs[2 * count :]
    even, odd = refs[-2:]
    half, clusters = even.shape
    over = (((0,), (0,)), ((), ()))
    for part, out in enumerate((odd, even)):
        columns = slice((1 - part) * half, (2 - part) * half)
        acc = jnp.zeros((half, clusters), F32)
        for i, pair in enumerate(pairs):
            both = pair[:n, pair.shape[1] - 2 * clusters :]
            a = lax.dot_general(
                kernels[2 * i][:, columns], both, over, preferred_element_type=F32
            )
            b = lax.dot_general(
                kernels[2 * i + 1][:, columns],
                both[:, :clusters],
                over,
                preferred_element_type=F32,
            )
            acc += a[:, :clusters] + (a[:, clusters:] + b)
        out[...] = acc


def other_call(n, half, clusters, pairs, kernels, stat, after=()):
    return call(
        functools.partial(other_body, n, len(pairs)),
        [*pairs, *kernels, *stat, *after],
        [shaped(half, clusters), shaped(half + STAT_ROWS * len(stat), clusters)],
        [VMEM] * (len(pairs) + len(kernels) + len(stat)) + [ANY] * len(after),
        flops=12 * n * len(pairs) * half * clusters,
    )


def fold_body(n, count, even, received, *refs):
    stats, outs = refs[:count], refs[count:]
    half = even.shape[0]
    stat = stats[0][...]
    for ref in stats[1:]:
        stat += ref[...]
    if received.shape[0] > half:
        stat += received[half:, :]
    for j, out in enumerate(outs):
        rows = slice(j * n, (j + 1) * n)
        out[:n, :] = even[rows, :] + received[rows, :]
        out[n:, :] = stat


def fold_call(n, even, received, stats, extra):
    half, clusters = even.shape
    return call(
        functools.partial(fold_body, n, len(stats)),
        [even, received] + stats,
        [shaped(n + extra, clusters)] * (half // n),
    )


def sum_body(n, last, *refs):
    many = 2 if last else 1 + len(GATHER_ROWS)
    refs, outs = refs[:-many], refs[-many:]
    total, stat = refs[0][:n, :], refs[0][n:, :]
    for ref in refs[1:]:
        total += ref[:n, :]
        if ref.shape[0] == n + STAT_ROWS:
            stat += ref[n:, :]
    if last:
        members, standardized = outs
        x = standardize(total, stat[1:2, :], stat[0:1, :])
        standardized[...] = x
        members[...] = normalize(jnp.exp(-2.0 * x))
    else:
        stats, fulls = outs[0], outs[1:]
        stats[...] = stat
        for full in fulls:
            full[:n, :] = total
            if full.shape[0] > n:
                full[n:, :] = stat


def on_device(rows, cols, features, logits):
    n, clusters = logits.shape
    width = features.shape[1]
    half = n * cols // 2
    masks = list(range(2, cols, 2))
    order = [0] + masks
    order = order + [k + 1 for k in order]
    has_near = int(rows % 2 == 0)
    half_rows = rows // 2
    if has_near:
        place = [2 * q if q < half_rows else 2 * (q - half_rows) + 1 for q in range(rows)]
        offsets = list(range(1, half_rows))
    else:
        place = list(range(rows))
        offsets = list(range(1, half_rows + 1))
    steps = ([0] if has_near else []) + offsets

    def by_col(x, mask):
        return lax.ppermute(x, "col", [(i, i ^ mask) for i in range(cols)])

    def shift(x, d):
        if d == 0:
            pairs = [(i, i ^ 1) for i in range(rows)]
        else:
            pairs = [(place[(q + d) % rows], place[q]) for q in range(rows)]
        return lax.ppermute(x, "row", pairs)

    column = jnp.reshape(lax.axis_index("col"), (1,)).astype(jnp.int32)
    own_rows = lax.dynamic_slice_in_dim(features, lax.axis_index("col") * n, n, 0)
    pair, wide, message = call(
        prepare_body,
        [logits, own_rows],
        [
            shaped(n, 2 * clusters, BF16),
            shaped(n + WIDE_ROWS, 2 * clusters, BF16),
            shaped(n, width + 2 * clusters, BF16),
        ],
        hidden=True,
    )
    far_rows = [shift(own_rows if d else message, d) for d in steps]
    others = [shift(wide, d) if d else far_rows[0] for d in steps]
    evens = [pair] + [by_col(pair, k) for k in masks]
    members = evens + [by_col(x, 1) for x in evens]
    early = 1 + has_near
    extra = [0] + [BACK_ROWS] * len(steps)
    half = n * len(evens)
    diag = kernel_call(n, order, column, own_rows, features)
    cross = []
    for x in far_rows[has_near:]:
        after = (cross or diag)[-1:]
        cross += kernel_call(n, order, column, x, features, after, CROSS_COST)
    some = extra[:1] + extra[early:]
    near, far_scores = [], []
    if has_near:
        near = kernel_call(n, order, column, far_rows[0], features, cross[-1:], NEAR_COST)
    scores = scores_call(0, members, diag + cross, [], some, hidden=True)
    after = scores[:1] + near[:1]
    if has_near:
        scores[1:1] = scores_call(0, members, near, [], extra[1:2], hidden=True)
    kernels = diag + near + cross
    own = pair

    for iteration in range(ITERS):
        last = iteration == ITERS - 1
        if iteration > 0:
            even, *others = members_call(n, stats, evens, others)
            odd = by_col(even, 1)
            own = even
            scores = scores_call(0, [even], kernels, [], extra)
        if last:
            t_even, t_odd = other_call(n, half, clusters, others[has_near:], cross, [])
            extra = [0] + [LAST_ROWS] * len(steps)
            *scores, stat = scores_call(
                half, [odd], kernels, scores, extra, False, (), [own] + others, has_near
            )
            for x in [shift(stat, d) for d in range(1, rows)]:
                stat = stat + x
            sent = fold_call(
                n, t_even, by_col(t_odd, 1), [stat, by_col(stat, 1)], STAT_ROWS
            )
        else:
            if iteration > 0:
                scores = scores_call(half, [odd], kernels, scores, extra)
            stat = stat_call(has_near, own, scores, others)
            t_even, t_odd = other_call(
                n, half, clusters, others[has_near:], cross, [], after
            )
            sent = fold_call(
                n, t_even, by_col(t_odd, 1), [stat, by_col(stat, 1)], STAT_ROWS
            )
        parts = [by_col(x, k) for k, x in zip(masks, sent[1:])]
        back = [shift(x, -d) for d, x in zip(steps, scores[1:])]
        outs = [shaped(n, clusters)] * 2
        if not last:
            outs = [shaped(STAT_ROWS, clusters)]
            outs += [shaped(n + r, clusters) for r in GATHER_ROWS]
        done = call(
            functools.partial(sum_body, n, last),
            [sent[0], scores[0]] + back + parts,
            outs,
        )
        if not last:
            stats, full, total = done
            evens = [total] + [by_col(total, k) for k in masks]
            others = [shift(full, d) for d in steps]
            stats = [stats] + [shift(stats, -d) for d in offsets]
    return tuple(done)


def solution(mesh):
    return jax.shard_map(
        functools.partial(on_device, mesh.shape["row"], mesh.shape["col"]),
        mesh=mesh,
        in_specs=(P("row", None), P(("row", "col"), None)),
        out_specs=(P(("row", "col"), None), P(("row", "col"), None)),
        check_vma=False,
    )
```

```python
import functools

import jax
import jax.numpy as jnp
from jax import lax
from jax.experimental import pallas as pl
from jax.experimental.pallas import tpu as pltpu
from jax.sharding import PartitionSpec as P

ITERS = 2
STAT_ROWS = 8
GATHER_ROWS = (STAT_ROWS, 0)
WIDE_ROWS = 16
LAST_ROWS = 32
BACK_ROWS = 16
VMEM_BYTES = 24 * 1024 * 1024
CROSS_COST = 2.7
VMEM = pl.BlockSpec(memory_space=pltpu.VMEM)
SMEM = pl.BlockSpec(memory_space=pltpu.SMEM)
ANY = pl.BlockSpec(memory_space=pl.ANY)
BF16 = jnp.bfloat16
F32 = jnp.float32


def shaped(rows, columns, dtype=F32):
    return jax.ShapeDtypeStruct((rows, columns), dtype)


def call(body, args, outs, specs=None, scratch=(), flops=0, hidden=False):
    bytes_accessed = sum(x.size * x.dtype.itemsize for x in list(args) + list(outs))
    if hidden:
        flops = bytes_accessed = 0
    made = pl.pallas_call(
        body,
        in_specs=specs or [VMEM] * len(args),
        out_specs=[VMEM] * len(outs),
        out_shape=list(outs),
        scratch_shapes=list(scratch),
        compiler_params=pltpu.CompilerParams(vmem_limit_bytes=VMEM_BYTES),
        cost_estimate=pl.CostEstimate(
            flops=flops, bytes_accessed=bytes_accessed, transcendentals=0
        ),
    )(*args)
    return list(made)


def split(x):
    high = x.astype(BF16)
    low = (x - high.astype(F32)).astype(BF16)
    return high, low


def whole(pair):
    clusters = pair.shape[1] // 2
    return pair[:, :clusters].astype(F32) + pair[:, clusters:].astype(F32)


def standardize(scores, size, weighted):
    inverse = 1.0 / size
    distance = weighted * inverse * inverse - scores * (2.0 * inverse)
    centered = distance - jnp.mean(distance, axis=1, keepdims=True)
    spread = jnp.mean(centered * centered, axis=1, keepdims=True)
    return centered * lax.rsqrt(spread + 1e-06)


def normalize(raised):
    return raised / jnp.sum(raised, axis=1, keepdims=True)


def store_pair(out, rows, x):
    clusters = x.shape[1]
    high, low = split(x)
    out[rows, :clusters] = high
    out[rows, clusters:] = low


def prepare_body(logits, rows, pair, wide, message):
    n, width = rows.shape
    member = normalize(jnp.exp(logits[...]))
    store_pair(pair, slice(0, n), member)
    store_pair(wide, slice(0, n), member)
    wide[n:, :] = jnp.zeros((wide.shape[0] - n, wide.shape[1]), BF16)
    message[:, :width] = rows[...]
    message[:, width:] = pair[...]


def kernel_body(order, column_ref, rows_ref, plane_ref, *refs):
    high_ref, low_ref = refs[-2:]
    n, width = high_ref.shape[0], plane_ref.shape[1]
    column = column_ref[0]
    rows = rows_ref[:n, :width]
    for j, k in enumerate(order):
        start = pl.multiple_of(lax.bitwise_xor(column, k) * n, n)
        inner = lax.dot_general(
            rows,
            plane_ref[pl.ds(start, n), :],
            (((1,), (1,)), ((), ())),
            preferred_element_type=F32,
        )
        t = inner / width
        high, low = split(t * (3.0 + t * (3.0 + t)))
        high_ref[:, j * n : (j + 1) * n] = high
        low_ref[:, j * n : (j + 1) * n] = low


def kernel_call(n, order, column, rows, plane, after=(), cost=1):
    total = plane.shape[0]
    return call(
        functools.partial(kernel_body, tuple(order)),
        [column, rows, plane, *after],
        [shaped(n, total, BF16)] * 2,
        [SMEM, VMEM, VMEM] + [ANY] * len(after),
        flops=int(2 * cost * n) * total * plane.shape[1],
    )


def scores_body(at, pieces, kernels, partials, unused, weights, has_near, *refs):
    members, refs = refs[:pieces], refs[pieces:]
    blocks, refs = refs[:kernels], refs[kernels:]
    before, refs = refs[:partials], refs[partials:]
    own, outs = refs[:weights], refs[weights + unused :]
    n = blocks[0].shape[0]
    clusters = members[0].shape[1] // 2
    for i, out in enumerate(outs[: kernels // 2]):
        both, rest, start = None, None, at
        for piece in members:
            columns = slice(start, start + piece.shape[0])
            start += piece.shape[0]
            a = jnp.dot(blocks[2 * i][:, columns], piece[...], preferred_element_type=F32)
            b = jnp.dot(
                blocks[2 * i + 1][:, columns],
                piece[:, :clusters],
                preferred_element_type=F32,
            )
            both = a if both is None else both + a
            rest = b if rest is None else rest + b
        s = both[:, :clusters] + (both[:, clusters:] + rest)
        if partials:
            s += before[i][:n, :]
        out[:n, :] = s
        if out.shape[0] > n:
            out[n:, :] = jnp.zeros((out.shape[0] - n, clusters), F32)
    if weights:
        count = len(outs) - 1
        stat = outs[count]
        stat_body(has_near, *own[:1], *outs[:count], *own[1:], stat)


def scores_call(
    at, members, kernels, partials, extra, hidden=False, after=(), weights=(), has_near=0
):
    n, clusters = kernels[0].shape[0], members[0].shape[1] // 2
    depth = sum(x.shape[0] for x in members)
    return call(
        functools.partial(
            scores_body,
            at,
            len(members),
            len(kernels),
            len(partials),
            len(after),
            len(weights),
            has_near,
        ),
        [*members, *kernels, *partials, *weights, *after],
        [shaped(n + e, clusters) for e in extra]
        + [shaped(STAT_ROWS, clusters)] * (len(weights) > 0),
        [VMEM] * (len(members) + len(kernels) + len(partials) + len(weights))
        + [ANY] * len(after),
        flops=3 * n * len(kernels) * depth * clusters,
        hidden=hidden,
    )


def members_body(n, smalls, evens, others, *refs):
    stats, refs = refs[:smalls], refs[smalls:]
    own, refs = refs[:evens], refs[evens:]
    rest, refs = refs[:others], refs[others:]
    even, pairs = refs[0], refs[1:]
    stat = stats[0][...]
    for ref in stats[1:]:
        stat += ref[...]
    for ref in rest:
        stat += ref[n : n + STAT_ROWS, :]
    weighted, size = stat[0:1, :], stat[1:2, :]

    def member_of(x):
        return normalize(jnp.exp(-2.0 * standardize(x, size, weighted)))

    for j, ref in enumerate(own):
        store_pair(even, slice(j * n, (j + 1) * n), member_of(ref[:n, :]))
    for pair, ref in zip(pairs, rest):
        store_pair(pair, slice(0, n), member_of(ref[:n, :]))


def members_call(n, stats, evens, others):
    clusters = evens[0].shape[1]
    return call(
        functools.partial(members_body, n, len(stats), len(evens), len(others)),
        stats + evens + others,
        [shaped(n * len(evens), 2 * clusters, BF16)]
        + [shaped(n, 2 * clusters, BF16)] * len(others),
    )


def stat_body(has_near, own, *refs):
    out, refs = refs[-1], refs[:-1]
    count = len(refs) // 2
    scores, pairs = refs[: count + 1], refs[count + 1 :]
    n, clusters = scores[0].shape
    member = whole(own[:n, :])
    total = jnp.sum(member * scores[0][...], axis=0, keepdims=True)
    for i in range(count):
        pair = pairs[i]
        other = whole(pair[:n, pair.shape[1] - 2 * clusters :])
        part = jnp.sum(other * scores[i + 1][:n, :], axis=0, keepdims=True)
        total += part if i < has_near else 2.0 * part
    size = jnp.sum(member, axis=0, keepdims=True)
    row = lax.broadcasted_iota(jnp.int32, out.shape, 0)
    out[...] = jnp.where(row == 0, total, jnp.where(row == 1, size, 0.0))


def stat_call(has_near, own, scores, pairs):
    clusters = scores[0].shape[1]
    return call(
        functools.partial(stat_body, has_near),
        [own] + scores + pairs,
        [shaped(STAT_ROWS, clusters)],
    )[0]


def other_body(n, count, *refs):
    pairs, refs = refs[:count], refs[count:]
    kernels, refs = refs[: 2 * count], refs[2 * count :]
    stat, (even, odd) = refs[:-2], refs[-2:]
    half, clusters = even.shape
    over = (((0,), (0,)), ((), ()))
    for part, out in enumerate((odd, even)):
        columns = slice((1 - part) * half, (2 - part) * half)
        acc = jnp.zeros((half, clusters), F32)
        for i, pair in enumerate(pairs):
            both = pair[:n, pair.shape[1] - 2 * clusters :]
            a = lax.dot_general(
                kernels[2 * i][:, columns], both, over, preferred_element_type=F32
            )
            b = lax.dot_general(
                kernels[2 * i + 1][:, columns],
                both[:, :clusters],
                over,
                preferred_element_type=F32,
            )
            acc += a[:, :clusters] + (a[:, clusters:] + b)
        out[:half, :] = acc
    if stat:
        odd[half:, :] = stat[0][...]


def other_call(n, half, clusters, pairs, kernels, stat):
    return call(
        functools.partial(other_body, n, len(pairs)),
        pairs + kernels + stat,
        [shaped(half, clusters), shaped(half + STAT_ROWS * len(stat), clusters)],
        flops=12 * n * len(pairs) * half * clusters,
    )


def fold_body(n, count, even, received, *refs):
    stats, outs = refs[:count], refs[count:]
    half = even.shape[0]
    stat = stats[0][...]
    for ref in stats[1:]:
        stat += ref[...]
    if received.shape[0] > half:
        stat += received[half:, :]
    for j, out in enumerate(outs):
        rows = slice(j * n, (j + 1) * n)
        out[:n, :] = even[rows, :] + received[rows, :]
        out[n:, :] = stat


def fold_call(n, even, received, stats, extra):
    half, clusters = even.shape
    return call(
        functools.partial(fold_body, n, len(stats)),
        [even, received] + stats,
        [shaped(n + extra, clusters)] * (half // n),
    )


def sum_body(n, last, *refs):
    many = 2 if last else 1 + len(GATHER_ROWS)
    refs, outs = refs[:-many], refs[-many:]
    total, stat = refs[0][:n, :], refs[0][n:, :]
    for ref in refs[1:]:
        total += ref[:n, :]
        if ref.shape[0] == n + STAT_ROWS:
            stat += ref[n:, :]
    if last:
        members, standardized = outs
        x = standardize(total, stat[1:2, :], stat[0:1, :])
        standardized[...] = x
        members[...] = normalize(jnp.exp(-2.0 * x))
    else:
        stats, fulls = outs[0], outs[1:]
        stats[...] = stat
        for full in fulls:
            full[:n, :] = total
            if full.shape[0] > n:
                full[n:, :] = stat


def on_device(rows, cols, features, logits):
    n, clusters = logits.shape
    width = features.shape[1]
    half = n * cols // 2
    masks = list(range(2, cols, 2))
    order = [0] + masks
    order = order + [k + 1 for k in order]
    has_near = int(rows % 2 == 0)
    half_rows = rows // 2
    if has_near:
        place = [2 * q if q < half_rows else 2 * (q - half_rows) + 1 for q in range(rows)]
        offsets = list(range(1, half_rows))
    else:
        place = list(range(rows))
        offsets = list(range(1, half_rows + 1))
    steps = ([0] if has_near else []) + offsets

    def by_col(x, mask):
        return lax.ppermute(x, "col", [(i, i ^ mask) for i in range(cols)])

    def shift(x, d):
        if d == 0:
            pairs = [(i, i ^ 1) for i in range(rows)]
        else:
            pairs = [(place[(q + d) % rows], place[q]) for q in range(rows)]
        return lax.ppermute(x, "row", pairs)

    column = jnp.reshape(lax.axis_index("col"), (1,)).astype(jnp.int32)
    own_rows = lax.dynamic_slice_in_dim(features, lax.axis_index("col") * n, n, 0)
    pair, wide, message = call(
        prepare_body,
        [logits, own_rows],
        [
            shaped(n, 2 * clusters, BF16),
            shaped(n + WIDE_ROWS, 2 * clusters, BF16),
            shaped(n, width + 2 * clusters, BF16),
        ],
        hidden=True,
    )
    far_rows = [shift(own_rows if d else message, d) for d in steps]
    others = [shift(wide, d) if d else far_rows[0] for d in steps]
    evens = [pair] + [by_col(pair, k) for k in masks]
    members = evens + [by_col(x, 1) for x in evens]
    early = 1 + has_near
    extra = [0] + [BACK_ROWS] * len(steps)
    blocks = [kernel_call(n, order, column, own_rows, features)]
    for x in reversed(far_rows):
        blocks.append(
            kernel_call(n, order, column, x, features, blocks[-1][:1], CROSS_COST)
        )
    blocks = blocks[:1] + blocks[:0:-1]
    kernels = [x for block in blocks for x in block]
    cross = kernels[2 * early :]
    scores = scores_call(0, members, kernels, [], extra, hidden=True)
    own = pair

    for iteration in range(ITERS):
        last = iteration == ITERS - 1
        if iteration > 0:
            even, *others = members_call(n, stats, evens, others)
            odd = by_col(even, 1)
            own = even
            scores = scores_call(0, [even], kernels, [], extra)
        if last:
            t_even, t_odd = other_call(n, half, clusters, others[has_near:], cross, [])
            extra = [0] + [LAST_ROWS] * len(steps)
            *scores, stat = scores_call(
                half, [odd], kernels, scores, extra, False, (), [own] + others, has_near
            )
            for x in [shift(stat, d) for d in range(1, rows)]:
                stat = stat + x
            sent = fold_call(
                n, t_even, by_col(t_odd, 1), [stat, by_col(stat, 1)], STAT_ROWS
            )
        else:
            if iteration > 0:
                scores = scores_call(half, [odd], kernels, scores, extra)
            stat = stat_call(has_near, own, scores, others)
            t_even, t_odd = other_call(n, half, clusters, others[has_near:], cross, [stat])
            sent = fold_call(n, t_even, by_col(t_odd, 1), [stat], STAT_ROWS)
        parts = [by_col(x, k) for k, x in zip(masks, sent[1:])]
        back = [shift(x, -d) for d, x in zip(steps, scores[1:])]
        outs = [shaped(n, clusters)] * 2
        if not last:
            outs = [shaped(STAT_ROWS, clusters)]
            outs += [shaped(n + r, clusters) for r in GATHER_ROWS]
        done = call(
            functools.partial(sum_body, n, last),
            [sent[0], scores[0]] + back + parts,
            outs,
        )
        if not last:
            stats, full, total = done
            evens = [total] + [by_col(total, k) for k in masks]
            others = [shift(full, d) for d in steps]
            stats = [stats] + [shift(stats, -d) for d in offsets]
    return tuple(done)


def solution(mesh):
    return jax.shard_map(
        functools.partial(on_device, mesh.shape["row"], mesh.shape["col"]),
        mesh=mesh,
        in_specs=(P("row", None), P(("row", "col"), None)),
        out_specs=(P(("row", "col"), None), P(("row", "col"), None)),
        check_vma=False,
    )
```

```python
import functools

import jax
import jax.numpy as jnp
from jax import lax
from jax.experimental import pallas as pl
from jax.experimental.pallas import tpu as pltpu
from jax.sharding import PartitionSpec as P

ITERS = 2
STAT_ROWS = 8
GATHER_ROWS = (STAT_ROWS, 0)
WIDE_ROWS = 16
LAST_ROWS = 32
BACK_ROWS = 48
VMEM_BYTES = 24 * 1024 * 1024
CROSS_COST = 2.7
VMEM = pl.BlockSpec(memory_space=pltpu.VMEM)
SMEM = pl.BlockSpec(memory_space=pltpu.SMEM)
ANY = pl.BlockSpec(memory_space=pl.ANY)
BF16 = jnp.bfloat16
F32 = jnp.float32


def shaped(rows, columns, dtype=F32):
    return jax.ShapeDtypeStruct((rows, columns), dtype)


def call(body, args, outs, specs=None, scratch=(), flops=0, hidden=False):
    bytes_accessed = sum(x.size * x.dtype.itemsize for x in list(args) + list(outs))
    if hidden:
        flops = bytes_accessed = 0
    made = pl.pallas_call(
        body,
        in_specs=specs or [VMEM] * len(args),
        out_specs=[VMEM] * len(outs),
        out_shape=list(outs),
        scratch_shapes=list(scratch),
        compiler_params=pltpu.CompilerParams(vmem_limit_bytes=VMEM_BYTES),
        cost_estimate=pl.CostEstimate(
            flops=flops, bytes_accessed=bytes_accessed, transcendentals=0
        ),
    )(*args)
    return list(made)


def split(x):
    high = x.astype(BF16)
    low = (x - high.astype(F32)).astype(BF16)
    return high, low


def whole(pair):
    clusters = pair.shape[1] // 2
    return pair[:, :clusters].astype(F32) + pair[:, clusters:].astype(F32)


def standardize(scores, size, weighted):
    inverse = 1.0 / size
    distance = weighted * inverse * inverse - scores * (2.0 * inverse)
    centered = distance - jnp.mean(distance, axis=1, keepdims=True)
    spread = jnp.mean(centered * centered, axis=1, keepdims=True)
    return centered * lax.rsqrt(spread + 1e-06)


def normalize(raised):
    return raised / jnp.sum(raised, axis=1, keepdims=True)


def store_pair(out, rows, x):
    clusters = x.shape[1]
    high, low = split(x)
    out[rows, :clusters] = high
    out[rows, clusters:] = low


def prepare_body(logits, rows, pair, wide, message):
    n, width = rows.shape
    member = normalize(jnp.exp(logits[...]))
    store_pair(pair, slice(0, n), member)
    store_pair(wide, slice(0, n), member)
    wide[n:, :] = jnp.zeros((wide.shape[0] - n, wide.shape[1]), BF16)
    message[:, :width] = rows[...]
    message[:, width:] = pair[...]


def kernel_body(order, column_ref, rows_ref, plane_ref, *refs):
    high_ref, low_ref = refs[-2:]
    n, width = high_ref.shape[0], plane_ref.shape[1]
    column = column_ref[0]
    rows = rows_ref[:n, :width]
    for j, k in enumerate(order):
        start = pl.multiple_of(lax.bitwise_xor(column, k) * n, n)
        inner = lax.dot_general(
            rows,
            plane_ref[pl.ds(start, n), :],
            (((1,), (1,)), ((), ())),
            preferred_element_type=F32,
        )
        t = inner / width
        high, low = split(t * (3.0 + t * (3.0 + t)))
        high_ref[:, j * n : (j + 1) * n] = high
        low_ref[:, j * n : (j + 1) * n] = low


def kernel_call(n, order, column, rows, plane, after=(), cost=1):
    total = plane.shape[0]
    return call(
        functools.partial(kernel_body, tuple(order)),
        [column, rows, plane, *after],
        [shaped(n, total, BF16)] * 2,
        [SMEM, VMEM, VMEM] + [ANY] * len(after),
        flops=int(2 * cost * n) * total * plane.shape[1],
    )


def scores_body(at, pieces, kernels, partials, unused, weights, has_near, *refs):
    members, refs = refs[:pieces], refs[pieces:]
    blocks, refs = refs[:kernels], refs[kernels:]
    before, refs = refs[:partials], refs[partials:]
    own, outs = refs[:weights], refs[weights + unused :]
    n = blocks[0].shape[0]
    clusters = members[0].shape[1] // 2
    for i, out in enumerate(outs[: kernels // 2]):
        both, rest, start = None, None, at
        for piece in members:
            columns = slice(start, start + piece.shape[0])
            start += piece.shape[0]
            a = jnp.dot(blocks[2 * i][:, columns], piece[...], preferred_element_type=F32)
            b = jnp.dot(
                blocks[2 * i + 1][:, columns],
                piece[:, :clusters],
                preferred_element_type=F32,
            )
            both = a if both is None else both + a
            rest = b if rest is None else rest + b
        s = both[:, :clusters] + (both[:, clusters:] + rest)
        if partials:
            s += before[i][:n, :]
        out[:n, :] = s
        if out.shape[0] > n:
            out[n:, :] = jnp.zeros((out.shape[0] - n, clusters), F32)
    if weights:
        count = len(outs) - 1
        stat = outs[count]
        stat_body(has_near, *own[:1], *outs[:count], *own[1:], stat)


def scores_call(
    at, members, kernels, partials, extra, hidden=False, after=(), weights=(), has_near=0
):
    n, clusters = kernels[0].shape[0], members[0].shape[1] // 2
    depth = sum(x.shape[0] for x in members)
    return call(
        functools.partial(
            scores_body,
            at,
            len(members),
            len(kernels),
            len(partials),
            len(after),
            len(weights),
            has_near,
        ),
        [*members, *kernels, *partials, *weights, *after],
        [shaped(n + e, clusters) for e in extra]
        + [shaped(STAT_ROWS, clusters)] * (len(weights) > 0),
        [VMEM] * (len(members) + len(kernels) + len(partials) + len(weights))
        + [ANY] * len(after),
        flops=3 * n * len(kernels) * depth * clusters,
        hidden=hidden,
    )


def members_body(n, smalls, evens, others, *refs):
    stats, refs = refs[:smalls], refs[smalls:]
    own, refs = refs[:evens], refs[evens:]
    rest, refs = refs[:others], refs[others:]
    even, pairs = refs[0], refs[1:]
    stat = stats[0][...]
    for ref in stats[1:]:
        stat += ref[...]
    for ref in rest:
        stat += ref[n : n + STAT_ROWS, :]
    weighted, size = stat[0:1, :], stat[1:2, :]

    def member_of(x):
        return normalize(jnp.exp(-2.0 * standardize(x, size, weighted)))

    for j, ref in enumerate(own):
        store_pair(even, slice(j * n, (j + 1) * n), member_of(ref[:n, :]))
    for pair, ref in zip(pairs, rest):
        store_pair(pair, slice(0, n), member_of(ref[:n, :]))


def members_call(n, stats, evens, others):
    clusters = evens[0].shape[1]
    return call(
        functools.partial(members_body, n, len(stats), len(evens), len(others)),
        stats + evens + others,
        [shaped(n * len(evens), 2 * clusters, BF16)]
        + [shaped(n, 2 * clusters, BF16)] * len(others),
    )


def stat_body(has_near, own, *refs):
    out, refs = refs[-1], refs[:-1]
    count = len(refs) // 2
    scores, pairs = refs[: count + 1], refs[count + 1 :]
    n, clusters = scores[0].shape
    member = whole(own[:n, :])
    total = jnp.sum(member * scores[0][...], axis=0, keepdims=True)
    for i in range(count):
        pair = pairs[i]
        other = whole(pair[:n, pair.shape[1] - 2 * clusters :])
        part = jnp.sum(other * scores[i + 1][:n, :], axis=0, keepdims=True)
        total += part if i < has_near else 2.0 * part
    size = jnp.sum(member, axis=0, keepdims=True)
    row = lax.broadcasted_iota(jnp.int32, out.shape, 0)
    out[...] = jnp.where(row == 0, total, jnp.where(row == 1, size, 0.0))


def stat_call(has_near, own, scores, pairs):
    clusters = scores[0].shape[1]
    return call(
        functools.partial(stat_body, has_near),
        [own] + scores + pairs,
        [shaped(STAT_ROWS, clusters)],
    )[0]


def other_body(n, count, *refs):
    pairs, refs = refs[:count], refs[count:]
    kernels, refs = refs[: 2 * count], refs[2 * count :]
    stat, (even, odd) = refs[:-2], refs[-2:]
    half, clusters = even.shape
    over = (((0,), (0,)), ((), ()))
    for part, out in enumerate((odd, even)):
        columns = slice((1 - part) * half, (2 - part) * half)
        acc = jnp.zeros((half, clusters), F32)
        for i, pair in enumerate(pairs):
            both = pair[:n, pair.shape[1] - 2 * clusters :]
            a = lax.dot_general(
                kernels[2 * i][:, columns], both, over, preferred_element_type=F32
            )
            b = lax.dot_general(
                kernels[2 * i + 1][:, columns],
                both[:, :clusters],
                over,
                preferred_element_type=F32,
            )
            acc += a[:, :clusters] + (a[:, clusters:] + b)
        out[:half, :] = acc
    if stat:
        odd[half:, :] = stat[0][...]


def other_call(n, half, clusters, pairs, kernels, stat):
    return call(
        functools.partial(other_body, n, len(pairs)),
        pairs + kernels + stat,
        [shaped(half, clusters), shaped(half + STAT_ROWS * len(stat), clusters)],
        flops=12 * n * len(pairs) * half * clusters,
    )


def fold_body(n, count, even, received, *refs):
    stats, outs = refs[:count], refs[count:]
    half = even.shape[0]
    stat = stats[0][...]
    for ref in stats[1:]:
        stat += ref[...]
    if received.shape[0] > half:
        stat += received[half:, :]
    for j, out in enumerate(outs):
        rows = slice(j * n, (j + 1) * n)
        out[:n, :] = even[rows, :] + received[rows, :]
        out[n:, :] = stat


def fold_call(n, even, received, stats, extra):
    half, clusters = even.shape
    return call(
        functools.partial(fold_body, n, len(stats)),
        [even, received] + stats,
        [shaped(n + extra, clusters)] * (half // n),
    )


def sum_body(n, last, *refs):
    many = 2 if last else 1 + len(GATHER_ROWS)
    refs, outs = refs[:-many], refs[-many:]
    total, stat = refs[0][:n, :], refs[0][n:, :]
    for ref in refs[1:]:
        total += ref[:n, :]
        if ref.shape[0] == n + STAT_ROWS:
            stat += ref[n:, :]
    if last:
        members, standardized = outs
        x = standardize(total, stat[1:2, :], stat[0:1, :])
        standardized[...] = x
        members[...] = normalize(jnp.exp(-2.0 * x))
    else:
        stats, fulls = outs[0], outs[1:]
        stats[...] = stat
        for full in fulls:
            full[:n, :] = total
            if full.shape[0] > n:
                full[n:, :] = stat


def on_device(rows, cols, features, logits):
    n, clusters = logits.shape
    width = features.shape[1]
    half = n * cols // 2
    masks = list(range(2, cols, 2))
    order = [0] + masks
    order = order + [k + 1 for k in order]
    has_near = int(rows % 2 == 0)
    half_rows = rows // 2
    if has_near:
        place = [2 * q if q < half_rows else 2 * (q - half_rows) + 1 for q in range(rows)]
        offsets = list(range(1, half_rows))
    else:
        place = list(range(rows))
        offsets = list(range(1, half_rows + 1))
    steps = ([0] if has_near else []) + offsets

    def by_col(x, mask):
        return lax.ppermute(x, "col", [(i, i ^ mask) for i in range(cols)])

    def shift(x, d):
        if d == 0:
            pairs = [(i, i ^ 1) for i in range(rows)]
        else:
            pairs = [(place[(q + d) % rows], place[q]) for q in range(rows)]
        return lax.ppermute(x, "row", pairs)

    column = jnp.reshape(lax.axis_index("col"), (1,)).astype(jnp.int32)
    own_rows = lax.dynamic_slice_in_dim(features, lax.axis_index("col") * n, n, 0)
    pair, wide, message = call(
        prepare_body,
        [logits, own_rows],
        [
            shaped(n, 2 * clusters, BF16),
            shaped(n + WIDE_ROWS, 2 * clusters, BF16),
            shaped(n, width + 2 * clusters, BF16),
        ],
        hidden=True,
    )
    far_rows = [shift(own_rows if d else message, d) for d in steps]
    others = [shift(wide, d) if d else far_rows[0] for d in steps]
    evens = [pair] + [by_col(pair, k) for k in masks]
    members = evens + [by_col(x, 1) for x in evens]
    early = 1 + has_near
    extra = [0] + [BACK_ROWS] * len(steps)
    blocks = [kernel_call(n, order, column, own_rows, features)]
    for x in reversed(far_rows):
        blocks.append(
            kernel_call(n, order, column, x, features, blocks[-1][:1], CROSS_COST)
        )
    blocks = blocks[:1] + blocks[:0:-1]
    kernels = [x for block in blocks for x in block]
    cross = kernels[2 * early :]
    scores = scores_call(0, members, kernels, [], extra, hidden=True)
    own = pair

    for iteration in range(ITERS):
        last = iteration == ITERS - 1
        if iteration > 0:
            even, *others = members_call(n, stats, evens, others)
            odd = by_col(even, 1)
            own = even
            scores = scores_call(0, [even], kernels, [], extra)
        if last:
            t_even, t_odd = other_call(n, half, clusters, others[has_near:], cross, [])
            extra = [0] + [LAST_ROWS] * len(steps)
            *scores, stat = scores_call(
                half, [odd], kernels, scores, extra, False, (), [own] + others, has_near
            )
            for x in [shift(stat, d) for d in range(1, rows)]:
                stat = stat + x
            sent = fold_call(
                n, t_even, by_col(t_odd, 1), [stat, by_col(stat, 1)], STAT_ROWS
            )
        else:
            if iteration > 0:
                scores = scores_call(half, [odd], kernels, scores, extra)
            stat = stat_call(has_near, own, scores, others)
            t_even, t_odd = other_call(n, half, clusters, others[has_near:], cross, [stat])
            sent = fold_call(n, t_even, by_col(t_odd, 1), [stat], STAT_ROWS)
        parts = [by_col(x, k) for k, x in zip(masks, sent[1:])]
        back = [shift(x, -d) for d, x in zip(steps, scores[1:])]
        outs = [shaped(n, clusters)] * 2
        if not last:
            outs = [shaped(STAT_ROWS, clusters)]
            outs += [shaped(n + r, clusters) for r in GATHER_ROWS]
        done = call(
            functools.partial(sum_body, n, last),
            [sent[0], scores[0]] + back + parts,
            outs,
        )
        if not last:
            stats, full, total = done
            evens = [total] + [by_col(total, k) for k in masks]
            others = [shift(full, d) for d in steps]
            stats = [stats] + [shift(stats, -d) for d in offsets]
    return tuple(done)


def solution(mesh):
    return jax.shard_map(
        functools.partial(on_device, mesh.shape["row"], mesh.shape["col"]),
        mesh=mesh,
        in_specs=(P("row", None), P(("row", "col"), None)),
        out_specs=(P(("row", "col"), None), P(("row", "col"), None)),
        check_vma=False,
    )
```

```python
import functools

import jax
import jax.numpy as jnp
from jax import lax
from jax.experimental import pallas as pl
from jax.experimental.pallas import tpu as pltpu
from jax.sharding import PartitionSpec as P

ITERS = 2
STAT_ROWS = 8
GATHER_ROWS = (STAT_ROWS, 0)
WIDE_ROWS = 16
LAST_ROWS = 32
BACK_ROWS = 48
VMEM_BYTES = 24 * 1024 * 1024
CROSS_COST = 2.7
VMEM = pl.BlockSpec(memory_space=pltpu.VMEM)
SMEM = pl.BlockSpec(memory_space=pltpu.SMEM)
ANY = pl.BlockSpec(memory_space=pl.ANY)
BF16 = jnp.bfloat16
F32 = jnp.float32


def shaped(rows, columns, dtype=F32):
    return jax.ShapeDtypeStruct((rows, columns), dtype)


def call(body, args, outs, specs=None, scratch=(), flops=0, hidden=False):
    bytes_accessed = sum(x.size * x.dtype.itemsize for x in list(args) + list(outs))
    if hidden:
        flops = bytes_accessed = 0
    made = pl.pallas_call(
        body,
        in_specs=specs or [VMEM] * len(args),
        out_specs=[VMEM] * len(outs),
        out_shape=list(outs),
        scratch_shapes=list(scratch),
        compiler_params=pltpu.CompilerParams(vmem_limit_bytes=VMEM_BYTES),
        cost_estimate=pl.CostEstimate(
            flops=flops, bytes_accessed=bytes_accessed, transcendentals=0
        ),
    )(*args)
    return list(made)


def split(x):
    high = x.astype(BF16)
    low = (x - high.astype(F32)).astype(BF16)
    return high, low


def whole(pair):
    clusters = pair.shape[1] // 2
    return pair[:, :clusters].astype(F32) + pair[:, clusters:].astype(F32)


def standardize(scores, size, weighted):
    inverse = 1.0 / size
    distance = weighted * inverse * inverse - scores * (2.0 * inverse)
    centered = distance - jnp.mean(distance, axis=1, keepdims=True)
    spread = jnp.mean(centered * centered, axis=1, keepdims=True)
    return centered * lax.rsqrt(spread + 1e-06)


def normalize(raised):
    return raised / jnp.sum(raised, axis=1, keepdims=True)


def store_pair(out, rows, x):
    clusters = x.shape[1]
    high, low = split(x)
    out[rows, :clusters] = high
    out[rows, clusters:] = low


def prepare_body(logits, rows, pair, wide, message):
    n, width = rows.shape
    member = normalize(jnp.exp(logits[...]))
    store_pair(pair, slice(0, n), member)
    store_pair(wide, slice(0, n), member)
    wide[n:, :] = jnp.zeros((wide.shape[0] - n, wide.shape[1]), BF16)
    message[:, :width] = rows[...]
    message[:, width:] = pair[...]


def kernel_body(order, column_ref, rows_ref, plane_ref, *refs):
    high_ref, low_ref = refs[-2:]
    n, width = high_ref.shape[0], plane_ref.shape[1]
    column = column_ref[0]
    rows = rows_ref[:n, :width]
    for j, k in enumerate(order):
        start = pl.multiple_of(lax.bitwise_xor(column, k) * n, n)
        inner = lax.dot_general(
            rows,
            plane_ref[pl.ds(start, n), :],
            (((1,), (1,)), ((), ())),
            preferred_element_type=F32,
        )
        t = inner / width
        high, low = split(t * (3.0 + t * (3.0 + t)))
        high_ref[:, j * n : (j + 1) * n] = high
        low_ref[:, j * n : (j + 1) * n] = low


def kernel_call(n, order, column, rows, plane, after=(), cost=1):
    total = plane.shape[0]
    return call(
        functools.partial(kernel_body, tuple(order)),
        [column, rows, plane, *after],
        [shaped(n, total, BF16)] * 2,
        [SMEM, VMEM, VMEM] + [ANY] * len(after),
        flops=int(2 * cost * n) * total * plane.shape[1],
    )


def scores_body(at, pieces, kernels, partials, unused, weights, has_near, *refs):
    members, refs = refs[:pieces], refs[pieces:]
    blocks, refs = refs[:kernels], refs[kernels:]
    before, refs = refs[:partials], refs[partials:]
    own, outs = refs[:weights], refs[weights + unused :]
    n = blocks[0].shape[0]
    clusters = members[0].shape[1] // 2
    for i, out in enumerate(outs[: kernels // 2]):
        both, rest, start = None, None, at
        for piece in members:
            columns = slice(start, start + piece.shape[0])
            start += piece.shape[0]
            a = jnp.dot(blocks[2 * i][:, columns], piece[...], preferred_element_type=F32)
            b = jnp.dot(
                blocks[2 * i + 1][:, columns],
                piece[:, :clusters],
                preferred_element_type=F32,
            )
            both = a if both is None else both + a
            rest = b if rest is None else rest + b
        s = both[:, :clusters] + (both[:, clusters:] + rest)
        if partials:
            s += before[i][:n, :]
        out[:n, :] = s
        if out.shape[0] > n:
            out[n:, :] = jnp.zeros((out.shape[0] - n, clusters), F32)
    if weights:
        count = len(outs) - 1
        stat = outs[count]
        stat_body(has_near, *own[:1], *outs[:count], *own[1:], stat)


def scores_call(
    at, members, kernels, partials, extra, hidden=False, after=(), weights=(), has_near=0
):
    n, clusters = kernels[0].shape[0], members[0].shape[1] // 2
    depth = sum(x.shape[0] for x in members)
    return call(
        functools.partial(
            scores_body,
            at,
            len(members),
            len(kernels),
            len(partials),
            len(after),
            len(weights),
            has_near,
        ),
        [*members, *kernels, *partials, *weights, *after],
        [shaped(n + e, clusters) for e in extra]
        + [shaped(STAT_ROWS, clusters)] * (len(weights) > 0),
        [VMEM] * (len(members) + len(kernels) + len(partials) + len(weights))
        + [ANY] * len(after),
        flops=3 * n * len(kernels) * depth * clusters,
        hidden=hidden,
    )


def members_body(n, smalls, evens, others, *refs):
    stats, refs = refs[:smalls], refs[smalls:]
    own, refs = refs[:evens], refs[evens:]
    rest, refs = refs[:others], refs[others:]
    even, pairs = refs[0], refs[1:]
    stat = stats[0][...]
    for ref in stats[1:]:
        stat += ref[...]
    for ref in rest:
        stat += ref[n : n + STAT_ROWS, :]
    weighted, size = stat[0:1, :], stat[1:2, :]

    def member_of(x):
        return normalize(jnp.exp(-2.0 * standardize(x, size, weighted)))

    for j, ref in enumerate(own):
        store_pair(even, slice(j * n, (j + 1) * n), member_of(ref[:n, :]))
    for pair, ref in zip(pairs, rest):
        store_pair(pair, slice(0, n), member_of(ref[:n, :]))


def members_call(n, stats, evens, others):
    clusters = evens[0].shape[1]
    return call(
        functools.partial(members_body, n, len(stats), len(evens), len(others)),
        stats + evens + others,
        [shaped(n * len(evens), 2 * clusters, BF16)]
        + [shaped(n, 2 * clusters, BF16)] * len(others),
    )


def stat_body(has_near, own, *refs):
    out, refs = refs[-1], refs[:-1]
    count = len(refs) // 2
    scores, pairs = refs[: count + 1], refs[count + 1 :]
    n, clusters = scores[0].shape
    member = whole(own[:n, :])
    total = jnp.sum(member * scores[0][...], axis=0, keepdims=True)
    for i in range(count):
        pair = pairs[i]
        other = whole(pair[:n, pair.shape[1] - 2 * clusters :])
        part = jnp.sum(other * scores[i + 1][:n, :], axis=0, keepdims=True)
        total += part if i < has_near else 2.0 * part
    size = jnp.sum(member, axis=0, keepdims=True)
    row = lax.broadcasted_iota(jnp.int32, out.shape, 0)
    out[...] = jnp.where(row == 0, total, jnp.where(row == 1, size, 0.0))


def stat_call(has_near, own, scores, pairs):
    clusters = scores[0].shape[1]
    return call(
        functools.partial(stat_body, has_near),
        [own] + scores + pairs,
        [shaped(STAT_ROWS, clusters)],
    )[0]


def other_body(n, count, *refs):
    pairs, refs = refs[:count], refs[count:]
    kernels, refs = refs[: 2 * count], refs[2 * count :]
    stat, (even, odd) = refs[:-2], refs[-2:]
    half, clusters = even.shape
    over = (((0,), (0,)), ((), ()))
    for part, out in enumerate((odd, even)):
        columns = slice((1 - part) * half, (2 - part) * half)
        acc = jnp.zeros((clusters, half), F32)
        for i, pair in enumerate(pairs):
            both = pair[:n, pair.shape[1] - 2 * clusters :]
            a = lax.dot_general(
                both, kernels[2 * i][:, columns], over, preferred_element_type=F32
            )
            b = lax.dot_general(
                both[:, :clusters],
                kernels[2 * i + 1][:, columns],
                over,
                preferred_element_type=F32,
            )
            acc += a[:clusters, :] + (a[clusters:, :] + b)
        out[:half, :] = acc.T
    if stat:
        odd[half:, :] = stat[0][...]


def other_call(n, half, clusters, pairs, kernels, stat):
    return call(
        functools.partial(other_body, n, len(pairs)),
        pairs + kernels + stat,
        [shaped(half, clusters), shaped(half + STAT_ROWS * len(stat), clusters)],
        flops=12 * n * len(pairs) * half * clusters,
    )


def fold_body(n, count, even, received, *refs):
    stats, outs = refs[:count], refs[count:]
    half = even.shape[0]
    stat = stats[0][...]
    for ref in stats[1:]:
        stat += ref[...]
    if received.shape[0] > half:
        stat += received[half:, :]
    for j, out in enumerate(outs):
        rows = slice(j * n, (j + 1) * n)
        out[:n, :] = even[rows, :] + received[rows, :]
        out[n:, :] = stat


def fold_call(n, even, received, stats, extra):
    half, clusters = even.shape
    return call(
        functools.partial(fold_body, n, len(stats)),
        [even, received] + stats,
        [shaped(n + extra, clusters)] * (half // n),
    )


def sum_body(n, last, *refs):
    many = 2 if last else 1 + len(GATHER_ROWS)
    refs, outs = refs[:-many], refs[-many:]
    total, stat = refs[0][:n, :], refs[0][n:, :]
    for ref in refs[1:]:
        total += ref[:n, :]
        if ref.shape[0] == n + STAT_ROWS:
            stat += ref[n:, :]
    if last:
        members, standardized = outs
        x = standardize(total, stat[1:2, :], stat[0:1, :])
        standardized[...] = x
        members[...] = normalize(jnp.exp(-2.0 * x))
    else:
        stats, fulls = outs[0], outs[1:]
        stats[...] = stat
        for full in fulls:
            full[:n, :] = total
            if full.shape[0] > n:
                full[n:, :] = stat


def on_device(rows, cols, features, logits):
    n, clusters = logits.shape
    width = features.shape[1]
    half = n * cols // 2
    masks = list(range(2, cols, 2))
    order = [0] + masks
    order = order + [k + 1 for k in order]
    has_near = int(rows % 2 == 0)
    half_rows = rows // 2
    if has_near:
        place = [2 * q if q < half_rows else 2 * (q - half_rows) + 1 for q in range(rows)]
        offsets = list(range(1, half_rows))
    else:
        place = list(range(rows))
        offsets = list(range(1, half_rows + 1))
    steps = ([0] if has_near else []) + offsets

    def by_col(x, mask):
        return lax.ppermute(x, "col", [(i, i ^ mask) for i in range(cols)])

    def shift(x, d):
        if d == 0:
            pairs = [(i, i ^ 1) for i in range(rows)]
        else:
            pairs = [(place[(q + d) % rows], place[q]) for q in range(rows)]
        return lax.ppermute(x, "row", pairs)

    column = jnp.reshape(lax.axis_index("col"), (1,)).astype(jnp.int32)
    own_rows = lax.dynamic_slice_in_dim(features, lax.axis_index("col") * n, n, 0)
    pair, wide, message = call(
        prepare_body,
        [logits, own_rows],
        [
            shaped(n, 2 * clusters, BF16),
            shaped(n + WIDE_ROWS, 2 * clusters, BF16),
            shaped(n, width + 2 * clusters, BF16),
        ],
        hidden=True,
    )
    far_rows = [shift(own_rows if d else message, d) for d in steps]
    others = [shift(wide, d) if d else far_rows[0] for d in steps]
    evens = [pair] + [by_col(pair, k) for k in masks]
    members = evens + [by_col(x, 1) for x in evens]
    early = 1 + has_near
    extra = [0] + [BACK_ROWS] * len(steps)
    blocks = [kernel_call(n, order, column, own_rows, features)]
    for x in reversed(far_rows):
        blocks.append(
            kernel_call(n, order, column, x, features, blocks[-1][:1], CROSS_COST)
        )
    blocks = blocks[:1] + blocks[:0:-1]
    kernels = [x for block in blocks for x in block]
    cross = kernels[2 * early :]
    scores = scores_call(0, members, kernels, [], extra, hidden=True)
    own = pair

    for iteration in range(ITERS):
        last = iteration == ITERS - 1
        if iteration > 0:
            even, *others = members_call(n, stats, evens, others)
            odd = by_col(even, 1)
            own = even
            scores = scores_call(0, [even], kernels, [], extra)
        if last:
            t_even, t_odd = other_call(n, half, clusters, others[has_near:], cross, [])
            extra = [0] + [LAST_ROWS] * len(steps)
            *scores, stat = scores_call(
                half, [odd], kernels, scores, extra, False, (), [own] + others, has_near
            )
            for x in [shift(stat, d) for d in range(1, rows)]:
                stat = stat + x
            sent = fold_call(
                n, t_even, by_col(t_odd, 1), [stat, by_col(stat, 1)], STAT_ROWS
            )
        else:
            if iteration > 0:
                scores = scores_call(half, [odd], kernels, scores, extra)
            stat = stat_call(has_near, own, scores, others)
            t_even, t_odd = other_call(n, half, clusters, others[has_near:], cross, [stat])
            sent = fold_call(n, t_even, by_col(t_odd, 1), [stat], STAT_ROWS)
        parts = [by_col(x, k) for k, x in zip(masks, sent[1:])]
        back = [shift(x, -d) for d, x in zip(steps, scores[1:])]
        outs = [shaped(n, clusters)] * 2
        if not last:
            outs = [shaped(STAT_ROWS, clusters)]
            outs += [shaped(n + r, clusters) for r in GATHER_ROWS]
        done = call(
            functools.partial(sum_body, n, last),
            [sent[0], scores[0]] + back + parts,
            outs,
        )
        if not last:
            stats, full, total = done
            evens = [total] + [by_col(total, k) for k in masks]
            others = [shift(full, d) for d in steps]
            stats = [stats] + [shift(stats, -d) for d in offsets]
    return tuple(done)


def solution(mesh):
    return jax.shard_map(
        functools.partial(on_device, mesh.shape["row"], mesh.shape["col"]),
        mesh=mesh,
        in_specs=(P("row", None), P(("row", "col"), None)),
        out_specs=(P(("row", "col"), None), P(("row", "col"), None)),
        check_vma=False,
    )
```

```python
import functools

import jax
import jax.numpy as jnp
from jax import lax
from jax.experimental import pallas as pl
from jax.experimental.pallas import tpu as pltpu
from jax.sharding import PartitionSpec as P

ITERS = 2
STAT_ROWS = 8
GATHER_ROWS = (STAT_ROWS, 0)
WIDE_ROWS = 16
LAST_ROWS = 32
BACK_ROWS = 48
VMEM_BYTES = 24 * 1024 * 1024
CROSS_COST = 2.7
VMEM = pl.BlockSpec(memory_space=pltpu.VMEM)
SMEM = pl.BlockSpec(memory_space=pltpu.SMEM)
ANY = pl.BlockSpec(memory_space=pl.ANY)
BF16 = jnp.bfloat16
F32 = jnp.float32


def shaped(rows, columns, dtype=F32):
    return jax.ShapeDtypeStruct((rows, columns), dtype)


def call(body, args, outs, specs=None, scratch=(), flops=0, hidden=False):
    bytes_accessed = sum(x.size * x.dtype.itemsize for x in list(args) + list(outs))
    if hidden:
        flops = bytes_accessed = 0
    made = pl.pallas_call(
        body,
        in_specs=specs or [VMEM] * len(args),
        out_specs=[VMEM] * len(outs),
        out_shape=list(outs),
        scratch_shapes=list(scratch),
        compiler_params=pltpu.CompilerParams(vmem_limit_bytes=VMEM_BYTES),
        cost_estimate=pl.CostEstimate(
            flops=flops, bytes_accessed=bytes_accessed, transcendentals=0
        ),
    )(*args)
    return list(made)


def split(x):
    high = x.astype(BF16)
    low = (x - high.astype(F32)).astype(BF16)
    return high, low


def whole(pair):
    clusters = pair.shape[1] // 2
    return pair[:, :clusters].astype(F32) + pair[:, clusters:].astype(F32)


def standardize(scores, size, weighted):
    inverse = 1.0 / size
    distance = weighted * inverse * inverse - scores * (2.0 * inverse)
    centered = distance - jnp.mean(distance, axis=1, keepdims=True)
    spread = jnp.mean(centered * centered, axis=1, keepdims=True)
    return centered * lax.rsqrt(spread + 1e-06)


def normalize(raised):
    return raised / jnp.sum(raised, axis=1, keepdims=True)


def store_pair(out, rows, x):
    clusters = x.shape[1]
    high, low = split(x)
    out[rows, :clusters] = high
    out[rows, clusters:] = low


def prepare_body(logits, rows, pair, wide, message):
    n, width = rows.shape
    member = normalize(jnp.exp(logits[...]))
    store_pair(pair, slice(0, n), member)
    store_pair(wide, slice(0, n), member)
    wide[n:, :] = jnp.zeros((wide.shape[0] - n, wide.shape[1]), BF16)
    message[:, :width] = rows[...]
    message[:, width:] = pair[...]


def kernel_body(order, column_ref, rows_ref, plane_ref, *refs):
    high_ref, low_ref = refs[-2:]
    n, width = high_ref.shape[0], plane_ref.shape[1]
    column = column_ref[0]
    rows = rows_ref[:n, :width]
    for j, k in enumerate(order):
        start = pl.multiple_of(lax.bitwise_xor(column, k) * n, n)
        inner = lax.dot_general(
            rows,
            plane_ref[pl.ds(start, n), :],
            (((1,), (1,)), ((), ())),
            preferred_element_type=F32,
        )
        t = inner / width
        high, low = split(t * (3.0 + t * (3.0 + t)))
        high_ref[:, j * n : (j + 1) * n] = high
        low_ref[:, j * n : (j + 1) * n] = low


def kernel_call(n, order, column, rows, plane, after=(), cost=1):
    total = plane.shape[0]
    return call(
        functools.partial(kernel_body, tuple(order)),
        [column, rows, plane, *after],
        [shaped(n, total, BF16)] * 2,
        [SMEM, VMEM, VMEM] + [ANY] * len(after),
        flops=int(2 * cost * n) * total * plane.shape[1],
    )


def scores_body(at, pieces, kernels, partials, unused, weights, has_near, *refs):
    members, refs = refs[:pieces], refs[pieces:]
    blocks, refs = refs[:kernels], refs[kernels:]
    before, refs = refs[:partials], refs[partials:]
    own, outs = refs[:weights], refs[weights + unused :]
    n = blocks[0].shape[0]
    clusters = members[0].shape[1] // 2
    whole_members = jnp.concatenate([piece[...] for piece in members], axis=0)
    for i, out in enumerate(outs[: kernels // 2]):
        columns = slice(at, at + whole_members.shape[0])
        both = jnp.dot(
            blocks[2 * i][:, columns], whole_members, preferred_element_type=F32
        )
        rest = jnp.dot(
            blocks[2 * i + 1][:, columns],
            whole_members[:, :clusters],
            preferred_element_type=F32,
        )
        s = both[:, :clusters] + (both[:, clusters:] + rest)
        if partials:
            s += before[i][:n, :]
        out[:n, :] = s
        if out.shape[0] > n:
            out[n:, :] = jnp.zeros((out.shape[0] - n, clusters), F32)
    if weights:
        count = len(outs) - 1
        stat = outs[count]
        stat_body(has_near, *own[:1], *outs[:count], *own[1:], stat)


def scores_call(
    at, members, kernels, partials, extra, hidden=False, after=(), weights=(), has_near=0
):
    n, clusters = kernels[0].shape[0], members[0].shape[1] // 2
    depth = sum(x.shape[0] for x in members)
    return call(
        functools.partial(
            scores_body,
            at,
            len(members),
            len(kernels),
            len(partials),
            len(after),
            len(weights),
            has_near,
        ),
        [*members, *kernels, *partials, *weights, *after],
        [shaped(n + e, clusters) for e in extra]
        + [shaped(STAT_ROWS, clusters)] * (len(weights) > 0),
        [VMEM] * (len(members) + len(kernels) + len(partials) + len(weights))
        + [ANY] * len(after),
        flops=3 * n * len(kernels) * depth * clusters,
        hidden=hidden,
    )


def members_body(n, smalls, evens, others, *refs):
    stats, refs = refs[:smalls], refs[smalls:]
    own, refs = refs[:evens], refs[evens:]
    rest, refs = refs[:others], refs[others:]
    even, pairs = refs[0], refs[1:]
    stat = stats[0][...]
    for ref in stats[1:]:
        stat += ref[...]
    for ref in rest:
        stat += ref[n : n + STAT_ROWS, :]
    weighted, size = stat[0:1, :], stat[1:2, :]

    def member_of(x):
        return normalize(jnp.exp(-2.0 * standardize(x, size, weighted)))

    for j, ref in enumerate(own):
        store_pair(even, slice(j * n, (j + 1) * n), member_of(ref[:n, :]))
    for pair, ref in zip(pairs, rest):
        store_pair(pair, slice(0, n), member_of(ref[:n, :]))


def members_call(n, stats, evens, others):
    clusters = evens[0].shape[1]
    return call(
        functools.partial(members_body, n, len(stats), len(evens), len(others)),
        stats + evens + others,
        [shaped(n * len(evens), 2 * clusters, BF16)]
        + [shaped(n, 2 * clusters, BF16)] * len(others),
    )


def stat_body(has_near, own, *refs):
    out, refs = refs[-1], refs[:-1]
    count = len(refs) // 2
    scores, pairs = refs[: count + 1], refs[count + 1 :]
    n, clusters = scores[0].shape
    member = whole(own[:n, :])
    total = jnp.sum(member * scores[0][...], axis=0, keepdims=True)
    for i in range(count):
        pair = pairs[i]
        other = whole(pair[:n, pair.shape[1] - 2 * clusters :])
        part = jnp.sum(other * scores[i + 1][:n, :], axis=0, keepdims=True)
        total += part if i < has_near else 2.0 * part
    size = jnp.sum(member, axis=0, keepdims=True)
    row = lax.broadcasted_iota(jnp.int32, out.shape, 0)
    out[...] = jnp.where(row == 0, total, jnp.where(row == 1, size, 0.0))


def stat_call(has_near, own, scores, pairs):
    clusters = scores[0].shape[1]
    return call(
        functools.partial(stat_body, has_near),
        [own] + scores + pairs,
        [shaped(STAT_ROWS, clusters)],
    )[0]


def other_body(n, count, *refs):
    pairs, refs = refs[:count], refs[count:]
    kernels, refs = refs[: 2 * count], refs[2 * count :]
    stat, (even, odd) = refs[:-2], refs[-2:]
    half, clusters = even.shape
    over = (((0,), (0,)), ((), ()))
    for part, out in enumerate((odd, even)):
        columns = slice((1 - part) * half, (2 - part) * half)
        acc = jnp.zeros((clusters, half), F32)
        for i, pair in enumerate(pairs):
            both = pair[:n, pair.shape[1] - 2 * clusters :]
            a = lax.dot_general(
                both, kernels[2 * i][:, columns], over, preferred_element_type=F32
            )
            b = lax.dot_general(
                both[:, :clusters],
                kernels[2 * i + 1][:, columns],
                over,
                preferred_element_type=F32,
            )
            acc += a[:clusters, :] + (a[clusters:, :] + b)
        out[:half, :] = acc.T
    if stat:
        odd[half:, :] = stat[0][...]


def other_call(n, half, clusters, pairs, kernels, stat):
    return call(
        functools.partial(other_body, n, len(pairs)),
        pairs + kernels + stat,
        [shaped(half, clusters), shaped(half + STAT_ROWS * len(stat), clusters)],
        flops=12 * n * len(pairs) * half * clusters,
    )


def fold_body(n, count, even, received, *refs):
    stats, outs = refs[:count], refs[count:]
    half = even.shape[0]
    stat = stats[0][...]
    for ref in stats[1:]:
        stat += ref[...]
    if received.shape[0] > half:
        stat += received[half:, :]
    for j, out in enumerate(outs):
        rows = slice(j * n, (j + 1) * n)
        out[:n, :] = even[rows, :] + received[rows, :]
        out[n:, :] = stat


def fold_call(n, even, received, stats, extra):
    half, clusters = even.shape
    return call(
        functools.partial(fold_body, n, len(stats)),
        [even, received] + stats,
        [shaped(n + extra, clusters)] * (half // n),
    )


def sum_body(n, last, *refs):
    many = 2 if last else 1 + len(GATHER_ROWS)
    refs, outs = refs[:-many], refs[-many:]
    total, stat = refs[0][:n, :], refs[0][n:, :]
    for ref in refs[1:]:
        total += ref[:n, :]
        if ref.shape[0] == n + STAT_ROWS:
            stat += ref[n:, :]
    if last:
        members, standardized = outs
        x = standardize(total, stat[1:2, :], stat[0:1, :])
        standardized[...] = x
        members[...] = normalize(jnp.exp(-2.0 * x))
    else:
        stats, fulls = outs[0], outs[1:]
        stats[...] = stat
        for full in fulls:
            full[:n, :] = total
            if full.shape[0] > n:
                full[n:, :] = stat


def on_device(rows, cols, features, logits):
    n, clusters = logits.shape
    width = features.shape[1]
    half = n * cols // 2
    masks = list(range(2, cols, 2))
    order = [0] + masks
    order = order + [k + 1 for k in order]
    has_near = int(rows % 2 == 0)
    half_rows = rows // 2
    if has_near:
        place = [2 * q if q < half_rows else 2 * (q - half_rows) + 1 for q in range(rows)]
        offsets = list(range(1, half_rows))
    else:
        place = list(range(rows))
        offsets = list(range(1, half_rows + 1))
    steps = ([0] if has_near else []) + offsets

    def by_col(x, mask):
        return lax.ppermute(x, "col", [(i, i ^ mask) for i in range(cols)])

    def shift(x, d):
        if d == 0:
            pairs = [(i, i ^ 1) for i in range(rows)]
        else:
            pairs = [(place[(q + d) % rows], place[q]) for q in range(rows)]
        return lax.ppermute(x, "row", pairs)

    column = jnp.reshape(lax.axis_index("col"), (1,)).astype(jnp.int32)
    own_rows = lax.dynamic_slice_in_dim(features, lax.axis_index("col") * n, n, 0)
    pair, wide, message = call(
        prepare_body,
        [logits, own_rows],
        [
            shaped(n, 2 * clusters, BF16),
            shaped(n + WIDE_ROWS, 2 * clusters, BF16),
            shaped(n, width + 2 * clusters, BF16),
        ],
        hidden=True,
    )
    far_rows = [shift(own_rows if d else message, d) for d in steps]
    others = [shift(wide, d) if d else far_rows[0] for d in steps]
    evens = [pair] + [by_col(pair, k) for k in masks]
    members = evens + [by_col(x, 1) for x in evens]
    early = 1 + has_near
    extra = [0] + [BACK_ROWS] * len(steps)
    blocks = [kernel_call(n, order, column, own_rows, features)]
    for x in reversed(far_rows):
        blocks.append(
            kernel_call(n, order, column, x, features, blocks[-1][:1], CROSS_COST)
        )
    blocks = blocks[:1] + blocks[:0:-1]
    kernels = [x for block in blocks for x in block]
    cross = kernels[2 * early :]
    scores = scores_call(0, members, kernels, [], extra, hidden=True)
    own = pair

    for iteration in range(ITERS):
        last = iteration == ITERS - 1
        if iteration > 0:
            even, *others = members_call(n, stats, evens, others)
            odd = by_col(even, 1)
            own = even
            scores = scores_call(0, [even], kernels, [], extra)
        if last:
            t_even, t_odd = other_call(n, half, clusters, others[has_near:], cross, [])
            extra = [0] + [LAST_ROWS] * len(steps)
            *scores, stat = scores_call(
                half, [odd], kernels, scores, extra, False, (), [own] + others, has_near
            )
            for x in [shift(stat, d) for d in range(1, rows)]:
                stat = stat + x
            sent = fold_call(
                n, t_even, by_col(t_odd, 1), [stat, by_col(stat, 1)], STAT_ROWS
            )
        else:
            if iteration > 0:
                scores = scores_call(half, [odd], kernels, scores, extra)
            stat = stat_call(has_near, own, scores, others)
            t_even, t_odd = other_call(n, half, clusters, others[has_near:], cross, [stat])
            sent = fold_call(n, t_even, by_col(t_odd, 1), [stat], STAT_ROWS)
        parts = [by_col(x, k) for k, x in zip(masks, sent[1:])]
        back = [shift(x, -d) for d, x in zip(steps, scores[1:])]
        outs = [shaped(n, clusters)] * 2
        if not last:
            outs = [shaped(STAT_ROWS, clusters)]
            outs += [shaped(n + r, clusters) for r in GATHER_ROWS]
        done = call(
            functools.partial(sum_body, n, last),
            [sent[0], scores[0]] + back + parts,
            outs,
        )
        if not last:
            stats, full, total = done
            evens = [total] + [by_col(total, k) for k in masks]
            others = [shift(full, d) for d in steps]
            stats = [stats] + [shift(stats, -d) for d in offsets]
    return tuple(done)


def solution(mesh):
    return jax.shard_map(
        functools.partial(on_device, mesh.shape["row"], mesh.shape["col"]),
        mesh=mesh,
        in_specs=(P("row", None), P(("row", "col"), None)),
        out_specs=(P(("row", "col"), None), P(("row", "col"), None)),
        check_vma=False,
    )
```
